32 devices in a mesh: dp: 8 (over z, x), mp: 4 (over y, core).
Axes of the slice: x: 2, y: 2, z: 4, core: 2. Of those that a mesh axis runs over, the one named last changes fastest.
Arguments:
- history: bfloat16 [128, 32, 1024], P('dp', None, 'mp'), may hold values from -6 to 6
- lengths: int32 [128], replicated, may hold values from 1 to 32, 2048 in all
- source: int32 [128], replicated, may hold values from 0 to 127, as said below
- owners: int32 [4096, 8], P(('dp', 'mp')), may hold values from 0 to 31, all different within a row; in each aligned block of 128 rows (0 to 127, 128 to 255, ...) at most 48 rows name the same one
- item_rows: int32 [4096, 8], P(('dp', 'mp')), may hold values from 0 to 511
- catalogue: bfloat16 [16384, 1024], P(('dp', 'mp')), may hold values from -6 to 6
- w_in: bfloat16 [4, 1024, 1024], P(None, None, 'mp'), may hold values from -0.1875 to 0.1875
- w_out: bfloat16 [1024, 1024], P('mp'), may hold values from -0.1875 to 0.1875
Outputs:
- w_in_grad: float32 [4, 1024, 1024], P(None, 'dp', 'mp')
- w_out_grad: float32 [1024, 1024], P('mp', 'dp')
- cat_grad: float32 [16384, 1024], P(('dp', 'mp'))
The draws below stay inside these ranges and needn't reach their ends.
Inputs may be any that keep to these rules, and one draw needn't show every extreme that they name: `source`: a permutation; balanced slot k lies on index k // 16 of dp, and the 16 histories that start on one index of dp go to one index of dp at most (16 + 8 - 1) // 8 at a time, that many for some index. Each event names 8 different owners, column 0 the positive item's; the events of one device (aligned blocks of 128) name one owner at most 48 times.
All inputs are finite; a program needn't handle non-finite values.
Results may differ from the reference program's by a relative error of at most 0.017.
Values may be sent and summed in bfloat16 or wider, within the bound.
No kernel may reach another device: no remote copies, remote signals or barrier semaphores. Data moves between devices by JAX's collectives and lax.ppermute only.
A program may use at most 128 MiB of HBM per device.

```python
import math
import jax
import jax.numpy as jnp
import numpy as np
from jax import lax

D = 1024
H = 8
HD = 1024
LMAX = 32
SEQ_DEV = 16
TOP = 8
CAT_DEV = 512
SEQS = 128
EVENTS = 4096
EQ = 128
CAP = 48
CAT = 16384
DEVICES = 32


def draw_source(key, part):
    devices_n = SEQS // SEQ_DEV
    key_order, key_offset, key_slots = jax.random.split(jax.random.fold_in(key, 17), 3)
    order = jax.random.permutation(key_order, devices_n).astype(jnp.int32)
    offset = jax.random.permutation(key_offset, devices_n).astype(jnp.int32)
    slot_ids = jnp.arange(SEQ_DEV, dtype=jnp.int32)
    target = order[(offset[:, None] + slot_ids[None, :]) % devices_n].reshape(-1)
    noise = jax.random.permutation(key_slots, SEQS).astype(jnp.int32)
    scores = target * SEQS + noise
    rank_of = jnp.argsort(jnp.argsort(scores)).astype(jnp.int32)
    flat_src = jnp.arange(SEQS, dtype=jnp.int32)
    return jnp.zeros((SEQS,), jnp.int32).at[rank_of].set(flat_src)


def set_ends(entries, key, least, high):
    spot = [jax.random.randint(jax.random.fold_in(key, axis), (), 0, length) for axis, length in enumerate(entries.shape)]
    main_axis = entries.shape.index(max(entries.shape))
    neighbour = spot[:main_axis] + [(spot[main_axis] + 1) % entries.shape[main_axis]] + spot[main_axis + 1:]
    return entries.at[tuple(spot)].set(least).at[tuple(neighbour)].set(high)


def block_levels(own_key, dims, cuts, smallest, largest):
    loudness = 1.0
    for axis_at, blocks in cuts:
        heights = jax.random.uniform(jax.random.fold_in(jax.random.fold_in(own_key, 6), axis_at), (blocks,), jnp.float32, smallest / len(cuts), largest / len(cuts))
        loudness = loudness * jnp.repeat(jnp.exp(heights), dims[axis_at] // blocks).reshape((-1,) + (1,) * (len(dims) - 1 - axis_at))
    return loudness


def split_up(amount, total, bound, skew):
    loads = [(1 << 20) // math.isqrt(rank ** skew) + 1 for rank in range(2, amount + 1)]
    rest, given = total - bound - (amount - 1), [1] * (amount - 1)
    while rest > 0:
        movable = [i for i in range(amount - 1) if given[i] < bound]
        mass, budget = sum([loads[i] for i in movable]), rest
        for i in movable:
            more = min(bound - given[i], max(1, budget * loads[i] // mass), rest)
            given[i] = given[i] + more
            rest = rest - more
    return np.array([bound] + given)


def uneven(rng, count, total, limit, lean):
    if count == 2:
        one = jax.random.randint(rng, (), max(1, total - limit), min(limit, total - 1) + 1)
        return jnp.stack([one, total - one])
    sizes = jnp.asarray(split_up(count, total, limit, lean), jnp.int32)
    pairs = (count - 1) // 2
    giver, receiver = sizes[1:1 + 2 * pairs:2], sizes[2:2 + 2 * pairs:2]
    room = jnp.minimum(giver - 1, limit - receiver)
    shifted = jax.random.randint(jax.random.fold_in(rng, 1), (pairs,), 0, 1 << 20) % (room + 1)
    sizes = sizes.at[1:1 + 2 * pairs:2].set(giver - shifted).at[2:2 + 2 * pairs:2].set(receiver + shifted)
    return sizes[jax.random.permutation(jax.random.fold_in(rng, 2), count)]


def shared_out(own_key, own, number, rows, count, top, reach, lean):
    ranking = jax.random.permutation(own_key, count)
    crowded, usual = portions_of(count, rows * top, reach, lean, True), portions_of(count, rows * top, reach, lean, False)
    places = jnp.arange(count)

    def named(sizes, turn):
        used = int((sizes > 0).sum())
        fixed = max(1, used // 4)
        shifted = fixed + (places - fixed + turn * (used - fixed)) % max(1, count - fixed)
        return jnp.zeros((count,), jnp.int32).at[ranking[jnp.where(places < fixed, places, shifted)]].set(jnp.asarray(sizes, jnp.int32))

    sizes = jnp.where(number % 4 == 0, named(crowded, number // 4), named(usual, number - number // 4 - 1))
    mixed = jax.random.permutation(jax.random.fold_in(own, 3), count)
    giver, sink = mixed[0:count // 2 * 2:2], mixed[1:count // 2 * 2:2]
    slack = jnp.minimum(sizes[giver] - 1, reach - sizes[sink]) // 2
    slack = jnp.where((giver == ranking[0]) | (sink == ranking[0]) | (sizes[sink] == 0), 0, jnp.maximum(slack, 0))
    shifted = jax.random.randint(jax.random.fold_in(own, 4), (count // 2,), 0, 1 << 20) % (slack + 1)
    sizes = sizes.at[giver].add(-shifted).at[sink].add(shifted)
    members = jnp.searchsorted(jnp.cumsum(sizes), jnp.arange(rows * top), side="right").astype(jnp.int32)
    listing = members.reshape(top, rows).T
    listing = listing[jax.random.permutation(jax.random.fold_in(own, 1), rows)]
    turn = jax.random.randint(jax.random.fold_in(own, 2), (rows, 1), 0, top)
    return jnp.take_along_axis(listing, (jnp.arange(top)[None, :] + turn) % top, axis=1)


def portions_of(number_of, total, most, skew, full):
    weights = [(1 << 20) // math.isqrt(grade ** skew) + 1 for grade in range(1, number_of + 1)]
    largest = most if full else min(most, max(-(-total // number_of), total * weights[0] // sum(weights)))
    least = 1 if total - largest >= number_of - 1 else 0
    given, rest = [largest] + [least] * (number_of - 1), total - largest - least * (number_of - 1)
    while rest > 0:
        free = [i for i in range(1, number_of) if given[i] < largest] or [i for i in range(1, number_of) if given[i] < most]
        mass, left = sum([weights[i] for i in free]), rest
        for i in free:
            addition = min(most - given[i], max(1, left * weights[i] // mass), rest)
            given[i] = given[i] + addition
            rest = rest - addition
    return np.array(given)


def normal_values(own_key, dims, scale, reach, cuts=(), held_as=jnp.bfloat16):
    gain = block_levels(own_key, dims, cuts, -0.22, 0.18) if cuts else 1.0
    result = jax.random.normal(own_key, dims, jnp.float32) * scale * gain
    return jnp.minimum(jnp.maximum(result, -reach), reach).astype(held_as)


def setup_inputs(seed: int = 0) -> dict:
    key_list = jax.random.split(jax.random.key(seed), 9)
    history = normal_values(key_list[0], (SEQS, LMAX, D), 1.0, 6.0, ((0, 8), (2, 4)))
    lengths = uneven(key_list[1], SEQS, SEQS * LMAX // 2, LMAX, 2).astype(jnp.int32)
    source = draw_source(jax.random.fold_in(key_list[8], 71), 0)
    owners_keys = jax.random.split(jax.random.fold_in(key_list[3], 1), EVENTS // EQ)
    owners_turns = jax.random.permutation(jax.random.fold_in(key_list[3], 3), EVENTS // EQ)
    owners = jax.vmap(lambda own, number: shared_out(jax.random.fold_in(key_list[3], 2), own, number, EQ, DEVICES, TOP, CAP, 1))(owners_keys, owners_turns).reshape((EVENTS, TOP))
    item_rows = set_ends(jax.random.randint(key_list[4], (EVENTS, TOP), 0, CAT_DEV), jax.random.fold_in(key_list[4], 1), 0, CAT_DEV - 1).astype(jnp.int32)
    catalogue = normal_values(key_list[5], (CAT, D), 1.0, 6.0, ((0, 32),))
    w_in = normal_values(key_list[6], (4, D, HD), D ** -0.5, 0.1875, ((2, 4),))
    w_out = normal_values(key_list[7], (HD, D), HD ** -0.5, 0.1875, ((0, 4),))
    return {"history": history, "lengths": lengths, "source": source, "owners": owners, "item_rows": item_rows, "catalogue": catalogue, "w_in": w_in, "w_out": w_out}


cosine_divisor = 0.05
epsilon_norm = 1e-05
epsilon_unit = 1e-06

def normalize(rows_in):
    centered = rows_in - lax.optimization_barrier(jnp.mean(rows_in, axis=-1, keepdims=True))
    spread = lax.optimization_barrier(jnp.mean(centered * centered, axis=-1, keepdims=True))
    return centered / jnp.sqrt(spread + epsilon_norm)

def attend(projected, length_here):
    gating = projected[0].astype(jnp.float32)
    values = projected[1].astype(jnp.float32)
    queries = projected[2].astype(jnp.float32)
    key_rows = projected[3].astype(jnp.float32)
    steps_n = projected.shape[1]
    scores = jnp.einsum('thd,shd->hts', queries, key_rows) / jnp.sqrt(jnp.float32(projected.shape[3]))
    places = jnp.arange(steps_n, dtype=jnp.int32)
    allowed = (places[None, :] <= places[:, None]) & (places[None, :] < length_here)
    weights = jnp.where(allowed[None], jax.nn.silu(scores) / length_here.astype(jnp.float32), 0.0).astype(jnp.bfloat16)
    mixed_out = jnp.einsum('hts,shd->thd', weights.astype(jnp.float32), values)
    return (normalize(mixed_out) * gating).astype(jnp.bfloat16)

def loss_block(out_rows, valid_rows, fetched):
    out_norm = jnp.sqrt(lax.optimization_barrier(jnp.sum(out_rows * out_rows, axis=-1, keepdims=True)) + epsilon_unit)
    request_unit_vector = out_rows / out_norm
    item_f = fetched.astype(jnp.float32)
    item_norm = jnp.sqrt(lax.optimization_barrier(jnp.sum(item_f * item_f, axis=-1, keepdims=True)) + epsilon_unit)
    catalog_unit_vector = item_f / item_norm
    cosine_match_raw = jnp.einsum('qn,qgn->qg', request_unit_vector, catalog_unit_vector) / cosine_divisor
    expo = jnp.exp(cosine_match_raw)
    probs = expo / lax.optimization_barrier(jnp.sum(expo, axis=-1, keepdims=True))
    column = jnp.arange(cosine_match_raw.shape[1], dtype=jnp.int32)
    exponent_shares = (probs - (column[None, :] == 0).astype(jnp.float32)) * valid_rows[:, None].astype(jnp.float32)
    request_unit_vector_slope = jnp.einsum('as,asy->ay', exponent_shares, catalog_unit_vector) / cosine_divisor
    out_grad = (request_unit_vector_slope - request_unit_vector * lax.optimization_barrier(jnp.sum(request_unit_vector * request_unit_vector_slope, axis=-1, keepdims=True))) / out_norm
    catalog_unit_vector_slope = exponent_shares[:, :, None] * request_unit_vector[:, None, :] / cosine_divisor
    item_grad = (catalog_unit_vector_slope - catalog_unit_vector * lax.optimization_barrier(jnp.sum(catalog_unit_vector * catalog_unit_vector_slope, axis=-1, keepdims=True))) / item_norm
    return (out_grad, item_grad)

def silu_slope(preact):
    sigma = jax.nn.sigmoid(preact)
    return sigma * (1.0 + preact * (1.0 - sigma))

def reference(history, lengths, source, owners, item_rows, catalogue, w_in, w_out):
    seq_total, steps_n, width = history.shape
    balanced = history[source]
    counts = lengths[source]
    flat_rows = balanced.reshape(seq_total * steps_n, width)
    normed = normalize(flat_rows.astype(jnp.float32)).astype(jnp.bfloat16)
    preact = jnp.stack([jnp.dot(normed, w_in[part_id], preferred_element_type=jnp.float32) for part_id in range(4)])
    projected = jax.nn.silu(preact).astype(jnp.bfloat16)
    all_width = w_in.shape[2]
    head_size = all_width // H
    grouped = projected.reshape(4, seq_total, steps_n, H, head_size).transpose(1, 0, 2, 3, 4)

    def run_all(inputs):
        return lax.map(lambda pair: attend(pair[0], pair[1]), (inputs, counts))
    gated, back = jax.vjp(run_all, grouped)
    gated_flat = gated.reshape(seq_total * steps_n, all_width)
    output = flat_rows.astype(jnp.float32) + jnp.dot(gated_flat, w_out, preferred_element_type=jnp.float32)
    valid = (jnp.arange(steps_n, dtype=jnp.int32)[None, :] < counts[:, None]).reshape(-1)
    items = owners * CAT_DEV + item_rows
    blocks = seq_total * steps_n // EQ
    top_n = owners.shape[1]

    def one_block(carried, inputs):
        out_rows, valid_rows, item_ids = inputs
        fetched = catalogue[item_ids]
        out_grad, item_grad = loss_block(out_rows, valid_rows, fetched)
        carried = carried.at[item_ids.reshape(-1)].add(item_grad.reshape(-1, width))
        return (carried, out_grad)
    cat_grad, out_grads = lax.scan(one_block, jnp.zeros((catalogue.shape[0], width), jnp.float32), (output.reshape(blocks, EQ, width), valid.reshape(blocks, EQ), items.reshape(blocks, EQ, top_n)))
    out_cotangent = out_grads.reshape(seq_total * steps_n, width).astype(jnp.bfloat16)
    w_out_grad = jnp.dot(gated_flat.T, out_cotangent, preferred_element_type=jnp.float32)
    gated_cotangent = jnp.dot(out_cotangent, w_out.T, preferred_element_type=jnp.float32).astype(jnp.bfloat16)
    grouped_cotangent, = back(gated_cotangent.reshape(seq_total, steps_n, H, head_size))
    projected_cotangent = grouped_cotangent.transpose(1, 0, 2, 3, 4).reshape(4, seq_total * steps_n, all_width)
    preact_cotangent = (projected_cotangent.astype(jnp.float32) * silu_slope(preact)).astype(jnp.bfloat16)
    w_in_grad = jnp.stack([jnp.dot(normed.T, preact_cotangent[part_id], preferred_element_type=jnp.float32) for part_id in range(4)])
    return (w_in_grad, w_out_grad, cat_grad)
```

```python
import functools
import math

import jax
import jax.numpy as jnp
from jax import lax
from jax.experimental import pallas as pl
from jax.experimental.pallas import tpu as pltpu
from jax.sharding import PartitionSpec as P

DH = 128
COSINE_DIVISOR = 0.05
EPS_NORM = 1e-05
EPS_UNIT = 1e-06
BF = jnp.bfloat16
F32 = jnp.float32
I32 = jnp.int32
BLOCK = 128

VM = pl.BlockSpec(memory_space=pltpu.VMEM)
SM = pl.BlockSpec(memory_space=pltpu.SMEM)


def call(body, out_shape, in_specs, flops, nbytes, scratch=(), trans=0):
    many = isinstance(out_shape, (list, tuple))
    return pl.pallas_call(
        body,
        out_shape=out_shape,
        in_specs=in_specs,
        out_specs=[VM] * len(out_shape) if many else VM,
        scratch_shapes=list(scratch),
        compiler_params=pltpu.CompilerParams(vmem_limit_bytes=48 * 1024 * 1024),
        cost_estimate=pl.CostEstimate(
            flops=int(flops), bytes_accessed=int(nbytes), transcendentals=int(trans)
        ),
    )


def dot_nt(a, b):
    return lax.dot_general(a, b, (((1,), (1,)), ((), ())), preferred_element_type=F32)


def dot_tn(a, b):
    return lax.dot_general(a, b, (((0,), (0,)), ((), ())), preferred_element_type=F32)


def dot_nn(a, b):
    return jnp.dot(a, b, preferred_element_type=F32)


def iota(shape, dim):
    return lax.broadcasted_iota(I32, shape, dim)


def pack_kernel(source, place, hist, out, *, dp, seq_dev, per_peer):
    here = place[0]

    def per_dest(d, carry):
        def per_slot(i, count):
            src = source[d * seq_dev + i]
            hit = lax.div(src, seq_dev) == here

            @pl.when(hit)
            def _():
                out[d * per_peer + count] = hist[src - here * seq_dev]

            return count + hit.astype(I32)

        lax.fori_loop(0, seq_dev, per_slot, jnp.int32(0))
        return carry

    lax.fori_loop(0, dp, per_dest, jnp.int32(0))


def forward_kernel(
    source, lengths, place, *refs, mp, seq_dev, per_peer, steps, width, cols, quarter
):
    blocks = refs[:mp]
    w_in = refs[mp]
    normed_t, projected, slope, weights_o, dscale, norm_o, inv_o, gated, gated_t, own = refs[
        mp + 1 : mp + 11
    ]
    feat = refs[mp + 11]
    here_dp = place[0]
    here_mp = place[1]
    part = width // mp
    sources = [source[here_dp * seq_dev + k] for k in range(seq_dev)]
    anchors = [lax.div(s, seq_dev) for s in sources]
    counts = [lengths[s] for s in sources]
    for k in range(seq_dev):
        rank = jnp.int32(0)
        for earlier in range(k):
            rank = rank + (anchors[earlier] == anchors[k]).astype(I32)
        slot = anchors[k] * per_peer + rank
        for j in range(mp):
            start = pl.multiple_of(jnp.bitwise_xor(here_mp, j) * part, part)
            feat[k * steps : (k + 1) * steps, pl.ds(start, part)] = blocks[j][slot]
    rows_all = seq_dev * steps
    own[...] = feat[pl.ds(pl.multiple_of(here_mp * quarter, quarter), quarter), :]
    normed = []
    for g in range(rows_all // BLOCK):
        rows = slice(g * BLOCK, (g + 1) * BLOCK)
        x = feat[rows, :].astype(F32)
        centered = x - jnp.mean(x, axis=-1, keepdims=True)
        spread = jnp.mean(centered * centered, axis=-1, keepdims=True)
        y = (centered * lax.rsqrt(spread + EPS_NORM)).astype(BF)
        feat[rows, :] = y
        normed_t[:, rows] = y.T
    for c in range(4):
        pre = dot_nn(feat[...], w_in[c])
        sigma = jax.nn.sigmoid(pre)
        projected[c] = (pre * sigma).astype(BF)
        slope[c] = sigma * (1.0 + pre * (1.0 - sigma))
    root = 1.0 / math.sqrt(DH)
    t_id = iota((BLOCK, BLOCK), 0)
    s_id = iota((BLOCK, BLOCK), 1)
    per_block = BLOCK // steps
    causal = (t_id // steps == s_id // steps) & (s_id <= t_id)
    for g in range(rows_all // BLOCK):
        rows = slice(g * BLOCK, (g + 1) * BLOCK)
        count = jnp.zeros((BLOCK, BLOCK), I32)
        for i in range(per_block):
            count = jnp.where(t_id // steps == i, counts[g * per_block + i], count)
        allowed = causal & (s_id % steps < count)
        scale = jnp.where(allowed, 1.0 / count.astype(F32), 0.0)
        for h in range(cols // DH):
            lanes = slice(h * DH, (h + 1) * DH)
            scores = dot_nt(projected[2, rows, lanes], projected[3, rows, lanes]) * root
            sigma = jax.nn.sigmoid(scores)
            weights = (scores * sigma * scale).astype(BF)
            weights_o[h, rows, :] = weights
            dscale[h, rows, :] = sigma * (1.0 + scores * (1.0 - sigma)) * (scale * root)
            mixed = dot_nn(weights, projected[1, rows, lanes])
            centered = mixed - jnp.mean(mixed, axis=-1, keepdims=True)
            spread = jnp.mean(centered * centered, axis=-1, keepdims=True)
            inv = lax.rsqrt(spread + EPS_NORM)
            norm = centered * inv
            norm_o[rows, lanes] = norm
            inv_o[rows, lanes] = jnp.broadcast_to(inv, norm.shape)
            done = (norm * projected[0, rows, lanes].astype(F32)).astype(BF)
            gated[rows, lanes] = done
            gated_t[lanes, rows] = done.T


def out_kernel(place, gathered, own, *refs, mp):
    weights = refs[:mp]
    unit, unit_bf, inv_o = refs[mp:]
    here_mp = place[1]
    total = own[...].astype(F32)
    for j in range(mp):
        total = total + dot_nn(gathered[jnp.bitwise_xor(here_mp, j)], weights[j][...])
    inv = lax.rsqrt(jnp.sum(total * total, axis=-1, keepdims=True) + EPS_UNIT)
    u = total * inv
    unit[...] = u
    unit_bf[...] = u.astype(BF)
    inv_o[...] = jnp.broadcast_to(inv, inv_o.shape)


def ask_kernel(owners, rows, wanted, code, *, devices, capacity):
    events, top = owners.shape
    eye = (iota((events, events), 0) == iota((events, events), 1)).astype(F32)

    def turned(x):
        return lax.dot_general(
            x.astype(F32),
            eye,
            (((0,), (0,)), ((), ())),
            precision=lax.Precision.HIGHEST,
            preferred_element_type=F32,
        )

    owners_t = turned(owners[...])
    rows_t = turned(rows[...])
    o_id = iota((devices, events), 0).astype(F32)
    named = jnp.zeros((devices, events), F32)
    row = jnp.zeros((devices, events), F32)
    positive = jnp.zeros((devices, events), F32)
    for j in range(top):
        same = jnp.where(owners_t[j : j + 1, :] == o_id, 1.0, 0.0)
        named = named + same
        row = row + same * rows_t[j : j + 1, :]
        if j == 0:
            positive = same
    before = (iota((events, events), 0) < iota((events, events), 1)).astype(BF)
    rank = dot_nn(named.astype(BF), before)
    code[...] = jnp.where(named > 0.0, 2.0 * rank + 1.0 + positive, 0.0)
    rank = jnp.where(named > 0.0, rank, -1.0)
    lane = iota((devices, capacity), 1)
    result = jnp.zeros((devices, capacity), F32)
    for c in range(capacity):
        one = jnp.sum(jnp.where(rank == float(c), row, 0.0), axis=1, keepdims=True)
        result = jnp.where(lane == c, one, result)
    wanted[...] = result.astype(I32)


def look_kernel(incoming, catalogue, looked, *, chunk):
    stock, _ = catalogue.shape
    slots = incoming.shape[1]
    for s in range(0, slots, chunk):
        hot = jnp.where(iota((stock, chunk), 0) == incoming[:, s : s + chunk], 1.0, 0.0).astype(BF)
        looked[s : s + chunk, :] = dot_tn(hot, catalogue[...]).astype(BF)


def loss_kernel(
    source, lengths, place, items, code, unit, unit_bf, inv_out, out_cot, sending, hot, share,
    *, seq_dev, steps, devices, capacity, chunk,
):
    events, width = unit.shape
    slots = devices * capacity
    position = place[1] * events + iota((1, events), 1)
    valid = jnp.zeros((1, events), F32)
    for k in range(seq_dev):
        count = lengths[source[place[0] * seq_dev + k]]
        step = position - k * steps
        valid = jnp.where((step >= 0) & (step < count), 1.0, valid)
    total = jnp.zeros((1, events), F32)
    scaled = []
    for s in range(0, slots, chunk):
        rows = slice(s, s + chunk)
        x = items[rows, :]
        xf = x.astype(F32)
        inv = lax.rsqrt(jnp.sum(xf * xf, axis=-1, keepdims=True) + EPS_UNIT)
        logits = dot_nt(x, unit_bf[...]) * (inv * (1.0 / COSINE_DIVISOR))
        slot = s + iota((chunk, 1), 0).astype(F32)
        owner = jnp.floor((slot + 0.5) * (1.0 / capacity))
        local = slot - owner * capacity
        spread = (owner == iota((chunk, devices), 1).astype(F32)).astype(BF)
        codes = dot_nn(spread, code[...].astype(BF))
        first = codes == 2.0 * local + 2.0
        mine = first | (codes == 2.0 * local + 1.0)
        hot[rows, :] = mine.astype(BF)
        expo = jnp.where(mine, jnp.exp(logits), 0.0)
        total = total + jnp.sum(expo, axis=0, keepdims=True)
        share[rows, :] = expo
        scaled.append((first, inv))
    factor = valid / total
    slope = jnp.zeros((events, width), F32)
    for n, s in enumerate(range(0, slots, chunk)):
        rows = slice(s, s + chunk)
        first, inv = scaled[n]
        part = share[rows, :] * factor - jnp.where(first, valid, 0.0)
        part = part * (1.0 / COSINE_DIVISOR)
        slope = slope + dot_tn((part * inv).astype(BF), items[rows, :])
        weight = jnp.sum(part, axis=1, keepdims=True)
        sending[rows, :] = (dot_nn(hot[rows, :], unit_bf[...]) * weight).astype(BF)
    u = unit[...]
    along = jnp.sum(u * slope, axis=-1, keepdims=True)
    out_cot[...] = ((slope - u * along) * inv_out[:, 0:1]).astype(BF)


def spread_kernel(incoming, landed, catalogue, out, *, chunk):
    stock, _ = catalogue.shape
    slots = incoming.shape[1]
    for r in range(0, stock, chunk):
        hot = jnp.where(r + iota((chunk, slots), 0) == incoming[...], 1.0, 0.0).astype(BF)
        v = dot_nn(hot, landed[...])
        c = catalogue[r : r + chunk, :].astype(F32)
        inv = lax.rsqrt(jnp.sum(c * c, axis=-1, keepdims=True) + EPS_UNIT)
        c = c * inv
        out[r : r + chunk, :] = (v - c * jnp.sum(c * v, axis=-1, keepdims=True)) * inv


def w_out_kernel(place, *refs, mp, dp):
    blocks = refs[:mp]
    gated_t, out, whole = refs[mp:]
    quarter, width = blocks[0].shape
    for j in range(mp):
        start = pl.multiple_of(jnp.bitwise_xor(place[1], j) * quarter, quarter)
        whole[pl.ds(start, quarter), :] = blocks[j][...]
    part = dot_nn(gated_t[...], whole[...]).astype(BF)
    lanes = width // dp
    for d in range(dp):
        out[d] = part[:, d * lanes : (d + 1) * lanes]


def backward_kernel(place, *refs, mp, dp):
    blocks = refs[:mp]
    w_out, projected, slope, weights, dscale, norm, inv, normed_t, out, whole, cot = refs[mp:]
    quarter, width = blocks[0].shape
    for j in range(mp):
        start = pl.multiple_of(jnp.bitwise_xor(place[1], j) * quarter, quarter)
        whole[pl.ds(start, quarter), :] = blocks[j][...]
    rows_all = whole.shape[0]
    cols = w_out.shape[0]
    gated_cot = dot_nt(whole[...], w_out[...]).astype(BF).astype(F32)
    for g in range(rows_all // BLOCK):
        rows = slice(g * BLOCK, (g + 1) * BLOCK)
        for h in range(cols // DH):
            lanes = slice(h * DH, (h + 1) * DH)
            d_gated = gated_cot[rows, lanes]
            n = norm[rows, lanes]
            d_norm = d_gated * projected[0, rows, lanes].astype(F32)
            d_mixed = inv[rows, lanes] * (
                d_norm
                - jnp.mean(d_norm, axis=-1, keepdims=True)
                - n * jnp.mean(d_norm * n, axis=-1, keepdims=True)
            )
            d_mixed = d_mixed.astype(BF)
            d_weights = dot_nt(d_mixed, projected[1, rows, lanes]).astype(BF).astype(F32)
            d_values = dot_tn(weights[h, rows, :], d_mixed)
            d_scores = (d_weights * dscale[h, rows, :]).astype(BF)
            d_queries = dot_nn(d_scores, projected[3, rows, lanes])
            d_keys = dot_tn(d_scores, projected[2, rows, lanes])
            for c, d in enumerate((d_gated * n, d_values, d_queries, d_keys)):
                cot[c, rows, lanes] = (d.astype(BF).astype(F32) * slope[c, rows, lanes]).astype(BF)
    share = width // dp
    for c in range(4):
        part = dot_nn(normed_t[...], cot[c]).astype(BF)
        for d in range(dp):
            out[d, c] = part[d * share : (d + 1) * share, :]


def swapped(x, axis, bit):
    size = lax.axis_size(axis)
    return lax.ppermute(x, axis, [(a, a ^ bit) for a in range(size)])


def gather_blocks(x, axis):
    size = lax.axis_size(axis)
    blocks = {0: x}
    bit = size // 2
    while bit:
        for j in list(blocks):
            blocks[j ^ bit] = swapped(blocks[j], axis, bit)
        bit //= 2
    return [blocks[j] for j in range(size)]


def per_device(history, lengths, source, owners, item_rows, catalogue, w_in, w_out):
    dp = lax.axis_size("dp")
    mp = lax.axis_size("mp")
    devices = dp * mp
    seq_dev, steps, part = history.shape
    width = part * mp
    cols = w_in.shape[2]
    rows_all = seq_dev * steps
    quarter = rows_all // mp
    events, top = owners.shape
    asks = events * top
    capacity = max(2, (3 * asks + 2 * devices - 1) // (2 * devices))
    slots = devices * capacity
    stock = catalogue.shape[0]
    per_peer = (seq_dev + dp - 1) // dp
    chunk = math.gcd(slots, 512)
    S = jax.ShapeDtypeStruct
    place = jnp.stack([lax.axis_index("dp"), lax.axis_index("mp")]).astype(I32)

    wanted, code = call(
        functools.partial(ask_kernel, devices=devices, capacity=capacity),
        [S((devices, capacity), I32), S((devices, events), F32)],
        [VM, VM],
        1e6,
        1e5,
    )(owners, item_rows)
    incoming = lax.all_to_all(
        wanted, ("dp", "mp"), split_axis=0, concat_axis=0, tiled=True
    ).reshape(1, slots)
    looked = call(
        functools.partial(look_kernel, chunk=chunk),
        S((slots, width), BF),
        [VM, VM],
        2 * slots * stock * width,
        2 * (slots + stock) * width,
    )(incoming, catalogue)
    returned = lax.all_to_all(
        looked.reshape(devices, capacity, width),
        ("dp", "mp"),
        split_axis=0,
        concat_axis=0,
        tiled=True,
    ).reshape(slots, width)

    outgoing = call(
        functools.partial(pack_kernel, dp=dp, seq_dev=seq_dev, per_peer=per_peer),
        S((dp * per_peer, steps, part), BF),
        [SM, SM, VM],
        1e5,
        4 * history.size,
    )(source, place, history)
    arrived = lax.all_to_all(outgoing, "dp", split_axis=0, concat_axis=0, tiled=True)
    features = gather_blocks(arrived, "mp")
    heads = cols // DH
    (normed_t, projected, slope, weights, dscale, norm, inv, gated, gated_t, own) = call(
        functools.partial(
            forward_kernel,
            mp=mp,
            seq_dev=seq_dev,
            per_peer=per_peer,
            steps=steps,
            width=width,
            cols=cols,
            quarter=quarter,
        ),
        [
            S((width, rows_all), BF),
            S((4, rows_all, cols), BF),
            S((4, rows_all, cols), F32),
            S((heads, rows_all, BLOCK), BF),
            S((heads, rows_all, BLOCK), F32),
            S((rows_all, cols), F32),
            S((rows_all, cols), F32),
            S((rows_all, cols), BF),
            S((cols, rows_all), BF),
            S((quarter, width), BF),
        ],
        [SM, SM, SM] + [VM] * (mp + 1),
        8 * rows_all * width * cols,
        12 * 2**20,
        scratch=[pltpu.VMEM((rows_all, width), BF)],
        trans=6 * rows_all * cols,
    )(source, lengths, place, *features, w_in)
    w_out_blocks = gather_blocks(w_out, "mp")
    gathered = lax.all_to_all(
        gated.reshape(mp, quarter, cols), "mp", split_axis=0, concat_axis=0, tiled=True
    )
    unit, unit_bf, inv_out = call(
        functools.partial(out_kernel, mp=mp),
        [S((quarter, width), F32), S((quarter, width), BF), S((quarter, BLOCK), F32)],
        [SM] + [VM] * (mp + 2),
        2 * quarter * width * width,
        4 * 2**20,
    )(place, gathered, own, *w_out_blocks)

    out_cot, sending = call(
        functools.partial(
            loss_kernel,
            seq_dev=seq_dev,
            steps=steps,
            devices=devices,
            capacity=capacity,
            chunk=chunk,
        ),
        [S((quarter, width), BF), S((slots, width), BF)],
        [SM, SM, SM] + [VM] * 5,
        6 * slots * width * events,
        4 * slots * width,
        scratch=[pltpu.VMEM((slots, events), BF), pltpu.VMEM((slots, events), F32)],
    )(source, lengths, place, returned, code, unit, unit_bf, inv_out)
    landed = lax.all_to_all(
        sending.reshape(devices, capacity, width),
        ("dp", "mp"),
        split_axis=0,
        concat_axis=0,
        tiled=True,
    ).reshape(slots, width)

    cots = gather_blocks(out_cot, "mp")
    w_out_part = call(
        functools.partial(w_out_kernel, mp=mp, dp=dp),
        S((dp, cols, width // dp), BF),
        [SM] + [VM] * (mp + 1),
        2 * rows_all * width * cols,
        3 * 2**20,
        scratch=[pltpu.VMEM((rows_all, width), BF)],
    )(place, *cots, gated_t)
    w_in_part = call(
        functools.partial(backward_kernel, mp=mp, dp=dp),
        S((dp, 4, width // dp, cols), BF),
        [SM] + [VM] * (mp + 8),
        10 * rows_all * width * cols,
        12 * 2**20,
        scratch=[pltpu.VMEM((rows_all, width), BF), pltpu.VMEM((4, rows_all, cols), BF)],
    )(place, *cots, w_out, projected, slope, weights, dscale, norm, inv, normed_t)

    def summed(x):
        got = lax.all_to_all(x, "dp", split_axis=0, concat_axis=0, tiled=True)
        return jnp.sum(got.astype(F32), axis=0)

    w_out_grad = summed(w_out_part)
    w_in_grad = summed(w_in_part)
    cat_grad = call(
        functools.partial(spread_kernel, chunk=math.gcd(stock, 128)),
        S((stock, width), F32),
        [VM] * 3,
        2 * slots * stock * width,
        2 * slots * width + 6 * stock * width,
    )(incoming, landed, catalogue)
    return (w_in_grad, w_out_grad, cat_grad)


def solution(mesh):
    placed = (
        P("dp", None, "mp"),
        P(),
        P(),
        P(("dp", "mp"), None),
        P(("dp", "mp"), None),
        P(("dp", "mp"), None),
        P(None, None, "mp"),
        P("mp", None),
    )
    return jax.shard_map(
        per_device,
        mesh=mesh,
        in_specs=placed,
        out_specs=(P(None, "dp", "mp"), P("mp", "dp"), P(("dp", "mp"), None)),
        check_vma=False,
    )
```

```python
import functools
import math

import jax
import jax.numpy as jnp
from jax import lax
from jax.experimental import pallas as pl
from jax.experimental.pallas import tpu as pltpu
from jax.sharding import PartitionSpec as P

DH = 128
COSINE_DIVISOR = 0.05
EPS_NORM = 1e-05
EPS_UNIT = 1e-06
BF = jnp.bfloat16
F32 = jnp.float32
I32 = jnp.int32
BLOCK = 128

VM = pl.BlockSpec(memory_space=pltpu.VMEM)
SM = pl.BlockSpec(memory_space=pltpu.SMEM)


def call(body, out_shape, in_specs, flops, nbytes, scratch=(), trans=0, limit=24):
    many = isinstance(out_shape, (list, tuple))
    return pl.pallas_call(
        body,
        out_shape=out_shape,
        in_specs=in_specs,
        out_specs=[VM] * len(out_shape) if many else VM,
        scratch_shapes=list(scratch),
        compiler_params=pltpu.CompilerParams(vmem_limit_bytes=limit * 2**20),
        cost_estimate=pl.CostEstimate(
            flops=int(flops), bytes_accessed=int(nbytes), transcendentals=int(trans)
        ),
    )


def dot_nt(a, b):
    return lax.dot_general(a, b, (((1,), (1,)), ((), ())), preferred_element_type=F32)


def dot_tn(a, b):
    return lax.dot_general(a, b, (((0,), (0,)), ((), ())), preferred_element_type=F32)


def dot_nn(a, b):
    return jnp.dot(a, b, preferred_element_type=F32)


def iota(shape, dim):
    return lax.broadcasted_iota(I32, shape, dim)


def pack_kernel(source, place, hist, *outs, dp, seq_dev, per_peer):
    here = place[0]

    def per_dest(d, put):
        def per_slot(i, count):
            src = source[d * seq_dev + i]
            hit = lax.div(src, seq_dev) == here

            @pl.when(hit)
            def _():
                put(count, hist[src - here * seq_dev])

            return count + hit.astype(I32)

        lax.fori_loop(0, seq_dev, per_slot, jnp.int32(0))

    if len(outs) == dp:
        for j in range(dp):

            def put(count, value, j=j):
                outs[j][count] = value

            per_dest(jnp.bitwise_xor(here, j), put)
    else:

        def body(d, carry):
            def put(count, value):
                outs[0][d, count] = value

            per_dest(d, put)
            return carry

        lax.fori_loop(0, dp, body, jnp.int32(0))


def take_kernel(source, place, *refs, dp, seq_dev, per_peer, steps):
    arrived, out, held = refs[:-2], refs[-2], refs[-1]
    here = place[0]
    if len(arrived) == dp:
        for j in range(dp):
            held[j] = arrived[j][...]
    else:
        held[...] = arrived[0][...]
    anchors = [lax.div(source[here * seq_dev + k], seq_dev) for k in range(seq_dev)]
    for k in range(seq_dev):
        rank = jnp.int32(0)
        for earlier in range(k):
            rank = rank + (anchors[earlier] == anchors[k]).astype(I32)
        piece = jnp.bitwise_xor(here, anchors[k]) if len(arrived) == dp else anchors[k]
        out[k * steps : (k + 1) * steps, :] = held[piece, rank]


def forward_kernel(source, lengths, place, *refs, mp, seq_dev, steps, width, cols, quarter):
    blocks = refs[:mp]
    w_in = refs[mp]
    normed_t, projected, slope, weights_o, dscale, norm_o, inv_o, gated_t, own = refs[
        mp + 1 : mp + 10
    ]
    gated_out = refs[mp + 10 : 2 * mp + 10]
    feat, gated = refs[2 * mp + 10 :]
    here_dp = place[0]
    here_mp = place[1]
    part = width // mp
    counts = [lengths[source[here_dp * seq_dev + k]] for k in range(seq_dev)]
    for j in range(mp):
        start = pl.multiple_of(jnp.bitwise_xor(here_mp, j) * part, part)
        feat[:, pl.ds(start, part)] = blocks[j][...]
    rows_all = seq_dev * steps
    own[...] = feat[pl.ds(pl.multiple_of(here_mp * quarter, quarter), quarter), :]
    for g in range(rows_all // BLOCK):
        rows = slice(g * BLOCK, (g + 1) * BLOCK)
        x = feat[rows, :].astype(F32)
        centered = x - jnp.mean(x, axis=-1, keepdims=True)
        spread = jnp.mean(centered * centered, axis=-1, keepdims=True)
        y = (centered * lax.rsqrt(spread + EPS_NORM)).astype(BF)
        feat[rows, :] = y
        normed_t[:, rows] = y.T
    for c in range(4):
        pre = dot_nn(feat[...], w_in[c])
        sigma = jax.nn.sigmoid(pre)
        projected[c] = (pre * sigma).astype(BF)
        slope[c] = sigma * (1.0 + pre * (1.0 - sigma))
    root = 1.0 / math.sqrt(DH)
    t_id = iota((BLOCK, BLOCK), 0)
    s_id = iota((BLOCK, BLOCK), 1)
    per_block = BLOCK // steps
    causal = (t_id // steps == s_id // steps) & (s_id <= t_id)
    for g in range(rows_all // BLOCK):
        rows = slice(g * BLOCK, (g + 1) * BLOCK)
        count = jnp.zeros((BLOCK, BLOCK), I32)
        for i in range(per_block):
            count = jnp.where(t_id // steps == i, counts[g * per_block + i], count)
        allowed = causal & (s_id % steps < count)
        scale = jnp.where(allowed, 1.0 / count.astype(F32), 0.0)
        for h in range(cols // DH):
            lanes = slice(h * DH, (h + 1) * DH)
            scores = dot_nt(projected[2, rows, lanes], projected[3, rows, lanes]) * root
            sigma = jax.nn.sigmoid(scores)
            weights = (scores * sigma * scale).astype(BF)
            weights_o[h, rows, :] = weights
            dscale[h, rows, :] = sigma * (1.0 + scores * (1.0 - sigma)) * (scale * root)
            mixed = dot_nn(weights, projected[1, rows, lanes])
            centered = mixed - jnp.mean(mixed, axis=-1, keepdims=True)
            spread = jnp.mean(centered * centered, axis=-1, keepdims=True)
            inv = lax.rsqrt(spread + EPS_NORM)
            norm = centered * inv
            norm_o[rows, lanes] = norm
            inv_o[rows, lanes] = jnp.broadcast_to(inv, norm.shape)
            done = (norm * projected[0, rows, lanes].astype(F32)).astype(BF)
            gated[rows, lanes] = done
            gated_t[lanes, rows] = done.T
    for j in range(mp):
        start = pl.multiple_of(jnp.bitwise_xor(here_mp, j) * quarter, quarter)
        gated_out[j][...] = gated[pl.ds(start, quarter), :]


def out_kernel(own, *refs, mp):
    gathered, weights = refs[:mp], refs[mp : 2 * mp]
    unit, unit_bf, inv_o = refs[2 * mp :]
    total = own[...].astype(F32)
    for j in range(mp):
        total = total + dot_nn(gathered[j][...], weights[j][...])
    inv = lax.rsqrt(jnp.sum(total * total, axis=-1, keepdims=True) + EPS_UNIT)
    u = total * inv
    unit[...] = u
    unit_bf[...] = u.astype(BF)
    inv_o[...] = jnp.broadcast_to(inv, inv_o.shape)


def ask_kernel(owners, rows, wanted, code, *, devices, capacity):
    events, top = owners.shape
    eye = (iota((events, events), 0) == iota((events, events), 1)).astype(F32)

    def turned(x):
        return lax.dot_general(
            x.astype(F32),
            eye,
            (((0,), (0,)), ((), ())),
            precision=lax.Precision.HIGHEST,
            preferred_element_type=F32,
        )

    owners_t = turned(owners[...])
    rows_t = turned(rows[...])
    o_id = iota((devices, events), 0).astype(F32)
    named = jnp.zeros((devices, events), F32)
    row = jnp.zeros((devices, events), F32)
    positive = jnp.zeros((devices, events), F32)
    for j in range(top):
        same = jnp.where(owners_t[j : j + 1, :] == o_id, 1.0, 0.0)
        named = named + same
        row = row + same * rows_t[j : j + 1, :]
        if j == 0:
            positive = same
    before = (iota((events, events), 0) < iota((events, events), 1)).astype(BF)
    rank = dot_nn(named.astype(BF), before)
    code[...] = jnp.where(named > 0.0, 2.0 * rank + 1.0 + positive, 0.0)
    rank = jnp.where(named > 0.0, rank, -1.0)
    lane = iota((devices, capacity), 1)
    result = jnp.zeros((devices, capacity), F32)
    for c in range(capacity):
        one = jnp.sum(jnp.where(rank == float(c), row, 0.0), axis=1, keepdims=True)
        result = jnp.where(lane == c, one, result)
    wanted[...] = result.astype(I32)


def look_kernel(incoming, catalogue, looked, *, chunk):
    stock, _ = catalogue.shape
    slots = incoming.shape[1]
    for s in range(0, slots, chunk):
        hot = jnp.where(iota((stock, chunk), 0) == incoming[:, s : s + chunk], 1.0, 0.0).astype(BF)
        looked[s : s + chunk, :] = dot_tn(hot, catalogue[...]).astype(BF)


def score_kernel(
    place, items, code, code_far, unit, unit_far, expo, inv_o, total_o,
    *, dp, devices, capacity, chunk,
):
    events = unit.shape[0]
    near = devices // 2
    slots = items.shape[0]
    half = pl.multiple_of(lax.div(place[0], dp // 2) * near, near)
    codes_in = [c[pl.ds(half, near), :].astype(BF) for c in (code, code_far)]
    for s in range(0, slots, chunk):
        rows = slice(s, s + chunk)
        x = items[rows, :]
        xf = x.astype(F32)
        inv = lax.rsqrt(jnp.sum(xf * xf, axis=-1, keepdims=True) + EPS_UNIT)
        inv_o[rows, :] = jnp.broadcast_to(inv, (chunk, BLOCK))
        slot = s + iota((chunk, 1), 0).astype(F32)
        owner = jnp.floor((slot + 0.5) * (1.0 / (2 * capacity)))
        local = slot - owner * (2 * capacity)
        far = local >= capacity
        local = jnp.where(far, local - capacity, local)
        named = owner == iota((chunk, near), 1).astype(F32)
        for side in range(2):
            lanes = slice(side * events, (side + 1) * events)
            u = (unit, unit_far)[side][...]
            logits = dot_nt(x, u) * (inv * (1.0 / COSINE_DIVISOR))
            spread = jnp.where(named & (far == (side == 1)), 1.0, 0.0).astype(BF)
            codes = dot_nn(spread, codes_in[side])
            first = codes == 2.0 * local + 2.0
            other = codes == 2.0 * local + 1.0
            e = jnp.exp(logits)
            total_o[:, lanes] = (
                jnp.sum(jnp.where(first | other, e, 0.0), axis=0, keepdims=True)
                + (total_o[:, lanes] if s else 0.0)
            )
            expo[rows, lanes] = jnp.where(first, -e, jnp.where(other, e, 0.0))


def shares(source, lengths, place, expo, total, total_far, dp, seq_dev, steps):
    events = total.shape[1] // 2
    position = place[1] * events + iota((1, events), 1)
    valid = []
    for base in (place[0], jnp.bitwise_xor(place[0], dp // 2)):
        v = jnp.zeros((1, events), F32)
        for k in range(seq_dev):
            step = position - k * steps
            v = jnp.where((step >= 0) & (step < lengths[source[base * seq_dev + k]]), 1.0, v)
        valid.append(v)
    valid = jnp.concatenate(valid, axis=1) * (1.0 / COSINE_DIVISOR)
    full = total[...] + jnp.concatenate([total_far[:, events:], total_far[:, :events]], axis=1)
    factor = valid / full
    return lambda rows: jnp.abs(expo[rows, :]) * factor - jnp.where(expo[rows, :] < 0.0, valid, 0.0)


def slope_kernel(
    source, lengths, place, items, expo, inv, total, total_far, slope, slope_far,
    *, dp, seq_dev, steps, chunk,
):
    share = shares(source, lengths, place, expo, total, total_far, dp, seq_dev, steps)
    events, width = slope.shape
    both = jnp.zeros((2 * events, width), F32)
    for s in range(0, items.shape[0], chunk):
        rows = slice(s, s + chunk)
        both = both + dot_tn((share(rows) * inv[rows, 0:1]).astype(BF), items[rows, :])
    slope[...] = both[:events]
    slope_far[...] = both[events:].astype(BF)


def send_kernel(
    source, lengths, place, expo, total, total_far, unit, unit_far, sending,
    *, dp, seq_dev, steps, chunk,
):
    share = shares(source, lengths, place, expo, total, total_far, dp, seq_dev, steps)
    events = unit.shape[0]
    for s in range(0, expo.shape[0], chunk):
        rows = slice(s, s + chunk)
        hot = jnp.where(expo[rows, :] == 0.0, 0.0, 1.0).astype(BF)
        unit_rows = dot_nn(hot[:, :events], unit[...]) + dot_nn(hot[:, events:], unit_far[...])
        weight = jnp.sum(share(rows), axis=1, keepdims=True)
        sending[rows, :] = (unit_rows * weight).astype(BF)


def out_cot_kernel(unit, inv_out, slope, slope_far, out_cot):
    u = unit[...]
    s = slope[...] + slope_far[...].astype(F32)
    along = jnp.sum(u * s, axis=-1, keepdims=True)
    out_cot[...] = ((s - u * along) * inv_out[:, 0:1]).astype(BF)


def spread_kernel(incoming, landed, catalogue, out, *, chunk):
    stock, _ = catalogue.shape
    slots = incoming.shape[1]
    for r in range(0, stock, chunk):
        hot = jnp.where(r + iota((chunk, slots), 0) == incoming[...], 1.0, 0.0).astype(BF)
        v = dot_nn(hot, landed[...])
        c = catalogue[r : r + chunk, :].astype(F32)
        inv = lax.rsqrt(jnp.sum(c * c, axis=-1, keepdims=True) + EPS_UNIT)
        c = c * inv
        out[r : r + chunk, :] = (v - c * jnp.sum(c * v, axis=-1, keepdims=True)) * inv


def put_pieces(outs, index, here, dp, whole, share):
    if len(outs) == dp:
        for j in range(dp):
            start = pl.multiple_of(jnp.bitwise_xor(here, j) * share, share)
            outs[j][index] = whole[pl.ds(start, share), :]
    else:
        for d in range(dp):
            outs[0][(d,) + index] = whole[d * share : (d + 1) * share, :]


def w_out_kernel(place, *refs, mp, dp):
    blocks, gated_t, outs, whole = refs[:mp], refs[mp], refs[mp + 1 : -1], refs[-1]
    quarter, width = blocks[0].shape
    for j in range(mp):
        start = pl.multiple_of(jnp.bitwise_xor(place[1], j) * quarter, quarter)
        whole[pl.ds(start, quarter), :] = blocks[j][...]
    part = dot_nn(gated_t[...], whole[...]).astype(BF)
    lanes = width // dp
    if len(outs) == dp:
        spare = jnp.stack([part[:, d * lanes : (d + 1) * lanes] for d in range(dp)])
        for d in range(dp):
            for j in range(dp):

                @pl.when(jnp.bitwise_xor(place[0], j) == d)
                def _(d=d, j=j):
                    outs[j][...] = spare[d]
    else:
        for d in range(dp):
            outs[0][d] = part[:, d * lanes : (d + 1) * lanes]


def backward_kernel(place, *refs, mp, dp):
    blocks = refs[:mp]
    w_out, projected, slope, weights, dscale, norm, inv, normed_t = refs[mp : mp + 8]
    outs = refs[mp + 8 : -3]
    whole, cot, parts = refs[-3:]
    quarter, width = blocks[0].shape
    for j in range(mp):
        start = pl.multiple_of(jnp.bitwise_xor(place[1], j) * quarter, quarter)
        whole[pl.ds(start, quarter), :] = blocks[j][...]
    rows_all = whole.shape[0]
    cols = w_out.shape[0]
    gated_cot = dot_nt(whole[...], w_out[...]).astype(BF).astype(F32)
    for g in range(rows_all // BLOCK):
        rows = slice(g * BLOCK, (g + 1) * BLOCK)
        for h in range(cols // DH):
            lanes = slice(h * DH, (h + 1) * DH)
            d_gated = gated_cot[rows, lanes]
            n = norm[rows, lanes]
            d_norm = d_gated * projected[0, rows, lanes].astype(F32)
            d_mixed = inv[rows, lanes] * (
                d_norm
                - jnp.mean(d_norm, axis=-1, keepdims=True)
                - n * jnp.mean(d_norm * n, axis=-1, keepdims=True)
            )
            d_mixed = d_mixed.astype(BF)
            d_weights = dot_nt(d_mixed, projected[1, rows, lanes]).astype(BF).astype(F32)
            d_values = dot_tn(weights[h, rows, :], d_mixed)
            d_scores = (d_weights * dscale[h, rows, :]).astype(BF)
            d_queries = dot_nn(d_scores, projected[3, rows, lanes])
            d_keys = dot_tn(d_scores, projected[2, rows, lanes])
            for c, d in enumerate((d_gated * n, d_values, d_queries, d_keys)):
                cot[c, rows, lanes] = (d.astype(BF).astype(F32) * slope[c, rows, lanes]).astype(BF)
    share = width // dp
    for c in range(4):
        parts[...] = dot_nn(normed_t[...], cot[c]).astype(BF)
        put_pieces(outs, (c,), place[0], dp, parts, share)


def swapped(x, axis, bit):
    size = lax.axis_size(axis)
    return lax.ppermute(x, axis, [(a, a ^ bit) for a in range(size)])


def gather_blocks(x, axis):
    size = lax.axis_size(axis)
    blocks = {0: x}
    bit = size // 2
    while bit:
        for j in list(blocks):
            blocks[j ^ bit] = swapped(blocks[j], axis, bit)
        bit //= 2
    return [blocks[j] for j in range(size)]


def pieces(n, shape, dtype):
    S = jax.ShapeDtypeStruct
    return [S(shape, dtype)] * n if n <= 8 else [S((n,) + shape, dtype)]


def exchange(parts, axis):
    if len(parts) > 1:
        return [p if j == 0 else swapped(p, axis, j) for j, p in enumerate(parts)]
    return [lax.all_to_all(parts[0], axis, split_axis=0, concat_axis=0, tiled=True)]


def summed(parts):
    if len(parts) == 1:
        return jnp.sum(parts[0].astype(F32), axis=0)
    total = parts[0].astype(F32)
    for p in parts[1:]:
        total = total + p.astype(F32)
    return total


def per_device(history, lengths, source, owners, item_rows, catalogue, w_in, w_out):
    dp = lax.axis_size("dp")
    mp = lax.axis_size("mp")
    devices = dp * mp
    near = devices // 2
    seq_dev, steps, part = history.shape
    width = part * mp
    cols = w_in.shape[2]
    rows_all = seq_dev * steps
    quarter = rows_all // mp
    events, top = owners.shape
    asks = events * top
    capacity = max(2, (3 * asks + 2 * devices - 1) // (2 * devices))
    slots = devices * capacity
    stock = catalogue.shape[0]
    per_peer = (seq_dev + dp - 1) // dp
    chunk = math.gcd(slots, 512)
    heads = cols // DH
    S = jax.ShapeDtypeStruct
    here_dp = lax.axis_index("dp")
    place = jnp.stack([here_dp, lax.axis_index("mp")]).astype(I32)
    halves = [list(range(near)), list(range(near, devices))]

    def partner(x):
        return swapped(x, "dp", dp // 2)

    def in_half(x):
        return lax.all_to_all(
            x.reshape(near, 2 * capacity, width),
            ("dp", "mp"),
            split_axis=0,
            concat_axis=0,
            tiled=True,
            axis_index_groups=halves,
        ).reshape(slots, width)

    wanted, code = call(
        functools.partial(ask_kernel, devices=devices, capacity=capacity),
        [S((devices, capacity), I32), S((devices, events), F32)],
        [VM, VM],
        1e6,
        1e5,
    )(owners, item_rows)
    asked = lax.all_to_all(wanted, ("dp", "mp"), split_axis=0, concat_axis=0, tiled=True)
    asked = asked.reshape(2, near, capacity)
    incoming = jnp.where(here_dp < dp // 2, asked, asked[::-1])
    incoming = incoming.transpose(1, 0, 2).reshape(1, slots)
    looked = call(
        functools.partial(look_kernel, chunk=chunk),
        S((slots, width), BF),
        [VM, VM],
        2 * slots * stock * width,
        2 * (slots + stock) * width,
    )(incoming, catalogue)
    items = in_half(looked)

    packed = call(
        functools.partial(pack_kernel, dp=dp, seq_dev=seq_dev, per_peer=per_peer),
        pieces(dp, (per_peer, steps, part), BF),
        [SM, SM, VM],
        1e5,
        4 * history.size,
    )(source, place, history)
    arrived = exchange(packed, "dp")
    looked, arrived = lax.optimization_barrier((looked, arrived))
    rows = call(
        functools.partial(take_kernel, dp=dp, seq_dev=seq_dev, per_peer=per_peer, steps=steps),
        S((rows_all, part), BF),
        [SM, SM] + [VM] * len(arrived),
        1e5,
        4 * history.size,
        scratch=[pltpu.VMEM((dp, per_peer, steps, part), BF)],
    )(source, place, *arrived)
    features = gather_blocks(rows, "mp")
    w_out_blocks = gather_blocks(w_out, "mp")
    features, w_out_blocks = lax.optimization_barrier((features, w_out_blocks))
    (normed_t, projected, slope, weights, dscale, norm, inv, gated_t, own, *gated) = call(
        functools.partial(
            forward_kernel,
            mp=mp,
            seq_dev=seq_dev,
            steps=steps,
            width=width,
            cols=cols,
            quarter=quarter,
        ),
        [
            S((width, rows_all), BF),
            S((4, rows_all, cols), BF),
            S((4, rows_all, cols), F32),
            S((heads, rows_all, BLOCK), BF),
            S((heads, rows_all, BLOCK), F32),
            S((rows_all, cols), F32),
            S((rows_all, cols), F32),
            S((cols, rows_all), BF),
            S((quarter, width), BF),
        ]
        + [S((quarter, cols), BF)] * mp,
        [SM, SM, SM] + [VM] * (mp + 1),
        8 * rows_all * width * cols,
        12 * 2**20,
        scratch=[pltpu.VMEM((rows_all, width), BF), pltpu.VMEM((rows_all, cols), BF)],
        trans=6 * rows_all * cols,
    )(source, lengths, place, *features, w_in)
    gathered = exchange(gated, "mp")
    unit, unit_bf, inv_out = call(
        functools.partial(out_kernel, mp=mp),
        [S((quarter, width), F32), S((quarter, width), BF), S((quarter, BLOCK), F32)],
        [VM] * (2 * mp + 1),
        2 * quarter * width * width,
        4 * 2**20,
    )(own, *gathered, *w_out_blocks)

    code_far = partner(code)
    unit_far = partner(unit_bf)
    expo, inv_item, total = call(
        functools.partial(
            score_kernel, dp=dp, devices=devices, capacity=capacity, chunk=chunk
        ),
        [S((slots, 2 * events), F32), S((slots, BLOCK), F32), S((1, 2 * events), F32)],
        [SM] + [VM] * 5,
        4 * slots * width * events,
        2 * slots * width,
    )(place, items, code, code_far, unit_bf, unit_far)
    total_far = partner(total)
    sizes = dict(dp=dp, seq_dev=seq_dev, steps=steps, chunk=chunk)
    item_slope, slope_far = call(
        functools.partial(slope_kernel, **sizes),
        [S((events, width), F32), S((events, width), BF)],
        [SM, SM, SM] + [VM] * 5,
        4 * slots * width * events,
        2 * slots * width,
    )(source, lengths, place, items, expo, inv_item, total, total_far)
    slope_back = partner(slope_far)
    sending = call(
        functools.partial(send_kernel, **sizes),
        S((slots, width), BF),
        [SM, SM, SM] + [VM] * 5,
        4 * slots * width * events,
        2 * slots * width,
    )(source, lengths, place, expo, total, total_far, unit_bf, unit_far)
    landed = in_half(sending)
    out_cot = call(
        out_cot_kernel, S((events, width), BF), [VM] * 4, 1e6, 2 * 2**20
    )(unit, inv_out, item_slope, slope_back)

    cots = gather_blocks(out_cot, "mp")
    w_out_part = call(
        functools.partial(w_out_kernel, mp=mp, dp=dp),
        pieces(dp, (cols, width // dp), BF),
        [SM] + [VM] * (mp + 1),
        2 * rows_all * width * cols,
        3 * 2**20,
        scratch=[pltpu.VMEM((rows_all, width), BF)],
    )(place, *cots, gated_t)
    w_in_part = call(
        functools.partial(backward_kernel, mp=mp, dp=dp),
        pieces(dp, (4, width // dp, cols), BF),
        [SM] + [VM] * (mp + 8),
        10 * rows_all * width * cols,
        12 * 2**20,
        scratch=[
            pltpu.VMEM((rows_all, width), BF),
            pltpu.VMEM((4, rows_all, cols), BF),
            pltpu.VMEM((width, cols), BF),
        ],
    )(place, *cots, w_out, projected, slope, weights, dscale, norm, inv, normed_t)
    w_out_grad = summed(exchange(w_out_part, "dp"))
    w_in_grad = summed(exchange(w_in_part, "dp"))
    cat_grad = call(
        functools.partial(spread_kernel, chunk=math.gcd(stock, 128)),
        S((stock, width), F32),
        [VM] * 3,
        2 * slots * stock * width,
        2 * slots * width + 6 * stock * width,
    )(incoming, landed, catalogue)
    return (w_in_grad, w_out_grad, cat_grad)


def solution(mesh):
    placed = (
        P("dp", None, "mp"),
        P(),
        P(),
        P(("dp", "mp"), None),
        P(("dp", "mp"), None),
        P(("dp", "mp"), None),
        P(None, None, "mp"),
        P("mp", None),
    )
    return jax.shard_map(
        per_device,
        mesh=mesh,
        in_specs=placed,
        out_specs=(P(None, "dp", "mp"), P("mp", "dp"), P(("dp", "mp"), None)),
        check_vma=False,
    )
```

```python
import functools
import math

import jax
import jax.numpy as jnp
from jax import lax
from jax.experimental import pallas as pl
from jax.experimental.pallas import tpu as pltpu
from jax.sharding import PartitionSpec as P

DH = 128
COSINE_DIVISOR = 0.05
EPS_NORM = 1e-05
EPS_UNIT = 1e-06
BF = jnp.bfloat16
F32 = jnp.float32
I32 = jnp.int32
BLOCK = 128

VM = pl.BlockSpec(memory_space=pltpu.VMEM)
SM = pl.BlockSpec(memory_space=pltpu.SMEM)


def call(body, out_shape, in_specs, flops, nbytes, scratch=(), trans=0, limit=12):
    many = isinstance(out_shape, (list, tuple))
    return pl.pallas_call(
        body,
        out_shape=out_shape,
        in_specs=in_specs,
        out_specs=[VM] * len(out_shape) if many else VM,
        scratch_shapes=list(scratch),
        compiler_params=pltpu.CompilerParams(vmem_limit_bytes=limit * 2**20),
        cost_estimate=pl.CostEstimate(
            flops=int(flops), bytes_accessed=int(nbytes), transcendentals=int(trans)
        ),
    )


def dot_nt(a, b):
    return lax.dot_general(a, b, (((1,), (1,)), ((), ())), preferred_element_type=F32)


def dot_tn(a, b):
    return lax.dot_general(a, b, (((0,), (0,)), ((), ())), preferred_element_type=F32)


def dot_nn(a, b):
    return jnp.dot(a, b, preferred_element_type=F32)


def iota(shape, dim):
    return lax.broadcasted_iota(I32, shape, dim)


def pack_kernel(source, place, hist, *outs, dp, seq_dev, per_peer):
    here = place[0]

    def per_dest(d, put):
        def per_slot(i, count):
            src = source[d * seq_dev + i]
            hit = lax.div(src, seq_dev) == here

            @pl.when(hit)
            def _():
                put(count, hist[src - here * seq_dev])

            return count + hit.astype(I32)

        lax.fori_loop(0, seq_dev, per_slot, jnp.int32(0))

    if len(outs) == dp:
        for j in range(dp):

            def put(count, value, j=j):
                outs[j][count] = value

            per_dest(jnp.bitwise_xor(here, j), put)
    else:

        def body(d, carry):
            def put(count, value):
                outs[0][d, count] = value

            per_dest(d, put)
            return carry

        lax.fori_loop(0, dp, body, jnp.int32(0))


def take_kernel(source, place, *refs, dp, seq_dev, per_peer, steps):
    arrived, out, held = refs[:-2], refs[-2], refs[-1]
    here = place[0]
    if len(arrived) == dp:
        for j in range(dp):
            held[j] = arrived[j][...]
    else:
        held[...] = arrived[0][...]
    anchors = [lax.div(source[here * seq_dev + k], seq_dev) for k in range(seq_dev)]
    for k in range(seq_dev):
        rank = jnp.int32(0)
        for earlier in range(k):
            rank = rank + (anchors[earlier] == anchors[k]).astype(I32)
        piece = jnp.bitwise_xor(here, anchors[k]) if len(arrived) == dp else anchors[k]
        out[k * steps : (k + 1) * steps, :] = held[piece, rank]


def forward_kernel(source, lengths, place, *refs, mp, seq_dev, steps, width, cols, quarter):
    blocks = refs[:mp]
    w_in = refs[mp]
    normed_t, projected, slope, weights_o, dscale, norm_o, inv_o, gated_t, own = refs[
        mp + 1 : mp + 10
    ]
    gated_out = refs[mp + 10 : 2 * mp + 10]
    feat, gated = refs[2 * mp + 10 :]
    here_dp = place[0]
    here_mp = place[1]
    part = width // mp
    counts = [lengths[source[here_dp * seq_dev + k]] for k in range(seq_dev)]
    for j in range(mp):
        start = pl.multiple_of(jnp.bitwise_xor(here_mp, j) * part, part)
        feat[:, pl.ds(start, part)] = blocks[j][...]
    rows_all = seq_dev * steps
    own[...] = feat[pl.ds(pl.multiple_of(here_mp * quarter, quarter), quarter), :]
    for g in range(rows_all // BLOCK):
        rows = slice(g * BLOCK, (g + 1) * BLOCK)
        x = feat[rows, :].astype(F32)
        centered = x - jnp.mean(x, axis=-1, keepdims=True)
        spread = jnp.mean(centered * centered, axis=-1, keepdims=True)
        y = (centered * lax.rsqrt(spread + EPS_NORM)).astype(BF)
        feat[rows, :] = y
        normed_t[:, rows] = y.T
    for c in range(4):
        pre = dot_nn(feat[...], w_in[c])
        sigma = jax.nn.sigmoid(pre)
        projected[c] = (pre * sigma).astype(BF)
        slope[c] = sigma * (1.0 + pre * (1.0 - sigma))
    root = 1.0 / math.sqrt(DH)
    t_id = iota((BLOCK, BLOCK), 0)
    s_id = iota((BLOCK, BLOCK), 1)
    per_block = BLOCK // steps
    causal = (t_id // steps == s_id // steps) & (s_id <= t_id)
    for g in range(rows_all // BLOCK):
        rows = slice(g * BLOCK, (g + 1) * BLOCK)
        count = jnp.zeros((BLOCK, BLOCK), I32)
        for i in range(per_block):
            count = jnp.where(t_id // steps == i, counts[g * per_block + i], count)
        allowed = causal & (s_id % steps < count)
        scale = jnp.where(allowed, 1.0 / count.astype(F32), 0.0)
        for h in range(cols // DH):
            lanes = slice(h * DH, (h + 1) * DH)
            scores = dot_nt(projected[2, rows, lanes], projected[3, rows, lanes]) * root
            sigma = jax.nn.sigmoid(scores)
            weights = (scores * sigma * scale).astype(BF)
            weights_o[h, rows, :] = weights
            dscale[h, rows, :] = sigma * (1.0 + scores * (1.0 - sigma)) * (scale * root)
            mixed = dot_nn(weights, projected[1, rows, lanes])
            centered = mixed - jnp.mean(mixed, axis=-1, keepdims=True)
            spread = jnp.mean(centered * centered, axis=-1, keepdims=True)
            inv = lax.rsqrt(spread + EPS_NORM)
            norm = centered * inv
            norm_o[rows, lanes] = norm
            inv_o[rows, lanes] = jnp.broadcast_to(inv, norm.shape)
            done = (norm * projected[0, rows, lanes].astype(F32)).astype(BF)
            gated[rows, lanes] = done
            gated_t[lanes, rows] = done.T
    for j in range(mp):
        start = pl.multiple_of(jnp.bitwise_xor(here_mp, j) * quarter, quarter)
        gated_out[j][...] = gated[pl.ds(start, quarter), :]


def out_kernel(own, *refs, mp):
    gathered, weights = refs[:mp], refs[mp : 2 * mp]
    unit, unit_bf, inv_o = refs[2 * mp :]
    total = own[...].astype(F32)
    for j in range(mp):
        total = total + dot_nn(gathered[j][...], weights[j][...])
    inv = lax.rsqrt(jnp.sum(total * total, axis=-1, keepdims=True) + EPS_UNIT)
    u = total * inv
    unit[...] = u
    unit_bf[...] = u.astype(BF)
    inv_o[...] = jnp.broadcast_to(inv, inv_o.shape)


def ask_kernel(owners, rows, wanted, code, *, devices, capacity):
    events, top = owners.shape
    eye = (iota((events, events), 0) == iota((events, events), 1)).astype(F32)

    def turned(x):
        return lax.dot_general(
            x.astype(F32),
            eye,
            (((0,), (0,)), ((), ())),
            precision=lax.Precision.HIGHEST,
            preferred_element_type=F32,
        )

    owners_t = turned(owners[...])
    rows_t = turned(rows[...])
    o_id = iota((devices, events), 0).astype(F32)
    named = jnp.zeros((devices, events), F32)
    row = jnp.zeros((devices, events), F32)
    positive = jnp.zeros((devices, events), F32)
    for j in range(top):
        same = jnp.where(owners_t[j : j + 1, :] == o_id, 1.0, 0.0)
        named = named + same
        row = row + same * rows_t[j : j + 1, :]
        if j == 0:
            positive = same
    before = (iota((events, events), 0) < iota((events, events), 1)).astype(BF)
    rank = dot_nn(named.astype(BF), before)
    code[...] = jnp.where(named > 0.0, 2.0 * rank + 1.0 + positive, 0.0)
    rank = jnp.where(named > 0.0, rank, -1.0)
    lane = iota((devices, capacity), 1)
    result = jnp.zeros((devices, capacity), F32)
    for c in range(capacity):
        one = jnp.sum(jnp.where(rank == float(c), row, 0.0), axis=1, keepdims=True)
        result = jnp.where(lane == c, one, result)
    wanted[...] = result.astype(I32)


def look_kernel(incoming, catalogue, looked, *, chunk):
    stock, _ = catalogue.shape
    slots = incoming.shape[1]
    for s in range(0, slots, chunk):
        hot = jnp.where(iota((stock, chunk), 0) == incoming[:, s : s + chunk], 1.0, 0.0).astype(BF)
        looked[s : s + chunk, :] = dot_tn(hot, catalogue[...]).astype(BF)


def score_kernel(
    place, items, code, code_far, unit, unit_far, expo, inv_o, total_o,
    *, dp, devices, capacity, chunk,
):
    events = unit.shape[0]
    near = devices // 2
    slots = items.shape[0]
    half = pl.multiple_of(lax.div(place[0], dp // 2) * near, near)
    codes_in = [c[pl.ds(half, near), :].astype(BF) for c in (code, code_far)]
    for s in range(0, slots, chunk):
        rows = slice(s, s + chunk)
        x = items[rows, :]
        xf = x.astype(F32)
        inv = lax.rsqrt(jnp.sum(xf * xf, axis=-1, keepdims=True) + EPS_UNIT)
        inv_o[rows, :] = jnp.broadcast_to(inv, (chunk, BLOCK))
        slot = s + iota((chunk, 1), 0).astype(F32)
        owner = jnp.floor((slot + 0.5) * (1.0 / (2 * capacity)))
        local = slot - owner * (2 * capacity)
        far = local >= capacity
        local = jnp.where(far, local - capacity, local)
        named = owner == iota((chunk, near), 1).astype(F32)
        for side in range(2):
            lanes = slice(side * events, (side + 1) * events)
            u = (unit, unit_far)[side][...]
            logits = dot_nt(x, u) * (inv * (1.0 / COSINE_DIVISOR))
            spread = jnp.where(named & (far == (side == 1)), 1.0, 0.0).astype(BF)
            codes = dot_nn(spread, codes_in[side])
            first = codes == 2.0 * local + 2.0
            other = codes == 2.0 * local + 1.0
            e = jnp.exp(logits)
            total_o[:, lanes] = (
                jnp.sum(jnp.where(first | other, e, 0.0), axis=0, keepdims=True)
                + (total_o[:, lanes] if s else 0.0)
            )
            expo[rows, lanes] = jnp.where(first, -e, jnp.where(other, e, 0.0))


def shares(source, lengths, place, expo, total, total_far, dp, seq_dev, steps):
    events = total.shape[1] // 2
    position = place[1] * events + iota((1, events), 1)
    valid = []
    for base in (place[0], jnp.bitwise_xor(place[0], dp // 2)):
        v = jnp.zeros((1, events), F32)
        for k in range(seq_dev):
            step = position - k * steps
            v = jnp.where((step >= 0) & (step < lengths[source[base * seq_dev + k]]), 1.0, v)
        valid.append(v)
    valid = jnp.concatenate(valid, axis=1) * (1.0 / COSINE_DIVISOR)
    full = total[...] + jnp.concatenate([total_far[:, events:], total_far[:, :events]], axis=1)
    factor = valid / full
    return lambda rows: jnp.abs(expo[rows, :]) * factor - jnp.where(expo[rows, :] < 0.0, valid, 0.0)


def slope_kernel(
    source, lengths, place, items, expo, inv, total, total_far, slope, slope_far,
    *, dp, seq_dev, steps, chunk,
):
    share = shares(source, lengths, place, expo, total, total_far, dp, seq_dev, steps)
    events, width = slope.shape
    both = jnp.zeros((2 * events, width), F32)
    for s in range(0, items.shape[0], chunk):
        rows = slice(s, s + chunk)
        both = both + dot_tn((share(rows) * inv[rows, 0:1]).astype(BF), items[rows, :])
    slope[...] = both[:events]
    slope_far[...] = both[events:].astype(BF)


def send_kernel(
    source, lengths, place, expo, total, total_far, unit, unit_far, sending,
    *, dp, seq_dev, steps, chunk,
):
    share = shares(source, lengths, place, expo, total, total_far, dp, seq_dev, steps)
    events = unit.shape[0]
    for s in range(0, expo.shape[0], chunk):
        rows = slice(s, s + chunk)
        hot = jnp.where(expo[rows, :] == 0.0, 0.0, 1.0).astype(BF)
        unit_rows = dot_nn(hot[:, :events], unit[...]) + dot_nn(hot[:, events:], unit_far[...])
        weight = jnp.sum(share(rows), axis=1, keepdims=True)
        sending[rows, :] = (unit_rows * weight).astype(BF)


def out_cot_kernel(unit, inv_out, slope, slope_far, out_cot):
    u = unit[...]
    s = slope[...] + slope_far[...].astype(F32)
    along = jnp.sum(u * s, axis=-1, keepdims=True)
    out_cot[...] = ((s - u * along) * inv_out[:, 0:1]).astype(BF)


def spread_kernel(incoming, landed, catalogue, out, *, chunk):
    stock, _ = catalogue.shape
    slots = incoming.shape[1]
    for r in range(0, stock, chunk):
        hot = jnp.where(r + iota((chunk, slots), 0) == incoming[...], 1.0, 0.0).astype(BF)
        v = dot_nn(hot, landed[...])
        c = catalogue[r : r + chunk, :].astype(F32)
        inv = lax.rsqrt(jnp.sum(c * c, axis=-1, keepdims=True) + EPS_UNIT)
        c = c * inv
        out[r : r + chunk, :] = (v - c * jnp.sum(c * v, axis=-1, keepdims=True)) * inv


def put_pieces(outs, index, here, dp, whole, share):
    if len(outs) == dp:
        for j in range(dp):
            start = pl.multiple_of(jnp.bitwise_xor(here, j) * share, share)
            outs[j][index] = whole[pl.ds(start, share), :]
    else:
        for d in range(dp):
            outs[0][(d,) + index] = whole[d * share : (d + 1) * share, :]


def w_out_kernel(place, *refs, mp, dp):
    blocks, gated_t, outs, whole = refs[:mp], refs[mp], refs[mp + 1 : -1], refs[-1]
    quarter, width = blocks[0].shape
    for j in range(mp):
        start = pl.multiple_of(jnp.bitwise_xor(place[1], j) * quarter, quarter)
        whole[pl.ds(start, quarter), :] = blocks[j][...]
    part = dot_nn(gated_t[...], whole[...]).astype(BF)
    lanes = width // dp
    if len(outs) == dp:
        spare = jnp.stack([part[:, d * lanes : (d + 1) * lanes] for d in range(dp)])
        for d in range(dp):
            for j in range(dp):

                @pl.when(jnp.bitwise_xor(place[0], j) == d)
                def _(d=d, j=j):
                    outs[j][...] = spare[d]
    else:
        for d in range(dp):
            outs[0][d] = part[:, d * lanes : (d + 1) * lanes]


def backward_kernel(place, *refs, mp, dp):
    blocks = refs[:mp]
    w_out, projected, slope, weights, dscale, norm, inv, normed_t = refs[mp : mp + 8]
    outs = refs[mp + 8 : -3]
    whole, cot, parts = refs[-3:]
    quarter, width = blocks[0].shape
    for j in range(mp):
        start = pl.multiple_of(jnp.bitwise_xor(place[1], j) * quarter, quarter)
        whole[pl.ds(start, quarter), :] = blocks[j][...]
    rows_all = whole.shape[0]
    cols = w_out.shape[0]
    gated_cot = dot_nt(whole[...], w_out[...]).astype(BF).astype(F32)
    for g in range(rows_all // BLOCK):
        rows = slice(g * BLOCK, (g + 1) * BLOCK)
        for h in range(cols // DH):
            lanes = slice(h * DH, (h + 1) * DH)
            d_gated = gated_cot[rows, lanes]
            n = norm[rows, lanes]
            d_norm = d_gated * projected[0, rows, lanes].astype(F32)
            d_mixed = inv[rows, lanes] * (
                d_norm
                - jnp.mean(d_norm, axis=-1, keepdims=True)
                - n * jnp.mean(d_norm * n, axis=-1, keepdims=True)
            )
            d_mixed = d_mixed.astype(BF)
            d_weights = dot_nt(d_mixed, projected[1, rows, lanes]).astype(BF).astype(F32)
            d_values = dot_tn(weights[h, rows, :], d_mixed)
            d_scores = (d_weights * dscale[h, rows, :]).astype(BF)
            d_queries = dot_nn(d_scores, projected[3, rows, lanes])
            d_keys = dot_tn(d_scores, projected[2, rows, lanes])
            for c, d in enumerate((d_gated * n, d_values, d_queries, d_keys)):
                cot[c, rows, lanes] = (d.astype(BF).astype(F32) * slope[c, rows, lanes]).astype(BF)
    share = width // dp
    for c in range(4):
        parts[...] = dot_nn(normed_t[...], cot[c]).astype(BF)
        put_pieces(outs, (c,), place[0], dp, parts, share)


def swapped(x, axis, bit):
    size = lax.axis_size(axis)
    return lax.ppermute(x, axis, [(a, a ^ bit) for a in range(size)])


def gather_blocks(x, axis):
    size = lax.axis_size(axis)
    blocks = {0: x}
    bit = size // 2
    while bit:
        for j in list(blocks):
            blocks[j ^ bit] = swapped(blocks[j], axis, bit)
        bit //= 2
    return [blocks[j] for j in range(size)]


def pieces(n, shape, dtype):
    S = jax.ShapeDtypeStruct
    return [S(shape, dtype)] * n if n <= 8 else [S((n,) + shape, dtype)]


def exchange(parts, axis):
    if len(parts) > 1:
        return [p if j == 0 else swapped(p, axis, j) for j, p in enumerate(parts)]
    return [lax.all_to_all(parts[0], axis, split_axis=0, concat_axis=0, tiled=True)]


def summed(parts):
    if len(parts) == 1:
        return jnp.sum(parts[0].astype(F32), axis=0)
    total = parts[0].astype(F32)
    for p in parts[1:]:
        total = total + p.astype(F32)
    return total


def per_device(history, lengths, source, owners, item_rows, catalogue, w_in, w_out):
    dp = lax.axis_size("dp")
    mp = lax.axis_size("mp")
    devices = dp * mp
    near = devices // 2
    seq_dev, steps, part = history.shape
    width = part * mp
    cols = w_in.shape[2]
    rows_all = seq_dev * steps
    quarter = rows_all // mp
    events, top = owners.shape
    asks = events * top
    capacity = max(2, (3 * asks + 2 * devices - 1) // (2 * devices))
    slots = devices * capacity
    stock = catalogue.shape[0]
    per_peer = (seq_dev + dp - 1) // dp
    chunk = math.gcd(slots, 512)
    heads = cols // DH
    S = jax.ShapeDtypeStruct
    here_dp = lax.axis_index("dp")
    place = jnp.stack([here_dp, lax.axis_index("mp")]).astype(I32)
    halves = [list(range(near)), list(range(near, devices))]

    def partner(x):
        return swapped(x, "dp", dp // 2)

    def in_half(x):
        return lax.all_to_all(
            x.reshape(near, 2 * capacity, width),
            ("dp", "mp"),
            split_axis=0,
            concat_axis=0,
            tiled=True,
            axis_index_groups=halves,
        ).reshape(slots, width)

    w_out_blocks = gather_blocks(w_out, "mp")
    packed = call(
        functools.partial(pack_kernel, dp=dp, seq_dev=seq_dev, per_peer=per_peer),
        pieces(dp, (per_peer, steps, part), BF),
        [SM, SM, VM],
        1e5,
        4 * history.size,
    )(source, place, history)
    packed, owners = lax.optimization_barrier((packed, owners))
    arrived = exchange(packed, "dp")
    arrived, w_out_blocks = lax.optimization_barrier((arrived, w_out_blocks))

    wanted, code = call(
        functools.partial(ask_kernel, devices=devices, capacity=capacity),
        [S((devices, capacity), I32), S((devices, events), F32)],
        [VM, VM],
        1e6,
        1e5,
    )(owners, item_rows)
    asked = lax.all_to_all(wanted, ("dp", "mp"), split_axis=0, concat_axis=0, tiled=True)
    asked = asked.reshape(2, near, capacity)
    incoming = jnp.where(here_dp < dp // 2, asked, asked[::-1])
    incoming = incoming.transpose(1, 0, 2).reshape(1, slots)
    looked = call(
        functools.partial(look_kernel, chunk=chunk),
        S((slots, width), BF),
        [VM, VM],
        2 * slots * stock * width,
        2 * (slots + stock) * width,
    )(incoming, catalogue)

    rows = call(
        functools.partial(take_kernel, dp=dp, seq_dev=seq_dev, per_peer=per_peer, steps=steps),
        S((rows_all, part), BF),
        [SM, SM] + [VM] * len(arrived),
        1e5,
        4 * history.size,
        scratch=[pltpu.VMEM((dp, per_peer, steps, part), BF)],
    )(source, place, *arrived)
    features = gather_blocks(rows, "mp")
    code_far = partner(code)
    looked, features, code_far = lax.optimization_barrier((looked, features, code_far))
    items = in_half(looked)
    (normed_t, projected, slope, weights, dscale, norm, inv, gated_t, own, *gated) = call(
        functools.partial(
            forward_kernel,
            mp=mp,
            seq_dev=seq_dev,
            steps=steps,
            width=width,
            cols=cols,
            quarter=quarter,
        ),
        [
            S((width, rows_all), BF),
            S((4, rows_all, cols), BF),
            S((4, rows_all, cols), F32),
            S((heads, rows_all, BLOCK), BF),
            S((heads, rows_all, BLOCK), F32),
            S((rows_all, cols), F32),
            S((rows_all, cols), F32),
            S((cols, rows_all), BF),
            S((quarter, width), BF),
        ]
        + [S((quarter, cols), BF)] * mp,
        [SM, SM, SM] + [VM] * (mp + 1),
        8 * rows_all * width * cols,
        12 * 2**20,
        scratch=[pltpu.VMEM((rows_all, width), BF), pltpu.VMEM((rows_all, cols), BF)],
        trans=6 * rows_all * cols,
    )(source, lengths, place, *features, w_in)
    gathered = exchange(gated, "mp")
    unit, unit_bf, inv_out = call(
        functools.partial(out_kernel, mp=mp),
        [S((quarter, width), F32), S((quarter, width), BF), S((quarter, BLOCK), F32)],
        [VM] * (2 * mp + 1),
        2 * quarter * width * width,
        4 * 2**20,
    )(own, *gathered, *w_out_blocks)

    unit_far = partner(unit_bf)
    expo, inv_item, total = call(
        functools.partial(
            score_kernel, dp=dp, devices=devices, capacity=capacity, chunk=chunk
        ),
        [S((slots, 2 * events), F32), S((slots, BLOCK), F32), S((1, 2 * events), F32)],
        [SM] + [VM] * 5,
        4 * slots * width * events,
        2 * slots * width,
    )(place, items, code, code_far, unit_bf, unit_far)
    total_far = partner(total)
    sizes = dict(dp=dp, seq_dev=seq_dev, steps=steps, chunk=chunk)
    item_slope, slope_far = call(
        functools.partial(slope_kernel, **sizes),
        [S((events, width), F32), S((events, width), BF)],
        [SM, SM, SM] + [VM] * 5,
        4 * slots * width * events,
        2 * slots * width,
    )(source, lengths, place, items, expo, inv_item, total, total_far)
    slope_back = partner(slope_far)
    sending = call(
        functools.partial(send_kernel, **sizes),
        S((slots, width), BF),
        [SM, SM, SM] + [VM] * 5,
        4 * slots * width * events,
        2 * slots * width,
    )(source, lengths, place, expo, total, total_far, unit_bf, unit_far)
    out_cot = call(
        out_cot_kernel, S((events, width), BF), [VM] * 4, 1e6, 2 * 2**20
    )(unit, inv_out, item_slope, slope_back)

    cots = gather_blocks(out_cot, "mp")
    sending, cots = lax.optimization_barrier((sending, cots))
    landed = in_half(sending)
    w_out_part = call(
        functools.partial(w_out_kernel, mp=mp, dp=dp),
        pieces(dp, (cols, width // dp), BF),
        [SM] + [VM] * (mp + 1),
        2 * rows_all * width * cols,
        3 * 2**20,
        scratch=[pltpu.VMEM((rows_all, width), BF)],
    )(place, *cots, gated_t)
    w_in_part = call(
        functools.partial(backward_kernel, mp=mp, dp=dp),
        pieces(dp, (4, width // dp, cols), BF),
        [SM] + [VM] * (mp + 8),
        10 * rows_all * width * cols,
        12 * 2**20,
        scratch=[
            pltpu.VMEM((rows_all, width), BF),
            pltpu.VMEM((4, rows_all, cols), BF),
            pltpu.VMEM((width, cols), BF),
        ],
    )(place, *cots, w_out, projected, slope, weights, dscale, norm, inv, normed_t)
    w_out_grad = summed(exchange(w_out_part, "dp"))
    w_in_grad = summed(exchange(w_in_part, "dp"))
    cat_grad = call(
        functools.partial(spread_kernel, chunk=math.gcd(stock, 128)),
        S((stock, width), F32),
        [VM] * 3,
        2 * slots * stock * width,
        2 * slots * width + 6 * stock * width,
    )(incoming, landed, catalogue)
    return (w_in_grad, w_out_grad, cat_grad)


def solution(mesh):
    placed = (
        P("dp", None, "mp"),
        P(),
        P(),
        P(("dp", "mp"), None),
        P(("dp", "mp"), None),
        P(("dp", "mp"), None),
        P(None, None, "mp"),
        P("mp", None),
    )
    return jax.shard_map(
        per_device,
        mesh=mesh,
        in_specs=placed,
        out_specs=(P(None, "dp", "mp"), P("mp", "dp"), P(("dp", "mp"), None)),
        check_vma=False,
    )
```

```python
import functools
import math

import jax
import jax.numpy as jnp
from jax import lax
from jax.experimental import pallas as pl
from jax.experimental.pallas import tpu as pltpu
from jax.sharding import PartitionSpec as P

DH = 128
COSINE_DIVISOR = 0.05
EPS_NORM = 1e-05
EPS_UNIT = 1e-06
BF = jnp.bfloat16
F32 = jnp.float32
I32 = jnp.int32
BLOCK = 128

VM = pl.BlockSpec(memory_space=pltpu.VMEM)
SM = pl.BlockSpec(memory_space=pltpu.SMEM)
HB = pl.BlockSpec(memory_space=pl.ANY)


def call(body, out_shape, in_specs, us, scratch=(), limit=16, out_specs=None):
    many = isinstance(out_shape, (list, tuple))
    outs = list(out_shape) if many else [out_shape]
    out_specs = list(out_specs or [VM] * len(outs))

    def run(*args):
        args = list(args)
        far_in = [n for n, spec in enumerate(in_specs) if spec is HB]
        far_out = [n for n, spec in enumerate(out_specs) if spec is HB]
        n_in, n_out, n_own = len(in_specs), len(outs), len(scratch)
        extra = [pltpu.VMEM(args[n].shape, args[n].dtype) for n in far_in]
        extra += [pltpu.VMEM(outs[n].shape, outs[n].dtype) for n in far_out]
        moved = len(far_in) + len(far_out)

        def kernel(*refs):
            ins, res = list(refs[:n_in]), list(refs[n_in : n_in + n_out])
            own = refs[n_in + n_out : n_in + n_out + n_own]
            held = refs[n_in + n_out + n_own :]
            sems = held[-1] if moved else None
            copies = []
            for m, n in enumerate(far_in):
                copies.append(pltpu.make_async_copy(ins[n], held[m], sems.at[m]))
                ins[n] = held[m]
            for c in copies:
                c.start()
            for c in copies:
                c.wait()
            copies = []
            for m, n in enumerate(far_out):
                m += len(far_in)
                copies.append(pltpu.make_async_copy(held[m], res[n], sems.at[m]))
                res[n] = held[m]
            body(*ins, *res, *own)
            for c in copies:
                c.start()
            for c in copies:
                c.wait()

        result = pl.pallas_call(
            kernel,
            out_shape=outs,
            in_specs=list(in_specs),
            out_specs=out_specs,
            scratch_shapes=list(scratch)
            + extra
            + ([pltpu.SemaphoreType.DMA((moved,))] if moved else []),
            compiler_params=pltpu.CompilerParams(vmem_limit_bytes=limit * 2**20),
            cost_estimate=pl.CostEstimate(
                flops=0, bytes_accessed=int(us * 3.3e6), transcendentals=0
            ),
        )(*args)
        return result if many else result[0]

    return run


def dot_nt(a, b):
    return lax.dot_general(a, b, (((1,), (1,)), ((), ())), preferred_element_type=F32)


def dot_tn(a, b):
    return lax.dot_general(a, b, (((0,), (0,)), ((), ())), preferred_element_type=F32)


def dot_nn(a, b):
    return jnp.dot(a, b, preferred_element_type=F32)


def iota(shape, dim):
    return lax.broadcasted_iota(I32, shape, dim)


def length_of(meta, slot, seqs):
    return meta[2 + seqs + meta[2 + slot]]


def pack_kernel(meta, hist, *outs, dp, seq_dev, per_peer):
    here = meta[0]

    def per_dest(d, put):
        def per_slot(i, count):
            src = meta[2 + d * seq_dev + i]
            hit = lax.div(src, seq_dev) == here

            @pl.when(hit)
            def _():
                put(count, hist[src - here * seq_dev])

            return count + hit.astype(I32)

        lax.fori_loop(0, seq_dev, per_slot, jnp.int32(0))

    if len(outs) == dp:
        for j in range(dp):

            def put(count, value, j=j):
                outs[j][count] = value

            per_dest(jnp.bitwise_xor(here, j), put)
    else:

        def body(d, carry):
            def put(count, value):
                outs[0][d, count] = value

            per_dest(d, put)
            return carry

        lax.fori_loop(0, dp, body, jnp.int32(0))


def take_kernel(meta, *refs, dp, seq_dev, per_peer, steps):
    arrived, out, held = refs[:-2], refs[-2], refs[-1]
    here = meta[0]
    if len(arrived) == dp:
        for j in range(dp):
            held[j] = arrived[j][...]
    else:
        held[...] = arrived[0][...]
    anchors = [lax.div(meta[2 + here * seq_dev + k], seq_dev) for k in range(seq_dev)]
    for k in range(seq_dev):
        rank = jnp.int32(0)
        for earlier in range(k):
            rank = rank + (anchors[earlier] == anchors[k]).astype(I32)
        piece = jnp.bitwise_xor(here, anchors[k]) if len(arrived) == dp else anchors[k]
        out[k * steps : (k + 1) * steps, :] = held[piece, rank]


def forward_kernel(meta, *refs, mp, seqs, seq_dev, steps, width, cols, quarter):
    blocks = refs[:mp]
    w_in = refs[mp]
    normed_t, projected, slope, weights_o, dscale, norm_o, inv_o, gated_t, own = refs[
        mp + 1 : mp + 10
    ]
    gated_out = refs[mp + 10 : 2 * mp + 10]
    feat, gated = refs[2 * mp + 10 :]
    here_dp = meta[0]
    here_mp = meta[1]
    part = width // mp
    counts = [length_of(meta, here_dp * seq_dev + k, seqs) for k in range(seq_dev)]
    for j in range(mp):
        start = pl.multiple_of(jnp.bitwise_xor(here_mp, j) * part, part)
        feat[:, pl.ds(start, part)] = blocks[j][...]
    rows_all = seq_dev * steps
    own[...] = feat[pl.ds(pl.multiple_of(here_mp * quarter, quarter), quarter), :]
    for g in range(rows_all // BLOCK):
        rows = slice(g * BLOCK, (g + 1) * BLOCK)
        x = feat[rows, :].astype(F32)
        centered = x - jnp.mean(x, axis=-1, keepdims=True)
        spread = jnp.mean(centered * centered, axis=-1, keepdims=True)
        y = (centered * lax.rsqrt(spread + EPS_NORM)).astype(BF)
        feat[rows, :] = y
        normed_t[:, rows] = y.T
    for c in range(4):
        pre = dot_nn(feat[...], w_in[c])
        sigma = jax.nn.sigmoid(pre)
        projected[c] = (pre * sigma).astype(BF)
        slope[c] = sigma * (1.0 + pre * (1.0 - sigma))
    root = 1.0 / math.sqrt(DH)
    t_id = iota((BLOCK, BLOCK), 0)
    s_id = iota((BLOCK, BLOCK), 1)
    per_block = BLOCK // steps
    causal = (t_id // steps == s_id // steps) & (s_id <= t_id)
    for g in range(rows_all // BLOCK):
        rows = slice(g * BLOCK, (g + 1) * BLOCK)
        count = jnp.zeros((BLOCK, BLOCK), I32)
        for i in range(per_block):
            count = jnp.where(t_id // steps == i, counts[g * per_block + i], count)
        allowed = causal & (s_id % steps < count)
        scale = jnp.where(allowed, 1.0 / count.astype(F32), 0.0)
        for h in range(cols // DH):
            lanes = slice(h * DH, (h + 1) * DH)
            scores = dot_nt(projected[2, rows, lanes], projected[3, rows, lanes]) * root
            sigma = jax.nn.sigmoid(scores)
            weights = (scores * sigma * scale).astype(BF)
            weights_o[h, rows, :] = weights
            dscale[h, rows, :] = sigma * (1.0 + scores * (1.0 - sigma)) * (scale * root)
            mixed = dot_nn(weights, projected[1, rows, lanes])
            centered = mixed - jnp.mean(mixed, axis=-1, keepdims=True)
            spread = jnp.mean(centered * centered, axis=-1, keepdims=True)
            inv = lax.rsqrt(spread + EPS_NORM)
            norm = centered * inv
            norm_o[rows, lanes] = norm
            inv_o[rows, lanes] = jnp.broadcast_to(inv, norm.shape)
            done = (norm * projected[0, rows, lanes].astype(F32)).astype(BF)
            gated[rows, lanes] = done
            gated_t[lanes, rows] = done.T
    for j in range(mp):
        start = pl.multiple_of(jnp.bitwise_xor(here_mp, j) * quarter, quarter)
        gated_out[j][...] = gated[pl.ds(start, quarter), :]


def out_kernel(own, *refs, mp):
    gathered, weights = refs[:mp], refs[mp : 2 * mp]
    unit, unit_bf, inv_o = refs[2 * mp :]
    total = own[...].astype(F32)
    for j in range(mp):
        total = total + dot_nn(gathered[j][...], weights[j][...])
    inv = lax.rsqrt(jnp.sum(total * total, axis=-1, keepdims=True) + EPS_UNIT)
    u = total * inv
    unit[...] = u
    unit_bf[...] = u.astype(BF)
    inv_o[...] = jnp.broadcast_to(inv, inv_o.shape)


def ask_kernel(owners, rows, wanted, code, *, devices, capacity):
    events, top = owners.shape
    eye = (iota((events, events), 0) == iota((events, events), 1)).astype(F32)

    def turned(x):
        return lax.dot_general(
            x.astype(F32),
            eye,
            (((0,), (0,)), ((), ())),
            precision=lax.Precision.HIGHEST,
            preferred_element_type=F32,
        )

    owners_t = turned(owners[...])
    rows_t = turned(rows[...])
    o_id = iota((devices, events), 0).astype(F32)
    named = jnp.zeros((devices, events), F32)
    row = jnp.zeros((devices, events), F32)
    positive = jnp.zeros((devices, events), F32)
    for j in range(top):
        same = jnp.where(owners_t[j : j + 1, :] == o_id, 1.0, 0.0)
        named = named + same
        row = row + same * rows_t[j : j + 1, :]
        if j == 0:
            positive = same
    before = (iota((events, events), 0) < iota((events, events), 1)).astype(BF)
    rank = dot_nn(named.astype(BF), before)
    code[...] = jnp.where(named > 0.0, 2.0 * rank + 1.0 + positive, 0.0)
    rank = jnp.where(named > 0.0, rank, -1.0)
    lane = iota((devices, capacity), 1)
    result = jnp.zeros((devices, capacity), F32)
    for c in range(capacity):
        one = jnp.sum(jnp.where(rank == float(c), row, 0.0), axis=1, keepdims=True)
        result = jnp.where(lane == c, one, result)
    wanted[...] = result.astype(I32)


def look_kernel(incoming, catalogue, looked, *, chunk):
    stock, _ = catalogue.shape
    slots = incoming.shape[1]
    for s in range(0, slots, chunk):
        hot = jnp.where(iota((stock, chunk), 0) == incoming[:, s : s + chunk], 1.0, 0.0).astype(BF)
        looked[s : s + chunk, :] = dot_tn(hot, catalogue[...]).astype(BF)


def score_kernel(
    meta, items, code, code_far, unit, unit_far, expo, inv_o, total_o,
    *, dp, devices, capacity, chunk,
):
    events = unit.shape[0]
    near = devices // 2
    slots = items.shape[0]
    half = pl.multiple_of(lax.div(meta[0], dp // 2) * near, near)
    codes_in = [c[pl.ds(half, near), :].astype(BF) for c in (code, code_far)]
    for s in range(0, slots, chunk):
        rows = slice(s, s + chunk)
        x = items[rows, :]
        xf = x.astype(F32)
        inv = lax.rsqrt(jnp.sum(xf * xf, axis=-1, keepdims=True) + EPS_UNIT)
        inv_o[rows, :] = jnp.broadcast_to(inv, (chunk, BLOCK))
        slot = s + iota((chunk, 1), 0).astype(F32)
        owner = jnp.floor((slot + 0.5) * (1.0 / (2 * capacity)))
        local = slot - owner * (2 * capacity)
        far = local >= capacity
        local = jnp.where(far, local - capacity, local)
        named = owner == iota((chunk, near), 1).astype(F32)
        for side in range(2):
            lanes = slice(side * events, (side + 1) * events)
            u = (unit, unit_far)[side][...]
            logits = dot_nt(x, u) * (inv * (1.0 / COSINE_DIVISOR))
            spread = jnp.where(named & (far == (side == 1)), 1.0, 0.0).astype(BF)
            codes = dot_nn(spread, codes_in[side])
            first = codes == 2.0 * local + 2.0
            other = codes == 2.0 * local + 1.0
            e = jnp.exp(logits)
            total_o[:, lanes] = (
                jnp.sum(jnp.where(first | other, e, 0.0), axis=0, keepdims=True)
                + (total_o[:, lanes] if s else 0.0)
            )
            expo[rows, lanes] = jnp.where(first, -e, jnp.where(other, e, 0.0))


def shares(meta, expo, total, total_far, dp, seqs, seq_dev, steps):
    events = total.shape[1] // 2
    position = meta[1] * events + iota((1, events), 1)
    valid = []
    for base in (meta[0], jnp.bitwise_xor(meta[0], dp // 2)):
        v = jnp.zeros((1, events), F32)
        for k in range(seq_dev):
            step = position - k * steps
            v = jnp.where((step >= 0) & (step < length_of(meta, base * seq_dev + k, seqs)), 1.0, v)
        valid.append(v)
    valid = jnp.concatenate(valid, axis=1) * (1.0 / COSINE_DIVISOR)
    full = total[...] + jnp.concatenate([total_far[:, events:], total_far[:, :events]], axis=1)
    factor = valid / full
    return lambda rows: jnp.abs(expo[rows, :]) * factor - jnp.where(expo[rows, :] < 0.0, valid, 0.0)


def slope_kernel(
    meta, items, expo, inv, total, total_far, slope, slope_far,
    *, dp, seqs, seq_dev, steps, chunk,
):
    share = shares(meta, expo, total, total_far, dp, seqs, seq_dev, steps)
    events, width = slope.shape
    both = jnp.zeros((2 * events, width), F32)
    for s in range(0, items.shape[0], chunk):
        rows = slice(s, s + chunk)
        both = both + dot_tn((share(rows) * inv[rows, 0:1]).astype(BF), items[rows, :])
    slope[...] = both[:events]
    slope_far[...] = both[events:].astype(BF)


def send_kernel(
    meta, expo, total, total_far, unit, unit_far, sending,
    *, dp, seqs, seq_dev, steps, chunk,
):
    share = shares(meta, expo, total, total_far, dp, seqs, seq_dev, steps)
    events = unit.shape[0]
    for s in range(0, expo.shape[0], chunk):
        rows = slice(s, s + chunk)
        hot = jnp.where(expo[rows, :] == 0.0, 0.0, 1.0).astype(BF)
        unit_rows = dot_nn(hot[:, :events], unit[...]) + dot_nn(hot[:, events:], unit_far[...])
        weight = jnp.sum(share(rows), axis=1, keepdims=True)
        sending[rows, :] = (unit_rows * weight).astype(BF)


def out_cot_kernel(unit, inv_out, slope, slope_far, out_cot):
    u = unit[...]
    s = slope[...] + slope_far[...].astype(F32)
    along = jnp.sum(u * s, axis=-1, keepdims=True)
    out_cot[...] = ((s - u * along) * inv_out[:, 0:1]).astype(BF)


def spread_kernel(incoming, landed, catalogue, out, *, chunk):
    stock, _ = catalogue.shape
    slots = incoming.shape[1]
    for r in range(0, stock, chunk):
        hot = jnp.where(r + iota((chunk, slots), 0) == incoming[...], 1.0, 0.0).astype(BF)
        v = dot_nn(hot, landed[...])
        c = catalogue[r : r + chunk, :].astype(F32)
        inv = lax.rsqrt(jnp.sum(c * c, axis=-1, keepdims=True) + EPS_UNIT)
        c = c * inv
        out[r : r + chunk, :] = (v - c * jnp.sum(c * v, axis=-1, keepdims=True)) * inv


def put_pieces(outs, index, here, dp, whole, share):
    if len(outs) == dp:
        for j in range(dp):
            start = pl.multiple_of(jnp.bitwise_xor(here, j) * share, share)
            outs[j][index] = whole[pl.ds(start, share), :]
    else:
        for d in range(dp):
            outs[0][(d,) + index] = whole[d * share : (d + 1) * share, :]


def w_out_kernel(meta, *refs, mp, dp):
    blocks, gated_t, outs, whole = refs[:mp], refs[mp], refs[mp + 1 : -1], refs[-1]
    quarter, width = blocks[0].shape
    for j in range(mp):
        start = pl.multiple_of(jnp.bitwise_xor(meta[1], j) * quarter, quarter)
        whole[pl.ds(start, quarter), :] = blocks[j][...]
    part = dot_nn(gated_t[...], whole[...]).astype(BF)
    lanes = width // dp
    if len(outs) == dp:
        spare = jnp.stack([part[:, d * lanes : (d + 1) * lanes] for d in range(dp)])
        for d in range(dp):
            for j in range(dp):

                @pl.when(jnp.bitwise_xor(meta[0], j) == d)
                def _(d=d, j=j):
                    outs[j][...] = spare[d]
    else:
        for d in range(dp):
            outs[0][d] = part[:, d * lanes : (d + 1) * lanes]


def backward_kernel(meta, *refs, mp, dp):
    blocks = refs[:mp]
    w_out, projected, slope, weights, dscale, norm, inv, normed_t = refs[mp : mp + 8]
    outs = refs[mp + 8 : -3]
    whole, cot, parts = refs[-3:]
    quarter, width = blocks[0].shape
    for j in range(mp):
        start = pl.multiple_of(jnp.bitwise_xor(meta[1], j) * quarter, quarter)
        whole[pl.ds(start, quarter), :] = blocks[j][...]
    rows_all = whole.shape[0]
    cols = w_out.shape[0]
    gated_cot = dot_nt(whole[...], w_out[...]).astype(BF).astype(F32)
    for g in range(rows_all // BLOCK):
        rows = slice(g * BLOCK, (g + 1) * BLOCK)
        for h in range(cols // DH):
            lanes = slice(h * DH, (h + 1) * DH)
            d_gated = gated_cot[rows, lanes]
            n = norm[rows, lanes]
            d_norm = d_gated * projected[0, rows, lanes].astype(F32)
            d_mixed = inv[rows, lanes] * (
                d_norm
                - jnp.mean(d_norm, axis=-1, keepdims=True)
                - n * jnp.mean(d_norm * n, axis=-1, keepdims=True)
            )
            d_mixed = d_mixed.astype(BF)
            d_weights = dot_nt(d_mixed, projected[1, rows, lanes]).astype(BF).astype(F32)
            d_values = dot_tn(weights[h, rows, :], d_mixed)
            d_scores = (d_weights * dscale[h, rows, :]).astype(BF)
            d_queries = dot_nn(d_scores, projected[3, rows, lanes])
            d_keys = dot_tn(d_scores, projected[2, rows, lanes])
            for c, d in enumerate((d_gated * n, d_values, d_queries, d_keys)):
                cot[c, rows, lanes] = (d.astype(BF).astype(F32) * slope[c, rows, lanes]).astype(BF)
    share = width // dp
    for c in range(4):
        parts[...] = dot_nn(normed_t[...], cot[c]).astype(BF)
        put_pieces(outs, (c,), meta[0], dp, parts, share)


def swapped(x, axis, bit):
    size = lax.axis_size(axis)
    return lax.ppermute(x, axis, [(a, a ^ bit) for a in range(size)])


def gather_blocks(x, axis):
    size = lax.axis_size(axis)
    blocks = {0: x}
    bit = size // 2
    while bit:
        for j in list(blocks):
            blocks[j ^ bit] = swapped(blocks[j], axis, bit)
        bit //= 2
    return [blocks[j] for j in range(size)]


def pieces(n, shape, dtype):
    S = jax.ShapeDtypeStruct
    return [S(shape, dtype)] * n if n <= 8 else [S((n,) + shape, dtype)]


def exchange(parts, axis):
    if len(parts) > 1:
        return [p if j == 0 else swapped(p, axis, j) for j, p in enumerate(parts)]
    return [lax.all_to_all(parts[0], axis, split_axis=0, concat_axis=0, tiled=True)]


def summed(parts):
    if len(parts) == 1:
        return jnp.sum(parts[0].astype(F32), axis=0)
    total = parts[0].astype(F32)
    for p in parts[1:]:
        total = total + p.astype(F32)
    return total


def per_device(history, lengths, source, owners, item_rows, catalogue, w_in, w_out):
    dp = lax.axis_size("dp")
    mp = lax.axis_size("mp")
    devices = dp * mp
    near = devices // 2
    seq_dev, steps, part = history.shape
    width = part * mp
    cols = w_in.shape[2]
    rows_all = seq_dev * steps
    quarter = rows_all // mp
    events, top = owners.shape
    asks = events * top
    capacity = max(2, (3 * asks + 2 * devices - 1) // (2 * devices))
    slots = devices * capacity
    stock = catalogue.shape[0]
    per_peer = (seq_dev + dp - 1) // dp
    chunk = math.gcd(slots, 512)
    heads = cols // DH
    S = jax.ShapeDtypeStruct
    here_dp = lax.axis_index("dp")
    place = jnp.stack([here_dp, lax.axis_index("mp")]).astype(I32)
    meta = jnp.concatenate([place, source, lengths])
    seqs = source.shape[0]
    halves = [list(range(near)), list(range(near, devices))]

    def partner(x):
        return swapped(x, "dp", dp // 2)

    def in_half(x):
        return lax.all_to_all(
            x.reshape(near, 2 * capacity, width),
            ("dp", "mp"),
            split_axis=0,
            concat_axis=0,
            tiled=True,
            axis_index_groups=halves,
        ).reshape(slots, width)

    packed = call(
        functools.partial(pack_kernel, dp=dp, seq_dev=seq_dev, per_peer=per_peer),
        [S((dp, per_peer, steps, part), BF)],
        [SM, VM],
        3,
    )(meta, history)
    w_out_blocks = gather_blocks(w_out, "mp")
    arrived = exchange(packed, "dp")
    arrived, w_out_blocks, owners = lax.optimization_barrier((arrived, w_out_blocks, owners))
    rows = call(
        functools.partial(take_kernel, dp=dp, seq_dev=seq_dev, per_peer=per_peer, steps=steps),
        S((rows_all, part), BF),
        [SM] + [VM] * len(arrived),
        1,
        scratch=[pltpu.VMEM((dp, per_peer, steps, part), BF)],
    )(meta, *arrived)
    features = gather_blocks(rows, "mp")

    wanted, code = call(
        functools.partial(ask_kernel, devices=devices, capacity=capacity),
        [S((devices, capacity), I32), S((devices, events), F32)],
        [VM, VM],
        2,
    )(owners, item_rows)
    asked = lax.all_to_all(wanted, ("dp", "mp"), split_axis=0, concat_axis=0, tiled=True)
    asked = asked.reshape(2, near, capacity)
    incoming = jnp.where(here_dp < dp // 2, asked, asked[::-1])
    incoming = incoming.transpose(1, 0, 2).reshape(1, slots)
    looked = call(
        functools.partial(look_kernel, chunk=chunk),
        S((slots, width), BF),
        [VM, HB],
        3,
        out_specs=[HB],
    )(incoming, catalogue)
    code_far = partner(code)
    looked, features, code_far = lax.optimization_barrier((looked, features, code_far))
    items = in_half(looked)

    (normed_t, projected, slope, weights, dscale, norm, inv, gated_t, own, *gated) = call(
        functools.partial(
            forward_kernel,
            mp=mp,
            seqs=seqs,
            seq_dev=seq_dev,
            steps=steps,
            width=width,
            cols=cols,
            quarter=quarter,
        ),
        [
            S((width, rows_all), BF),
            S((4, rows_all, cols), BF),
            S((4, rows_all, cols), F32),
            S((heads, rows_all, BLOCK), BF),
            S((heads, rows_all, BLOCK), F32),
            S((rows_all, cols), F32),
            S((rows_all, cols), F32),
            S((cols, rows_all), BF),
            S((quarter, width), BF),
        ]
        + [S((quarter, cols), BF)] * mp,
        [SM] + [HB] * (mp + 1),
        6,
        scratch=[pltpu.VMEM((rows_all, width), BF), pltpu.VMEM((rows_all, cols), BF)],
        out_specs=[HB] * 9 + [VM] * mp,
        limit=24,
    )(meta, *features, w_in)
    gathered = exchange(gated, "mp")
    unit, unit_bf, inv_out = call(
        functools.partial(out_kernel, mp=mp),
        [S((quarter, width), F32), S((quarter, width), BF), S((quarter, BLOCK), F32)],
        [HB] + [VM] * mp + [HB] * mp,
        2,
    )(own, *gathered, *w_out_blocks)

    unit_far = partner(unit_bf)
    expo, inv_item, total = call(
        functools.partial(
            score_kernel, dp=dp, devices=devices, capacity=capacity, chunk=chunk
        ),
        [S((slots, 2 * events), F32), S((slots, BLOCK), F32), S((1, 2 * events), F32)],
        [SM, HB] + [VM] * 4,
        4,
    )(meta, items, code, code_far, unit_bf, unit_far)
    total_far = partner(total)
    sizes = dict(dp=dp, seqs=seqs, seq_dev=seq_dev, steps=steps, chunk=chunk)
    item_slope, slope_far = call(
        functools.partial(slope_kernel, **sizes),
        [S((events, width), F32), S((events, width), BF)],
        [SM, HB] + [VM] * 4,
        2,
    )(meta, items, expo, inv_item, total, total_far)
    slope_back = partner(slope_far)
    sending = call(
        functools.partial(send_kernel, **sizes),
        S((slots, width), BF),
        [SM] + [VM] * 5,
        3,
        out_specs=[HB],
    )(meta, expo, total, total_far, unit_bf, unit_far)
    out_cot = call(out_cot_kernel, S((events, width), BF), [VM] * 4, 1)(
        unit, inv_out, item_slope, slope_back
    )

    cots = gather_blocks(out_cot, "mp")
    sending, cots = lax.optimization_barrier((sending, cots))
    landed = in_half(sending)
    w_out_part = call(
        functools.partial(w_out_kernel, mp=mp, dp=dp),
        pieces(dp, (cols, width // dp), BF),
        [SM] + [HB] * (mp + 1),
        2,
        scratch=[pltpu.VMEM((rows_all, width), BF)],
    )(meta, *cots, gated_t)
    w_in_part = call(
        functools.partial(backward_kernel, mp=mp, dp=dp),
        pieces(dp, (4, width // dp, cols), BF),
        [SM] + [HB] * (mp + 8),
        6,
        scratch=[
            pltpu.VMEM((rows_all, width), BF),
            pltpu.VMEM((4, rows_all, cols), BF),
            pltpu.VMEM((width, cols), BF),
        ],
        limit=24,
    )(meta, *cots, w_out, projected, slope, weights, dscale, norm, inv, normed_t)
    w_out_grad = summed(exchange(w_out_part, "dp"))
    w_in_grad = summed(exchange(w_in_part, "dp"))
    cat_grad = call(
        functools.partial(spread_kernel, chunk=math.gcd(stock, 128)),
        S((stock, width), F32),
        [VM, HB, HB],
        4,
        out_specs=[HB],
        limit=24,
    )(incoming, landed, catalogue)
    return (w_in_grad, w_out_grad, cat_grad)


def solution(mesh):
    placed = (
        P("dp", None, "mp"),
        P(),
        P(),
        P(("dp", "mp"), None),
        P(("dp", "mp"), None),
        P(("dp", "mp"), None),
        P(None, None, "mp"),
        P("mp", None),
    )
    return jax.shard_map(
        per_device,
        mesh=mesh,
        in_specs=placed,
        out_specs=(P(None, "dp", "mp"), P("mp", "dp"), P(("dp", "mp"), None)),
        check_vma=False,
    )
```

```python
import functools
import math

import jax
import jax.numpy as jnp
from jax import lax
from jax.experimental import pallas as pl
from jax.experimental.pallas import tpu as pltpu
from jax.sharding import PartitionSpec as P

DH = 128
COSINE_DIVISOR = 0.05
EPS_NORM = 1e-05
EPS_UNIT = 1e-06
BF = jnp.bfloat16
F32 = jnp.float32
I32 = jnp.int32
BLOCK = 128

VM = pl.BlockSpec(memory_space=pltpu.VMEM)
SM = pl.BlockSpec(memory_space=pltpu.SMEM)
HB = pl.BlockSpec(memory_space=pl.ANY)


def call(body, out_shape, in_specs, us, scratch=(), limit=16, out_specs=None):
    many = isinstance(out_shape, (list, tuple))
    outs = list(out_shape) if many else [out_shape]
    out_specs = list(out_specs or [VM] * len(outs))

    def run(*args):
        args = list(args)
        far_in = [n for n, spec in enumerate(in_specs) if spec is HB]
        far_out = [n for n, spec in enumerate(out_specs) if spec is HB]
        n_in, n_out, n_own = len(in_specs), len(outs), len(scratch)
        extra = [pltpu.VMEM(args[n].shape, args[n].dtype) for n in far_in]
        extra += [pltpu.VMEM(outs[n].shape, outs[n].dtype) for n in far_out]
        moved = len(far_in) + len(far_out)

        def kernel(*refs):
            ins, res = list(refs[:n_in]), list(refs[n_in : n_in + n_out])
            own = refs[n_in + n_out : n_in + n_out + n_own]
            held = refs[n_in + n_out + n_own :]
            sems = held[-1] if moved else None
            copies = []
            for m, n in enumerate(far_in):
                copies.append(pltpu.make_async_copy(ins[n], held[m], sems.at[m]))
                ins[n] = held[m]
            for c in copies:
                c.start()
            for c in copies:
                c.wait()
            copies = []
            for m, n in enumerate(far_out):
                m += len(far_in)
                copies.append(pltpu.make_async_copy(held[m], res[n], sems.at[m]))
                res[n] = held[m]
            body(*ins, *res, *own)
            for c in copies:
                c.start()
            for c in copies:
                c.wait()

        result = pl.pallas_call(
            kernel,
            out_shape=outs,
            in_specs=list(in_specs),
            out_specs=out_specs,
            scratch_shapes=list(scratch)
            + extra
            + ([pltpu.SemaphoreType.DMA((moved,))] if moved else []),
            compiler_params=pltpu.CompilerParams(vmem_limit_bytes=limit * 2**20),
            cost_estimate=pl.CostEstimate(
                flops=0, bytes_accessed=int(us * 3.3e6), transcendentals=0
            ),
        )(*args)
        return result if many else result[0]

    return run


def dot_nt(a, b):
    return lax.dot_general(a, b, (((1,), (1,)), ((), ())), preferred_element_type=F32)


def dot_tn(a, b):
    return lax.dot_general(a, b, (((0,), (0,)), ((), ())), preferred_element_type=F32)


def dot_nn(a, b):
    return jnp.dot(a, b, preferred_element_type=F32)


def iota(shape, dim):
    return lax.broadcasted_iota(I32, shape, dim)


def length_of(meta, slot, seqs):
    return meta[2 + seqs + meta[2 + slot]]


def pack_kernel(meta, hist, owners_t, rows_t, out, code, *, dp, seq_dev, per_peer, mp, capacity):
    here = meta[0]
    steps, part = hist.shape[1], hist.shape[2]

    def per_dest(d, carry):
        def per_slot(i, count):
            src = meta[2 + d * seq_dev + i]
            hit = lax.div(src, seq_dev) == here

            @pl.when(hit)
            def _():
                start = pl.multiple_of(count * steps, steps)
                out[d, pl.ds(start, steps), :] = hist[src - here * seq_dev]

            return count + hit.astype(I32)

        lax.fori_loop(0, seq_dev, per_slot, jnp.int32(0))
        return carry

    lax.fori_loop(0, dp, per_dest, jnp.int32(0))
    top, events = owners_t.shape
    devices = dp * mp
    o_id = iota((devices, events), 0)
    named = jnp.zeros((devices, events), F32)
    row = jnp.zeros((devices, events), F32)
    positive = jnp.zeros((devices, events), F32)
    for j in range(top):
        same = jnp.where(owners_t[j : j + 1, :] == o_id, 1.0, 0.0)
        named = named + same
        row = row + same * rows_t[j : j + 1, :].astype(F32)
        if j == 0:
            positive = same
    before = (iota((events, events), 0) < iota((events, events), 1)).astype(BF)
    rank = dot_nn(named.astype(BF), before)
    code[...] = jnp.where(named > 0.0, 2.0 * rank + 1.0 + positive, 0.0)
    rank = jnp.where(named > 0.0, rank, -1.0)
    lane = iota((devices, part), 1)
    wanted = jnp.zeros((devices, part), F32)
    for c in range(capacity):
        one = jnp.sum(jnp.where(rank == float(c), row, 0.0), axis=1, keepdims=True)
        wanted = jnp.where(lane == c, one, wanted)
    high = jnp.floor(wanted * (1.0 / 256.0))
    low = wanted - 256.0 * high
    none = jnp.zeros((8 - mp, part), F32)
    for d in range(dp):
        mine = slice(d * mp, (d + 1) * mp)
        digits = [high[mine], none, low[mine], none] if mp < 8 else [high[mine], low[mine]]
        out[d, per_peer * steps :, :] = jnp.concatenate(digits, axis=0).astype(BF)


def take_kernel(meta, arrived, out, *refs, dp, mp, seq_dev, per_peer, steps):
    asked, digits = refs[:mp], refs[mp]
    here = meta[0]
    anchors = [lax.div(meta[2 + here * seq_dev + k], seq_dev) for k in range(seq_dev)]
    for k in range(seq_dev):
        rank = jnp.int32(0)
        for earlier in range(k):
            rank = rank + (anchors[earlier] == anchors[k]).astype(I32)
        start = pl.multiple_of(rank * steps, steps)
        out[k * steps : (k + 1) * steps, :] = arrived[anchors[k], pl.ds(start, steps), :]
    digits[...] = arrived[:, per_peer * steps :, :].astype(F32)
    capacity = asked[0].shape[1]
    for j in range(mp):
        owner = jnp.bitwise_xor(meta[1], j)
        for d in range(dp):
            number = 256.0 * digits[d, pl.ds(owner, 1), :] + digits[d, pl.ds(8 + owner, 1), :]
            asked[j][d : d + 1, :] = number[:, :capacity].astype(I32)


def forward_kernel(meta, *refs, mp, seqs, seq_dev, steps, width, cols, quarter):
    blocks = refs[:mp]
    w_in = refs[mp]
    wide, projected, turned, own = refs[mp + 1 : mp + 5]
    gated_out = refs[mp + 5 : 2 * mp + 5]
    feat, gated = refs[2 * mp + 5 :]
    here_dp = meta[0]
    here_mp = meta[1]
    part = width // mp
    counts = [length_of(meta, here_dp * seq_dev + k, seqs) for k in range(seq_dev)]
    for j in range(mp):
        start = pl.multiple_of(jnp.bitwise_xor(here_mp, j) * part, part)
        feat[:, pl.ds(start, part)] = blocks[j][...]
    rows_all = seq_dev * steps
    own[...] = feat[pl.ds(pl.multiple_of(here_mp * quarter, quarter), quarter), :]
    for g in range(rows_all // BLOCK):
        rows = slice(g * BLOCK, (g + 1) * BLOCK)
        x = feat[rows, :].astype(F32)
        centered = x - jnp.mean(x, axis=-1, keepdims=True)
        spread = jnp.mean(centered * centered, axis=-1, keepdims=True)
        y = (centered * lax.rsqrt(spread + EPS_NORM)).astype(BF)
        feat[rows, :] = y
        turned[:width, rows] = y.T
    for c in range(4):
        pre = dot_nn(feat[...], w_in[c])
        sigma = jax.nn.sigmoid(pre)
        projected[c] = (pre * sigma).astype(BF)
        wide[c] = sigma * (1.0 + pre * (1.0 - sigma))
    root = 1.0 / math.sqrt(DH)
    t_id = iota((BLOCK, BLOCK), 0)
    s_id = iota((BLOCK, BLOCK), 1)
    per_block = BLOCK // steps
    causal = (t_id // steps == s_id // steps) & (s_id <= t_id)
    for g in range(rows_all // BLOCK):
        rows = slice(g * BLOCK, (g + 1) * BLOCK)
        count = jnp.zeros((BLOCK, BLOCK), I32)
        for i in range(per_block):
            count = jnp.where(t_id // steps == i, counts[g * per_block + i], count)
        allowed = causal & (s_id % steps < count)
        scale = jnp.where(allowed, 1.0 / count.astype(F32), 0.0)
        for h in range(cols // DH):
            lanes = slice(h * DH, (h + 1) * DH)
            scores = dot_nt(projected[2, rows, lanes], projected[3, rows, lanes]) * root
            sigma = jax.nn.sigmoid(scores)
            weights = (scores * sigma * scale).astype(BF)
            projected[4, rows, lanes] = weights
            wide[6, rows, lanes] = sigma * (1.0 + scores * (1.0 - sigma)) * (scale * root)
            mixed = dot_nn(weights, projected[1, rows, lanes])
            centered = mixed - jnp.mean(mixed, axis=-1, keepdims=True)
            spread = jnp.mean(centered * centered, axis=-1, keepdims=True)
            inv = lax.rsqrt(spread + EPS_NORM)
            norm = centered * inv
            wide[4, rows, lanes] = norm
            wide[5, rows, lanes] = jnp.broadcast_to(inv, norm.shape)
            done = (norm * projected[0, rows, lanes].astype(F32)).astype(BF)
            gated[rows, lanes] = done
            turned[width + h * DH : width + (h + 1) * DH, rows] = done.T
    for j in range(mp):
        start = pl.multiple_of(jnp.bitwise_xor(here_mp, j) * quarter, quarter)
        gated_out[j][...] = gated[pl.ds(start, quarter), :]


def out_kernel(meta, own, w_out, *refs, mp):
    gathered = refs[:mp]
    unit, unit_bf, inv_o = refs[mp:]
    cols = gathered[0].shape[1]
    total = own[...].astype(F32)
    for j in range(mp):
        start = pl.multiple_of(jnp.bitwise_xor(meta[1], j) * cols, cols)
        total = total + dot_nn(gathered[j][...], w_out[pl.ds(start, cols), :])
    inv = lax.rsqrt(jnp.sum(total * total, axis=-1, keepdims=True) + EPS_UNIT)
    u = total * inv
    unit[...] = u
    unit_bf[...] = u.astype(BF)
    inv_o[...] = jnp.broadcast_to(inv, inv_o.shape)


def look_kernel(meta, *refs, mp, dp, capacity, chunk, share):
    asked, catalogue, looked, incoming, returning = refs[:mp], *refs[mp:]
    stock, _ = catalogue.shape
    groups = dp * mp
    slots = groups * capacity
    half = dp // 2
    table = jnp.concatenate([a[...] for a in asked], axis=0).astype(F32)
    slot = iota((1, slots), 1).astype(F32)
    group = jnp.floor((slot + 0.5) * (1.0 / capacity))
    local = slot - group * capacity
    column = (iota((capacity, slots), 0).astype(F32) == local).astype(F32)
    spread = lax.dot_general(
        table,
        column,
        (((1,), (0,)), ((), ())),
        precision=lax.Precision.HIGHEST,
        preferred_element_type=F32,
    )
    line = iota((groups, 1), 0)
    offset = lax.div(line, dp)
    index = line - offset * dp
    side = (index >= half) != (meta[0] >= half)
    near = jnp.where(index >= half, index - half, index)
    first = (near * mp + jnp.bitwise_xor(offset, meta[1])) * 2 + side.astype(I32)
    here = jnp.where(meta[0] >= half, meta[0] - half, meta[0])
    second = (offset * half + jnp.bitwise_xor(near, here)) * 2 + side.astype(I32)
    rows = [
        jnp.sum(jnp.where(group == g.astype(F32), spread, 0.0), axis=0, keepdims=True).astype(I32)
        for g in (first, second)
    ]
    incoming[...] = rows[0]
    returning[...] = rows[1] if share else rows[0]
    for s in range(0, slots, chunk):
        hot = jnp.where(iota((stock, chunk), 0) == incoming[:, s : s + chunk], 1.0, 0.0).astype(BF)
        looked[s : s + chunk, :] = dot_tn(hot, catalogue[...]).astype(BF)


def score_kernel(
    meta, items, code, code_far, unit, unit_far, expo, inv_o, total_o,
    *, dp, devices, capacity, chunk,
):
    events = unit.shape[0]
    near = devices // 2
    slots = items.shape[0]
    half = pl.multiple_of(lax.div(meta[0], dp // 2) * near, near)
    codes_in = [c[pl.ds(half, near), :].astype(BF) for c in (code, code_far)]
    for s in range(0, slots, chunk):
        rows = slice(s, s + chunk)
        x = items[rows, :]
        xf = x.astype(F32)
        inv = lax.rsqrt(jnp.sum(xf * xf, axis=-1, keepdims=True) + EPS_UNIT)
        inv_o[rows, :] = jnp.broadcast_to(inv, (chunk, BLOCK))
        slot = s + iota((chunk, 1), 0).astype(F32)
        owner = jnp.floor((slot + 0.5) * (1.0 / (2 * capacity)))
        local = slot - owner * (2 * capacity)
        far = local >= capacity
        local = jnp.where(far, local - capacity, local)
        named = owner == iota((chunk, near), 1).astype(F32)
        for side in range(2):
            lanes = slice(side * events, (side + 1) * events)
            u = (unit, unit_far)[side][...]
            logits = dot_nt(x, u) * (inv * (1.0 / COSINE_DIVISOR))
            spread = jnp.where(named & (far == (side == 1)), 1.0, 0.0).astype(BF)
            codes = dot_nn(spread, codes_in[side])
            first = codes == 2.0 * local + 2.0
            other = codes == 2.0 * local + 1.0
            e = jnp.exp(logits)
            total_o[:, lanes] = (
                jnp.sum(jnp.where(first | other, e, 0.0), axis=0, keepdims=True)
                + (total_o[:, lanes] if s else 0.0)
            )
            expo[rows, lanes] = jnp.where(first, -e, jnp.where(other, e, 0.0))


def shares(meta, expo, total, total_far, dp, seqs, seq_dev, steps):
    events = total.shape[1] // 2
    position = meta[1] * events + iota((1, events), 1)
    valid = []
    for base in (meta[0], jnp.bitwise_xor(meta[0], dp // 2)):
        v = jnp.zeros((1, events), F32)
        for k in range(seq_dev):
            step = position - k * steps
            v = jnp.where((step >= 0) & (step < length_of(meta, base * seq_dev + k, seqs)), 1.0, v)
        valid.append(v)
    valid = jnp.concatenate(valid, axis=1) * (1.0 / COSINE_DIVISOR)
    full = total[...] + jnp.concatenate([total_far[:, events:], total_far[:, :events]], axis=1)
    factor = valid / full
    return lambda rows: jnp.abs(expo[rows, :]) * factor - jnp.where(expo[rows, :] < 0.0, valid, 0.0)


def slope_kernel(
    meta, items, code, code_far, expo, inv, total, total_far, slope, slope_far, ledger,
    *, dp, seqs, seq_dev, steps, chunk,
):
    share = shares(meta, expo, total, total_far, dp, seqs, seq_dev, steps)
    events, width = slope.shape
    both = jnp.zeros((2 * events, width), F32)
    for s in range(0, items.shape[0], chunk):
        rows = slice(s, s + chunk)
        both = both + dot_tn((share(rows) * inv[rows, 0:1]).astype(BF), items[rows, :])
    near = ledger.shape[0] // 2
    each = items.shape[0] // near
    for o in range(near):
        part = share(slice(o * each, (o + 1) * each))
        ledger[o : o + 1, :] = jnp.sum(part, axis=0, keepdims=True)
    half = pl.multiple_of(lax.div(meta[0], dp // 2) * near, near)
    for side, c in enumerate((code, code_far)):
        ledger[near:, side * events : (side + 1) * events] = c[pl.ds(half, near), :]
    slope[...] = both[:events]
    slope_far[...] = both[events:].astype(BF)


def send_kernel(
    meta, expo, total, total_far, unit, unit_far, sending,
    *, dp, seqs, seq_dev, steps, chunk,
):
    share = shares(meta, expo, total, total_far, dp, seqs, seq_dev, steps)
    events = unit.shape[0]
    for s in range(0, expo.shape[0], chunk):
        rows = slice(s, s + chunk)
        hot = jnp.where(expo[rows, :] == 0.0, 0.0, 1.0).astype(BF)
        unit_rows = dot_nn(hot[:, :events], unit[...]) + dot_nn(hot[:, events:], unit_far[...])
        weight = jnp.sum(share(rows), axis=1, keepdims=True)
        sending[rows, :] = (unit_rows * weight).astype(BF)


def mail_kernel(meta, *refs, half, mp, capacity):
    units, ledgers, outs, hots = refs[: 2 * half], refs[2 * half : 3 * half], refs[3 * half : -1], refs[-1]
    events, width = units[0].shape
    near = ledgers[0].shape[0] // 2
    here = jnp.where(meta[0] >= half, meta[0] - half, meta[0])
    slot = iota((2 * capacity, 2 * events), 0)
    event = iota((2 * capacity, 2 * events), 1)
    far = slot >= capacity
    local = jnp.where(far, slot - capacity, slot).astype(F32)
    same = far == (event >= events)
    for j in range(half):
        weights = []
        for k in range(mp):
            o = here * mp + jnp.bitwise_xor(meta[1], k)
            code = ledgers[j][pl.ds(near + o, 1), :]
            mine = same & (jnp.floor((code - 1.0) * 0.5) == local)
            hots[k * 2 * capacity : (k + 1) * 2 * capacity, :] = mine.astype(BF)
            weight = jnp.where(mine, ledgers[j][pl.ds(o, 1), :], 0.0)
            weights.append(jnp.sum(weight, axis=1, keepdims=True))
        rows = dot_nn(hots[:, :events], units[2 * j][...])
        rows = rows + dot_nn(hots[:, events:], units[2 * j + 1][...])
        for k in range(mp):
            part = rows[k * 2 * capacity : (k + 1) * 2 * capacity] * weights[k]
            outs[k][j * 2 * capacity : (j + 1) * 2 * capacity, :] = part.astype(BF)


def out_cot_kernel(unit, inv_out, slope, slope_far, out_cot):
    u = unit[...]
    s = slope[...] + slope_far[...].astype(F32)
    along = jnp.sum(u * s, axis=-1, keepdims=True)
    out_cot[...] = ((s - u * along) * inv_out[:, 0:1]).astype(BF)


def spread_kernel(incoming, catalogue, *refs, chunk):
    landed, out = refs[:-1], refs[-1]
    stock, _ = catalogue.shape
    slots = incoming.shape[1]
    for r in range(0, stock, chunk):
        hot = jnp.where(r + iota((chunk, slots), 0) == incoming[...], 1.0, 0.0).astype(BF)
        v, at = 0.0, 0
        for part in landed:
            v = v + dot_nn(hot[:, at : at + part.shape[0]], part[...])
            at += part.shape[0]
        c = catalogue[r : r + chunk, :].astype(F32)
        inv = lax.rsqrt(jnp.sum(c * c, axis=-1, keepdims=True) + EPS_UNIT)
        c = c * inv
        out[r : r + chunk, :] = (v - c * jnp.sum(c * v, axis=-1, keepdims=True)) * inv


def w_out_kernel(meta, *refs, mp, dp):
    blocks, turned, out, whole = refs[:mp], *refs[mp:]
    quarter, width = blocks[0].shape
    for j in range(mp):
        start = pl.multiple_of(jnp.bitwise_xor(meta[1], j) * quarter, quarter)
        whole[pl.ds(start, quarter), :] = blocks[j][...]
    part = dot_nn(turned[width:, :], whole[...]).astype(BF)
    lanes = width // dp
    for d in range(dp):
        out[d] = part[:, d * lanes : (d + 1) * lanes]


def backward_kernel(meta, *refs, mp, dp):
    blocks = refs[:mp]
    w_out, wide, projected, turned, out, whole, cot = refs[mp:]
    quarter, width = blocks[0].shape
    for j in range(mp):
        start = pl.multiple_of(jnp.bitwise_xor(meta[1], j) * quarter, quarter)
        whole[pl.ds(start, quarter), :] = blocks[j][...]
    rows_all = whole.shape[0]
    cols = w_out.shape[0]
    gated_cot = dot_nt(whole[...], w_out[...]).astype(BF).astype(F32)
    for g in range(rows_all // BLOCK):
        rows = slice(g * BLOCK, (g + 1) * BLOCK)
        for h in range(cols // DH):
            lanes = slice(h * DH, (h + 1) * DH)
            d_gated = gated_cot[rows, lanes]
            n = wide[4, rows, lanes]
            d_norm = d_gated * projected[0, rows, lanes].astype(F32)
            d_mixed = wide[5, rows, lanes] * (
                d_norm
                - jnp.mean(d_norm, axis=-1, keepdims=True)
                - n * jnp.mean(d_norm * n, axis=-1, keepdims=True)
            )
            d_mixed = d_mixed.astype(BF)
            d_weights = dot_nt(d_mixed, projected[1, rows, lanes]).astype(BF).astype(F32)
            d_values = dot_tn(projected[4, rows, lanes], d_mixed)
            d_scores = (d_weights * wide[6, rows, lanes]).astype(BF)
            d_queries = dot_nn(d_scores, projected[3, rows, lanes])
            d_keys = dot_tn(d_scores, projected[2, rows, lanes])
            for c, d in enumerate((d_gated * n, d_values, d_queries, d_keys)):
                cot[c, rows, lanes] = (d.astype(BF).astype(F32) * wide[c, rows, lanes]).astype(BF)
    share = width // dp
    for c in range(4):
        part = dot_nn(turned[:width, :], cot[c]).astype(BF)
        for d in range(dp):
            out[d, c] = part[d * share : (d + 1) * share, :]


def swapped(x, axis, bit):
    size = lax.axis_size(axis)
    return lax.ppermute(x, axis, [(a, a ^ bit) for a in range(size)])


def gather_blocks(x, axis):
    size = lax.axis_size(axis)
    blocks = {0: x}
    bit = size // 2
    while bit:
        for j in list(blocks):
            blocks[j ^ bit] = swapped(blocks[j], axis, bit)
        bit //= 2
    return [blocks[j] for j in range(size)]


def exchange(parts, axis):
    return [p if j == 0 else swapped(p, axis, j) for j, p in enumerate(parts)]


def summed(x):
    got = lax.all_to_all(x, "dp", split_axis=0, concat_axis=0, tiled=True)
    return jnp.sum(got.astype(F32), axis=0)


def per_device(history, lengths, source, owners, item_rows, catalogue, w_in, w_out):
    dp = lax.axis_size("dp")
    mp = lax.axis_size("mp")
    devices = dp * mp
    near = devices // 2
    seq_dev, steps, part = history.shape
    width = part * mp
    cols = w_in.shape[2]
    rows_all = seq_dev * steps
    quarter = rows_all // mp
    events, top = owners.shape
    asks = events * top
    capacity = max(2, (3 * asks + 2 * devices - 1) // (2 * devices))
    slots = devices * capacity
    stock = catalogue.shape[0]
    per_peer = (seq_dev + dp - 1) // dp
    chunk = math.gcd(slots, 512)
    short = dp <= 8
    S = jax.ShapeDtypeStruct
    here_dp = lax.axis_index("dp")
    place = jnp.stack([here_dp, lax.axis_index("mp")]).astype(I32)
    meta = jnp.concatenate([place, source, lengths])
    seqs = source.shape[0]
    halves = [list(range(near)), list(range(near, devices))]

    def partner(x):
        return swapped(x, "dp", dp // 2)

    def in_half(x):
        return lax.all_to_all(
            x.reshape(near, 2 * capacity, width),
            ("dp", "mp"),
            split_axis=0,
            concat_axis=0,
            tiled=True,
            axis_index_groups=halves,
        ).reshape(slots, width)

    w_out_all = lax.all_gather(w_out, "mp", axis=0, tiled=True)
    packed, code = call(
        functools.partial(
            pack_kernel, dp=dp, seq_dev=seq_dev, per_peer=per_peer, mp=mp, capacity=capacity
        ),
        [S((dp, per_peer * steps + 16, part), BF), S((devices, events), F32)],
        [SM, VM, VM, VM],
        4,
    )(meta, history, owners.T, item_rows.T)
    arrived = lax.all_to_all(packed, "dp", split_axis=0, concat_axis=0, tiled=True)
    rows, *asked = call(
        functools.partial(
            take_kernel, dp=dp, mp=mp, seq_dev=seq_dev, per_peer=per_peer, steps=steps
        ),
        [S((rows_all, part), BF)] + [S((dp, capacity), I32)] * mp,
        [SM, VM],
        1,
        scratch=[pltpu.VMEM((dp, 16, part), F32)],
    )(meta, arrived)
    features = gather_blocks(rows, "mp")
    asked = exchange(asked, "mp")
    code_far = partner(code)
    looked, incoming, returning = call(
        functools.partial(
            look_kernel, mp=mp, dp=dp, capacity=capacity, chunk=chunk, share=short
        ),
        [S((slots, width), BF), S((1, slots), I32), S((1, slots), I32)],
        [SM] + [VM] * mp + [HB],
        4,
        out_specs=[HB, VM, VM],
    )(meta, *asked, catalogue)
    looked, features, code_far = lax.optimization_barrier((looked, features, code_far))
    items = in_half(looked)

    wide, projected, turned, own, *gated = call(
        functools.partial(
            forward_kernel,
            mp=mp,
            seqs=seqs,
            seq_dev=seq_dev,
            steps=steps,
            width=width,
            cols=cols,
            quarter=quarter,
        ),
        [
            S((7, rows_all, cols), F32),
            S((5, rows_all, cols), BF),
            S((width + cols, rows_all), BF),
            S((quarter, width), BF),
        ]
        + [S((quarter, cols), BF)] * mp,
        [SM] + [HB] * (mp + 1),
        6,
        scratch=[pltpu.VMEM((rows_all, width), BF), pltpu.VMEM((rows_all, cols), BF)],
        out_specs=[HB] * 4 + [VM] * mp,
        limit=24,
    )(meta, *features, w_in)
    gathered = exchange(gated, "mp")
    unit, unit_bf, inv_out = call(
        functools.partial(out_kernel, mp=mp),
        [S((quarter, width), F32), S((quarter, width), BF), S((quarter, BLOCK), F32)],
        [SM, HB, HB] + [VM] * mp,
        2,
    )(meta, own, w_out_all, *gathered)

    unit_far = partner(unit_bf)
    expo, inv_item, total = call(
        functools.partial(
            score_kernel, dp=dp, devices=devices, capacity=capacity, chunk=chunk
        ),
        [S((slots, 2 * events), F32), S((slots, BLOCK), F32), S((1, 2 * events), F32)],
        [SM, HB] + [VM] * 4,
        4,
    )(meta, items, code, code_far, unit_bf, unit_far)
    total_far = partner(total)
    sizes = dict(dp=dp, seqs=seqs, seq_dev=seq_dev, steps=steps, chunk=chunk)
    item_slope, slope_far, ledger = call(
        functools.partial(slope_kernel, **sizes),
        [S((events, width), F32), S((events, width), BF), S((2 * near, 2 * events), F32)],
        [SM, HB] + [VM] * 6,
        3,
    )(meta, items, code, code_far, expo, inv_item, total, total_far)
    slope_back = partner(slope_far)
    out_cot = call(out_cot_kernel, S((events, width), BF), [VM] * 4, 1)(
        unit, inv_out, item_slope, slope_back
    )
    cots = gather_blocks(out_cot, "mp")
    if short:
        _, mail_unit, mail_far, mail_ledger = lax.optimization_barrier(
            (out_cot, unit_bf, unit_far, ledger)
        )
        ledgers = [ledger] + [swapped(mail_ledger, "dp", j) for j in range(1, dp // 2)]
        units = [unit_bf, unit_far]
        for j in range(1, dp // 2):
            units += [swapped(mail_unit, "dp", j), swapped(mail_far, "dp", j)]

    w_out_part = call(
        functools.partial(w_out_kernel, mp=mp, dp=dp),
        S((dp, cols, width // dp), BF),
        [SM] + [HB] * (mp + 1),
        2,
        scratch=[pltpu.VMEM((rows_all, width), BF)],
    )(meta, *cots, turned)
    w_in_part = call(
        functools.partial(backward_kernel, mp=mp, dp=dp),
        S((dp, 4, width // dp, cols), BF),
        [SM] + [HB] * (mp + 4),
        6,
        scratch=[
            pltpu.VMEM((rows_all, width), BF),
            pltpu.VMEM((4, rows_all, cols), BF),
        ],
        limit=24,
    )(meta, *cots, w_out, wide, projected, turned)
    w_out_grad = summed(w_out_part)
    w_in_grad = summed(w_in_part)

    if short:
        _, units, ledgers = lax.optimization_barrier((w_in_part, units, ledgers))
        mail = call(
            functools.partial(mail_kernel, half=dp // 2, mp=mp, capacity=capacity),
            [S((dp * capacity, width), BF)] * mp,
            [SM] + [HB] * len(units) + [VM] * len(ledgers),
            4,
            scratch=[pltpu.VMEM((mp * 2 * capacity, 2 * events), BF)],
        )(meta, *units, *ledgers)
        landed = exchange(mail, "mp")
    else:
        sending = call(
            functools.partial(send_kernel, **sizes),
            S((slots, width), BF),
            [SM] + [VM] * 5,
            3,
        )(meta, expo, total, total_far, unit_bf, unit_far)
        landed = [in_half(sending)]
    cat_grad = call(
        functools.partial(spread_kernel, chunk=math.gcd(stock, 128)),
        S((stock, width), F32),
        [VM, HB] + [HB] * len(landed),
        4,
        out_specs=[HB],
        limit=24,
    )(returning, catalogue, *landed)
    return (w_in_grad, w_out_grad, cat_grad)


def solution(mesh):
    placed = (
        P("dp", None, "mp"),
        P(),
        P(),
        P(("dp", "mp"), None),
        P(("dp", "mp"), None),
        P(("dp", "mp"), None),
        P(None, None, "mp"),
        P("mp", None),
    )
    return jax.shard_map(
        per_device,
        mesh=mesh,
        in_specs=placed,
        out_specs=(P(None, "dp", "mp"), P("mp", "dp"), P(("dp", "mp"), None)),
        check_vma=False,
    )
```

```python
import functools
import math

import jax
import jax.numpy as jnp
from jax import lax
from jax.experimental import pallas as pl
from jax.experimental.pallas import tpu as pltpu
from jax.sharding import PartitionSpec as P

DH = 128
COSINE_DIVISOR = 0.05
EPS_NORM = 1e-05
EPS_UNIT = 1e-06
BF = jnp.bfloat16
F32 = jnp.float32
I32 = jnp.int32
BLOCK = 128

VM = pl.BlockSpec(memory_space=pltpu.VMEM)
SM = pl.BlockSpec(memory_space=pltpu.SMEM)
HB = pl.BlockSpec(memory_space=pltpu.HBM)


def call(body, out_shape, in_specs, us, scratch=(), limit=16, out_specs=None):
    many = isinstance(out_shape, (list, tuple))
    outs = list(out_shape) if many else [out_shape]
    out_specs = list(out_specs or [VM] * len(outs))

    def run(*args):
        args = list(args)
        far_in = [n for n, spec in enumerate(in_specs) if spec is HB]
        far_out = [n for n, spec in enumerate(out_specs) if spec is HB]
        n_in, n_out, n_own = len(in_specs), len(outs), len(scratch)
        extra = [pltpu.VMEM(args[n].shape, args[n].dtype) for n in far_in]
        extra += [pltpu.VMEM(outs[n].shape, outs[n].dtype) for n in far_out]
        moved = len(far_in) + len(far_out)

        def kernel(*refs):
            ins, res = list(refs[:n_in]), list(refs[n_in : n_in + n_out])
            own = refs[n_in + n_out : n_in + n_out + n_own]
            held = refs[n_in + n_out + n_own :]
            sems = held[-1] if moved else None
            copies = []
            for m, n in enumerate(far_in):
                copies.append(pltpu.make_async_copy(ins[n], held[m], sems.at[m]))
                ins[n] = held[m]
            for c in copies:
                c.start()
            for c in copies:
                c.wait()
            copies = []
            for m, n in enumerate(far_out):
                m += len(far_in)
                copies.append(pltpu.make_async_copy(held[m], res[n], sems.at[m]))
                res[n] = held[m]
            body(*ins, *res, *own)
            for c in copies:
                c.start()
            for c in copies:
                c.wait()

        result = pl.pallas_call(
            kernel,
            out_shape=outs,
            in_specs=list(in_specs),
            out_specs=out_specs,
            scratch_shapes=list(scratch)
            + extra
            + ([pltpu.SemaphoreType.DMA((moved,))] if moved else []),
            compiler_params=pltpu.CompilerParams(vmem_limit_bytes=limit * 2**20),
            cost_estimate=pl.CostEstimate(
                flops=0, bytes_accessed=int(us * 3.3e6), transcendentals=0
            ),
        )(*args)
        return result if many else result[0]

    return run


def dot_nt(a, b):
    return lax.dot_general(a, b, (((1,), (1,)), ((), ())), preferred_element_type=F32)


def dot_tn(a, b):
    return lax.dot_general(a, b, (((0,), (0,)), ((), ())), preferred_element_type=F32)


def dot_nn(a, b):
    return jnp.dot(a, b, preferred_element_type=F32)


def iota(shape, dim):
    return lax.broadcasted_iota(I32, shape, dim)


def length_of(meta, slot, seqs):
    return meta[2 + seqs + meta[2 + slot]]


def pack_kernel(meta, hist, owners_t, rows_t, out, code, *, dp, seq_dev, per_peer, mp, capacity):
    here = meta[0]
    steps, part = hist.shape[1], hist.shape[2]

    def per_dest(d, carry):
        def per_slot(i, count):
            src = meta[2 + d * seq_dev + i]
            hit = lax.div(src, seq_dev) == here

            @pl.when(hit)
            def _():
                value = hist[src - here * seq_dev]
                for side in range(2):
                    start = pl.multiple_of((side * per_peer + count) * steps, steps)
                    out[jnp.bitwise_xor(d, side * (dp // 2)), pl.ds(start, steps), :] = value

            return count + hit.astype(I32)

        lax.fori_loop(0, seq_dev, per_slot, jnp.int32(0))
        return carry

    lax.fori_loop(0, dp, per_dest, jnp.int32(0))
    top, events = owners_t.shape
    devices = dp * mp
    o_id = iota((devices, events), 0)
    named = jnp.zeros((devices, events), F32)
    row = jnp.zeros((devices, events), F32)
    positive = jnp.zeros((devices, events), F32)
    for j in range(top):
        same = jnp.where(owners_t[j : j + 1, :] == o_id, 1.0, 0.0)
        named = named + same
        row = row + same * rows_t[j : j + 1, :].astype(F32)
        if j == 0:
            positive = same
    before = (iota((events, events), 0) < iota((events, events), 1)).astype(BF)
    rank = dot_nn(named.astype(BF), before)
    code[...] = jnp.where(named > 0.0, 2.0 * rank + 1.0 + positive, 0.0)
    rank = jnp.where(named > 0.0, rank, -1.0)
    lane = iota((devices, part), 1)
    wanted = jnp.zeros((devices, part), F32)
    for c in range(capacity):
        one = jnp.sum(jnp.where(rank == float(c), row, 0.0), axis=1, keepdims=True)
        wanted = jnp.where(lane == c, one, wanted)
    high = jnp.floor(wanted * (1.0 / 256.0))
    low = wanted - 256.0 * high
    none = jnp.zeros((8 - mp, part), F32)
    for d in range(dp):
        mine = slice(d * mp, (d + 1) * mp)
        digits = [high[mine], none, low[mine], none] if mp < 8 else [high[mine], low[mine]]
        out[d, 2 * per_peer * steps :, :] = jnp.concatenate(digits, axis=0).astype(BF)


def take_kernel(meta, arrived, out, *, dp, seq_dev, per_peer, steps):
    for side in range(2):
        block = jnp.bitwise_xor(meta[0], side * (dp // 2))
        anchors = [lax.div(meta[2 + block * seq_dev + k], seq_dev) for k in range(seq_dev)]
        for k in range(seq_dev):
            rank = jnp.int32(side * per_peer)
            for earlier in range(k):
                rank = rank + (anchors[earlier] == anchors[k]).astype(I32)
            start = pl.multiple_of(rank * steps, steps)
            at = (side * seq_dev + k) * steps
            out[at : at + steps, :] = arrived[anchors[k], pl.ds(start, steps), :]
    base = 2 * seq_dev * steps
    for d in range(dp):
        out[base + d * 16 : base + (d + 1) * 16, :] = arrived[d, 2 * per_peer * steps :, :]


def forward_kernel(meta, *refs, mp, dp, seqs, seq_dev, steps, width, cols, quarter):
    blocks = refs[:mp]
    w_in = refs[mp]
    wide, projected, turned, own = refs[mp + 1 : mp + 5]
    gated_out = refs[mp + 5 : 2 * mp + 5]
    feat, gated = refs[2 * mp + 5 :]
    here_mp = meta[1]
    part = width // mp
    counts = [
        length_of(meta, block * seq_dev + k, seqs)
        for block in (meta[0], jnp.bitwise_xor(meta[0], dp // 2))
        for k in range(seq_dev)
    ]
    half_rows = seq_dev * steps
    rows_all = 2 * half_rows
    for j in range(mp):
        start = pl.multiple_of(jnp.bitwise_xor(here_mp, j) * part, part)
        feat[:, pl.ds(start, part)] = blocks[j][:rows_all, :]
    for side in range(2):
        start = pl.multiple_of(side * half_rows + here_mp * quarter, quarter)
        own[side * quarter : (side + 1) * quarter, :] = feat[pl.ds(start, quarter), :]
    for g in range(rows_all // BLOCK):
        rows = slice(g * BLOCK, (g + 1) * BLOCK)
        x = feat[rows, :].astype(F32)
        centered = x - jnp.mean(x, axis=-1, keepdims=True)
        spread = jnp.mean(centered * centered, axis=-1, keepdims=True)
        y = (centered * lax.rsqrt(spread + EPS_NORM)).astype(BF)
        feat[rows, :] = y
        turned[:width, rows] = y.T
    for c in range(4):
        pre = dot_nn(feat[...], w_in[c])
        sigma = jax.nn.sigmoid(pre)
        projected[c] = (pre * sigma).astype(BF)
        projected[5 + c] = (sigma * (1.0 + pre * (1.0 - sigma))).astype(BF)
    root = 1.0 / math.sqrt(DH)
    t_id = iota((BLOCK, BLOCK), 0)
    s_id = iota((BLOCK, BLOCK), 1)
    per_block = BLOCK // steps
    causal = (t_id // steps == s_id // steps) & (s_id <= t_id)
    for g in range(rows_all // BLOCK):
        rows = slice(g * BLOCK, (g + 1) * BLOCK)
        count = jnp.zeros((BLOCK, BLOCK), I32)
        for i in range(per_block):
            count = jnp.where(t_id // steps == i, counts[g * per_block + i], count)
        allowed = causal & (s_id % steps < count)
        scale = jnp.where(allowed, 1.0 / count.astype(F32), 0.0)
        for h in range(cols // DH):
            lanes = slice(h * DH, (h + 1) * DH)
            scores = dot_nt(projected[2, rows, lanes], projected[3, rows, lanes]) * root
            sigma = jax.nn.sigmoid(scores)
            weights = (scores * sigma * scale).astype(BF)
            projected[4, rows, lanes] = weights
            wide[2, rows, lanes] = sigma * (1.0 + scores * (1.0 - sigma)) * (scale * root)
            mixed = dot_nn(weights, projected[1, rows, lanes])
            centered = mixed - jnp.mean(mixed, axis=-1, keepdims=True)
            spread = jnp.mean(centered * centered, axis=-1, keepdims=True)
            inv = lax.rsqrt(spread + EPS_NORM)
            norm = centered * inv
            wide[0, rows, lanes] = norm
            wide[1, rows, lanes] = jnp.broadcast_to(inv, norm.shape)
            done = (norm * projected[0, rows, lanes].astype(F32)).astype(BF)
            gated[rows, lanes] = done
            turned[width + h * DH : width + (h + 1) * DH, rows] = done.T
    for j in range(mp):
        for side in range(2):
            start = side * half_rows + jnp.bitwise_xor(here_mp, j) * quarter
            start = pl.multiple_of(start, quarter)
            gated_out[j][side * quarter : (side + 1) * quarter, :] = gated[pl.ds(start, quarter), :]


def out_kernel(own, *refs, mp):
    gathered, weights = refs[:mp], refs[mp : 2 * mp]
    unit, unit_bf, inv_o = refs[2 * mp :]
    total = own[...].astype(F32)
    for j in range(mp):
        total = total + dot_nn(gathered[j][...], weights[j][...])
    inv = lax.rsqrt(jnp.sum(total * total, axis=-1, keepdims=True) + EPS_UNIT)
    u = total * inv
    unit[...] = u
    unit_bf[...] = u.astype(BF)
    inv_o[...] = jnp.broadcast_to(inv, inv_o.shape)


def look_kernel(meta, *refs, mp, dp, capacity, chunk, share):
    blocks, catalogue, looked, incoming, returning, digits, asked = refs[:mp], *refs[mp:]
    stock, _ = catalogue.shape
    base = blocks[0].shape[0] - 16 * dp
    for j in range(mp):
        digits[...] = blocks[j][base:, :].astype(F32)
        for d in range(dp):
            high = digits[pl.ds(d * 16 + meta[1], 1), :]
            low = digits[pl.ds(d * 16 + 8 + meta[1], 1), :]
            asked[j * dp + d : j * dp + d + 1, :] = (256.0 * high + low)[:, :capacity]
    groups = dp * mp
    slots = groups * capacity
    half = dp // 2
    table = asked[...]
    slot = iota((1, slots), 1).astype(F32)
    group = jnp.floor((slot + 0.5) * (1.0 / capacity))
    local = slot - group * capacity
    column = (iota((capacity, slots), 0).astype(F32) == local).astype(F32)
    spread = lax.dot_general(
        table,
        column,
        (((1,), (0,)), ((), ())),
        precision=lax.Precision.HIGHEST,
        preferred_element_type=F32,
    )
    line = iota((groups, 1), 0)
    offset = lax.div(line, dp)
    index = line - offset * dp
    side = (index >= half) != (meta[0] >= half)
    near = jnp.where(index >= half, index - half, index)
    first = (near * mp + jnp.bitwise_xor(offset, meta[1])) * 2 + side.astype(I32)
    here = jnp.where(meta[0] >= half, meta[0] - half, meta[0])
    second = (offset * half + jnp.bitwise_xor(near, here)) * 2 + side.astype(I32)
    rows = [
        jnp.sum(jnp.where(group == g.astype(F32), spread, 0.0), axis=0, keepdims=True).astype(I32)
        for g in (first, second)
    ]
    incoming[...] = rows[0]
    returning[...] = rows[1] if share else rows[0]
    for s in range(0, slots, chunk):
        hot = jnp.where(iota((stock, chunk), 0) == incoming[:, s : s + chunk], 1.0, 0.0).astype(BF)
        looked[s : s + chunk, :] = dot_tn(hot, catalogue[...]).astype(BF)


def score_kernel(
    meta, items, code, code_far, units, expo, inv_o, total_o,
    *, dp, devices, capacity, chunk,
):
    events = units.shape[0] // 2
    near = devices // 2
    slots = items.shape[0]
    half = pl.multiple_of(lax.div(meta[0], dp // 2) * near, near)
    codes_in = [c[pl.ds(half, near), :].astype(BF) for c in (code, code_far)]
    for s in range(0, slots, chunk):
        rows = slice(s, s + chunk)
        x = items[rows, :]
        xf = x.astype(F32)
        inv = lax.rsqrt(jnp.sum(xf * xf, axis=-1, keepdims=True) + EPS_UNIT)
        inv_o[rows, :] = jnp.broadcast_to(inv, (chunk, BLOCK))
        cosines = dot_nt(x, units[...]) * (inv * (1.0 / COSINE_DIVISOR))
        slot = s + iota((chunk, 1), 0).astype(F32)
        owner = jnp.floor((slot + 0.5) * (1.0 / (2 * capacity)))
        local = slot - owner * (2 * capacity)
        far = local >= capacity
        local = jnp.where(far, local - capacity, local)
        named = owner == iota((chunk, near), 1).astype(F32)
        for side in range(2):
            lanes = slice(side * events, (side + 1) * events)
            logits = cosines[:, lanes]
            spread = jnp.where(named & (far == (side == 1)), 1.0, 0.0).astype(BF)
            codes = dot_nn(spread, codes_in[side])
            first = codes == 2.0 * local + 2.0
            other = codes == 2.0 * local + 1.0
            e = jnp.exp(logits)
            total_o[:, lanes] = (
                jnp.sum(jnp.where(first | other, e, 0.0), axis=0, keepdims=True)
                + (total_o[:, lanes] if s else 0.0)
            )
            expo[rows, lanes] = jnp.where(first, -e, jnp.where(other, e, 0.0))


def shares(meta, expo, total, total_far, dp, seqs, seq_dev, steps):
    events = total.shape[1] // 2
    position = meta[1] * events + iota((1, events), 1)
    valid = []
    for base in (meta[0], jnp.bitwise_xor(meta[0], dp // 2)):
        v = jnp.zeros((1, events), F32)
        for k in range(seq_dev):
            step = position - k * steps
            v = jnp.where((step >= 0) & (step < length_of(meta, base * seq_dev + k, seqs)), 1.0, v)
        valid.append(v)
    valid = jnp.concatenate(valid, axis=1) * (1.0 / COSINE_DIVISOR)
    full = total[...] + jnp.concatenate([total_far[:, events:], total_far[:, :events]], axis=1)
    factor = valid / full
    return lambda rows: jnp.abs(expo[rows, :]) * factor - jnp.where(expo[rows, :] < 0.0, valid, 0.0)


def slope_kernel(
    meta, items, code, code_far, expo, inv, total, total_far, slopes, slopes_bf, ledger,
    *, dp, seqs, seq_dev, steps, chunk,
):
    share = shares(meta, expo, total, total_far, dp, seqs, seq_dev, steps)
    events, width = slopes.shape[0] // 2, slopes.shape[1]
    both = jnp.zeros((2 * events, width), F32)
    for s in range(0, items.shape[0], chunk):
        rows = slice(s, s + chunk)
        both = both + dot_tn((share(rows) * inv[rows, 0:1]).astype(BF), items[rows, :])
    slopes[...] = both
    slopes_bf[...] = both.astype(BF)
    near = ledger.shape[0]
    each = items.shape[0] // near
    weight = jnp.concatenate(
        [
            jnp.sum(share(slice(o * each, (o + 1) * each)), axis=0, keepdims=True)
            for o in range(near)
        ],
        axis=0,
    )
    high = weight.astype(BF)
    low = (weight - high.astype(F32)).astype(BF)
    half = pl.multiple_of(lax.div(meta[0], dp // 2) * near, near)
    codes = [c[pl.ds(half, near), :].astype(BF) for c in (code, code_far)]
    for n, part in enumerate([high, low, jnp.concatenate(codes, axis=1)]):
        ledger[:, n * 2 * events : (n + 1) * 2 * events] = part


def send_kernel(
    meta, expo, total, total_far, units, sending,
    *, dp, seqs, seq_dev, steps, chunk,
):
    share = shares(meta, expo, total, total_far, dp, seqs, seq_dev, steps)
    for s in range(0, expo.shape[0], chunk):
        rows = slice(s, s + chunk)
        hot = jnp.where(expo[rows, :] == 0.0, 0.0, 1.0).astype(BF)
        unit_rows = dot_nn(hot, units[...])
        weight = jnp.sum(share(rows), axis=1, keepdims=True)
        sending[rows, :] = (unit_rows * weight).astype(BF)


def mail_kernel(meta, *refs, half, mp, events, capacity):
    units, ledgers, outs = refs[:half], refs[half : 2 * half], refs[2 * half : -2]
    hots, ledger = refs[-2:]
    here = jnp.where(meta[0] >= half, meta[0] - half, meta[0])
    slot = iota((2 * capacity, 2 * events), 0)
    event = iota((2 * capacity, 2 * events), 1)
    far = slot >= capacity
    local = jnp.where(far, slot - capacity, slot).astype(F32)
    same = far == (event >= events)
    for j in range(half):
        ledger[...] = ledgers[j][...].astype(F32)
        weights = []
        for k in range(mp):
            line = ledger[pl.ds(here * mp + jnp.bitwise_xor(meta[1], k), 1), :]
            code = line[:, 4 * events : 6 * events]
            mine = same & (jnp.floor((code - 1.0) * 0.5) == local)
            hots[k * 2 * capacity : (k + 1) * 2 * capacity, :] = mine.astype(BF)
            weight = line[:, : 2 * events] + line[:, 2 * events : 4 * events]
            weights.append(jnp.sum(jnp.where(mine, weight, 0.0), axis=1, keepdims=True))
        rows = dot_nn(hots[...], units[j][...])
        for k in range(mp):
            part = rows[k * 2 * capacity : (k + 1) * 2 * capacity] * weights[k]
            outs[k][j * 2 * capacity : (j + 1) * 2 * capacity, :] = part.astype(BF)


def out_cot_kernel(units, inv_out, slopes, slopes_back, out_cot):
    events = units.shape[0] // 2
    for side in range(2):
        rows = slice(side * events, (side + 1) * events)
        there = slice((1 - side) * events, (2 - side) * events)
        u = units[rows, :]
        s = slopes[rows, :] + slopes_back[there, :].astype(F32)
        along = jnp.sum(u * s, axis=-1, keepdims=True)
        out_cot[rows, :] = ((s - u * along) * inv_out[rows, 0:1]).astype(BF)


def spread_kernel(incoming, catalogue, *refs, chunk):
    landed, out = refs[:-1], refs[-1]
    stock, _ = catalogue.shape
    slots = incoming.shape[1]
    for r in range(0, stock, chunk):
        hot = jnp.where(r + iota((chunk, slots), 0) == incoming[...], 1.0, 0.0).astype(BF)
        v, at = 0.0, 0
        for part in landed:
            v = v + dot_nn(hot[:, at : at + part.shape[0]], part[...])
            at += part.shape[0]
        c = catalogue[r : r + chunk, :].astype(F32)
        inv = lax.rsqrt(jnp.sum(c * c, axis=-1, keepdims=True) + EPS_UNIT)
        c = c * inv
        out[r : r + chunk, :] = (v - c * jnp.sum(c * v, axis=-1, keepdims=True)) * inv


def backward_kernel(meta, *refs, mp, dp):
    blocks = refs[:mp]
    w_out, wide, projected, turned = refs[mp : mp + 4]
    outs = refs[mp + 4 : -2]
    whole, cot = refs[-2:]
    half = dp // 2
    quarter, width = blocks[0].shape[0] // 2, blocks[0].shape[1]
    rows_all = whole.shape[0]
    cols = w_out.shape[0]
    for j in range(mp):
        for side in range(2):
            start = side * (rows_all // 2) + jnp.bitwise_xor(meta[1], j) * quarter
            rows = slice(side * quarter, (side + 1) * quarter)
            whole[pl.ds(pl.multiple_of(start, quarter), quarter), :] = blocks[j][rows, :]
    gated_cot = dot_nt(whole[...], w_out[...]).astype(BF).astype(F32)
    for g in range(rows_all // BLOCK):
        rows = slice(g * BLOCK, (g + 1) * BLOCK)
        for h in range(cols // DH):
            lanes = slice(h * DH, (h + 1) * DH)
            d_gated = gated_cot[rows, lanes]
            n = wide[0, rows, lanes]
            d_norm = d_gated * projected[0, rows, lanes].astype(F32)
            d_mixed = wide[1, rows, lanes] * (
                d_norm
                - jnp.mean(d_norm, axis=-1, keepdims=True)
                - n * jnp.mean(d_norm * n, axis=-1, keepdims=True)
            )
            d_mixed = d_mixed.astype(BF)
            d_weights = dot_nt(d_mixed, projected[1, rows, lanes]).astype(BF).astype(F32)
            d_values = dot_tn(projected[4, rows, lanes], d_mixed)
            d_scores = (d_weights * wide[2, rows, lanes]).astype(BF)
            d_queries = dot_nn(d_scores, projected[3, rows, lanes])
            d_keys = dot_tn(d_scores, projected[2, rows, lanes])
            for c, d in enumerate((d_gated * n, d_values, d_queries, d_keys)):
                step = projected[5 + c, rows, lanes].astype(F32)
                cot[c, rows, lanes] = (d.astype(BF).astype(F32) * step).astype(BF)
    share = width // dp
    mine = pl.multiple_of(lax.div(meta[0], half) * (width // 2), width // 2)
    here = jnp.where(meta[0] >= half, meta[0] - half, meta[0])
    normed = turned[pl.ds(mine, width // 2), :]
    for c in range(5):
        if c < 4:
            part = dot_nn(normed, cot[c]).astype(BF)
        else:
            lanes = pl.ds(mine, width // 2)
            part = dot_nn(turned[width:, :], whole[:, lanes]).T.astype(BF)
        for d in range(half):
            piece = part[d * share : (d + 1) * share, :]
            if len(outs) == 1:
                outs[0][d, c] = piece
                continue
            for j in range(half):

                @pl.when(jnp.bitwise_xor(here, j) == d)
                def _(j=j, piece=piece):
                    outs[j][c] = piece


def swapped(x, axis, bit):
    size = lax.axis_size(axis)
    return lax.ppermute(x, axis, [(a, a ^ bit) for a in range(size)])


def gather_blocks(x, axis, half=None):
    size = lax.axis_size(axis)
    blocks = {0: x} if half is None else {0: x, size // 2: half}
    bit = size // 2 if half is None else size // 4
    while bit:
        for j in list(blocks):
            blocks[j ^ bit] = swapped(blocks[j], axis, bit)
        bit //= 2
    return [blocks[j] for j in range(size)]


def exchange(parts, axis):
    return [p if j == 0 else swapped(p, axis, j) for j, p in enumerate(parts)]


def per_device(history, lengths, source, owners, item_rows, catalogue, w_in, w_out):
    dp = lax.axis_size("dp")
    mp = lax.axis_size("mp")
    devices = dp * mp
    near = devices // 2
    seq_dev, steps, part = history.shape
    width = part * mp
    cols = w_in.shape[2]
    rows_all = seq_dev * steps
    quarter = rows_all // mp
    events, top = owners.shape
    asks = events * top
    capacity = max(2, (3 * asks + 2 * devices - 1) // (2 * devices))
    slots = devices * capacity
    stock = catalogue.shape[0]
    per_peer = (seq_dev + dp - 1) // dp
    chunk = math.gcd(slots, 512)
    short = dp <= 8 and near <= 16 and 6 * events <= width
    S = jax.ShapeDtypeStruct
    here_dp = lax.axis_index("dp")
    place = jnp.stack([here_dp, lax.axis_index("mp")]).astype(I32)
    meta = jnp.concatenate([place, source, lengths])
    seqs = source.shape[0]
    halves = [list(range(near)), list(range(near, devices))]

    def partner(x):
        return swapped(x, "dp", dp // 2)

    def in_half(x):
        return lax.all_to_all(
            x.reshape(near, 2 * capacity, width),
            ("dp", "mp"),
            split_axis=0,
            concat_axis=0,
            tiled=True,
            axis_index_groups=halves,
        ).reshape(slots, width)

    w_out_y = swapped(w_out, "mp", mp // 2)
    packed, code = call(
        functools.partial(
            pack_kernel, dp=dp, seq_dev=seq_dev, per_peer=per_peer, mp=mp, capacity=capacity
        ),
        [S((dp, 2 * per_peer * steps + 16, part), BF), S((devices, events), F32)],
        [SM, VM, VM, VM],
        4,
    )(meta, history, owners.T, item_rows.T)
    arrived = lax.all_to_all(packed, "dp", split_axis=0, concat_axis=0, tiled=True)
    arrived, w_out_y = lax.optimization_barrier((arrived, w_out_y))
    rows = call(
        functools.partial(take_kernel, dp=dp, seq_dev=seq_dev, per_peer=per_peer, steps=steps),
        S((2 * rows_all + 16 * dp, part), BF),
        [SM, VM],
        1,
    )(meta, arrived)
    features = gather_blocks(rows, "mp")
    code_far = partner(code)
    looked, incoming, returning = call(
        functools.partial(
            look_kernel, mp=mp, dp=dp, capacity=capacity, chunk=chunk, share=short
        ),
        [S((slots, width), BF), S((1, slots), I32), S((1, slots), I32)],
        [SM] + [VM] * mp + [HB],
        4,
        scratch=[pltpu.VMEM((16 * dp, part), F32), pltpu.VMEM((devices, capacity), F32)],
    )(meta, *features, catalogue)
    looked, features, code_far = lax.optimization_barrier((looked, features, code_far))
    items = in_half(looked)

    wide, projected, turned, own, *gated = call(
        functools.partial(
            forward_kernel,
            mp=mp,
            dp=dp,
            seqs=seqs,
            seq_dev=seq_dev,
            steps=steps,
            width=width,
            cols=cols,
            quarter=quarter,
        ),
        [
            S((3, 2 * rows_all, cols), F32),
            S((9, 2 * rows_all, cols), BF),
            S((width + cols, 2 * rows_all), BF),
            S((2 * quarter, width), BF),
        ]
        + [S((2 * quarter, cols), BF)] * mp,
        [SM] + [VM] * mp + [HB],
        10,
        scratch=[pltpu.VMEM((2 * rows_all, width), BF), pltpu.VMEM((2 * rows_all, cols), BF)],
        out_specs=[HB] * 4 + [VM] * mp,
        limit=36,
    )(meta, *features, w_in)
    gathered = exchange(gated, "mp")
    w_out_blocks = gather_blocks(w_out, "mp", w_out_y)
    units, units_bf, inv_out = call(
        functools.partial(out_kernel, mp=mp),
        [
            S((2 * quarter, width), F32),
            S((2 * quarter, width), BF),
            S((2 * quarter, BLOCK), F32),
        ],
        [HB] + [VM] * (2 * mp),
        2,
    )(own, *gathered, *w_out_blocks)

    expo, inv_item, total = call(
        functools.partial(
            score_kernel, dp=dp, devices=devices, capacity=capacity, chunk=chunk
        ),
        [S((slots, 2 * events), F32), S((slots, BLOCK), F32), S((1, 2 * events), F32)],
        [SM, HB] + [VM] * 3,
        4,
    )(meta, items, code, code_far, units_bf)
    total_far = partner(total)
    sizes = dict(dp=dp, seqs=seqs, seq_dev=seq_dev, steps=steps, chunk=chunk)
    slopes, slopes_bf, ledger = call(
        functools.partial(slope_kernel, **sizes),
        [
            S((2 * events, width), F32),
            S((2 * events, width), BF),
            S((near, width), BF),
        ],
        [SM, HB] + [VM] * 6,
        3,
    )(meta, items, code, code_far, expo, inv_item, total, total_far)
    slopes_back = partner(slopes_bf)
    if short:
        column = range(1, dp // 2)
        ledgers = [ledger] + [swapped(ledger, "dp", j) for j in column]
        all_units = [units_bf] + [swapped(units_bf, "dp", j) for j in column]
        mail = call(
            functools.partial(
                mail_kernel, half=dp // 2, mp=mp, events=events, capacity=capacity
            ),
            [S((dp * capacity, width), BF)] * mp,
            [SM] + [VM] * dp,
            4,
            scratch=[
                pltpu.VMEM((mp * 2 * capacity, 2 * events), BF),
                pltpu.VMEM((near, width), F32),
            ],
        )(meta, *all_units, *ledgers)
        slopes_back, mail = lax.optimization_barrier((slopes_back, mail))
        landed = exchange(mail, "mp")
    out_cot = call(out_cot_kernel, S((2 * events, width), BF), [VM] * 4, 1)(
        units, inv_out, slopes, slopes_back
    )
    cots = gather_blocks(out_cot, "mp")
    pieces = [S((5, width // dp, cols), BF)] * (dp // 2)
    parts = call(
        functools.partial(backward_kernel, mp=mp, dp=dp),
        pieces if short else [S((dp // 2, 5, width // dp, cols), BF)],
        [SM] + [VM] * mp + [HB] * 4,
        10,
        scratch=[
            pltpu.VMEM((2 * rows_all, width), BF),
            pltpu.VMEM((4, 2 * rows_all, cols), BF),
        ],
        limit=36,
    )(meta, *cots, w_out, wide, projected, turned)
    if short:
        parts, landed = lax.optimization_barrier((parts, landed))
        grads = sum(p.astype(F32) for p in exchange(parts, "dp"))
    else:
        got = lax.all_to_all(
            parts[0],
            "dp",
            split_axis=0,
            concat_axis=0,
            tiled=True,
            axis_index_groups=[list(range(dp // 2)), list(range(dp // 2, dp))],
        )
        grads = jnp.sum(got.astype(F32), axis=0)
        sending = call(
            functools.partial(send_kernel, **sizes),
            S((slots, width), BF),
            [SM] + [VM] * 4,
            3,
        )(meta, expo, total, total_far, units_bf)
        landed = [in_half(sending)]
    cat_grad = call(
        functools.partial(spread_kernel, chunk=math.gcd(stock, 128)),
        S((stock, width), F32),
        [VM, HB] + [HB] * len(landed),
        4,
        out_specs=[HB],
        limit=24,
    )(returning, catalogue, *landed)
    return (grads[:4], grads[4].T, cat_grad)


def solution(mesh):
    placed = (
        P("dp", None, "mp"),
        P(),
        P(),
        P(("dp", "mp"), None),
        P(("dp", "mp"), None),
        P(("dp", "mp"), None),
        P(None, None, "mp"),
        P("mp", None),
    )
    return jax.shard_map(
        per_device,
        mesh=mesh,
        in_specs=placed,
        out_specs=(P(None, "dp", "mp"), P("mp", "dp"), P(("dp", "mp"), None)),
        check_vma=False,
    )
```

```python
import functools
import math

import jax
import jax.numpy as jnp
from jax import lax
from jax.experimental import pallas as pl
from jax.experimental.pallas import tpu as pltpu
from jax.sharding import PartitionSpec as P

DH = 128
COSINE_DIVISOR = 0.05
EPS_NORM = 1e-05
EPS_UNIT = 1e-06
BF = jnp.bfloat16
F32 = jnp.float32
I32 = jnp.int32
BLOCK = 128

VM = pl.BlockSpec(memory_space=pltpu.VMEM)
SM = pl.BlockSpec(memory_space=pltpu.SMEM)
HB = pl.BlockSpec(memory_space=pltpu.HBM)


def call(body, out_shape, in_specs, us, scratch=(), limit=16, out_specs=None, lazy=False):
    many = isinstance(out_shape, (list, tuple))
    outs = list(out_shape) if many else [out_shape]
    out_specs = list(out_specs or [VM] * len(outs))

    def run(*args):
        args = list(args)
        far_in = [n for n, spec in enumerate(in_specs) if spec is HB]
        far_out = [n for n, spec in enumerate(out_specs) if spec is HB]
        n_in, n_out, n_own = len(in_specs), len(outs), len(scratch)
        extra = [pltpu.VMEM(args[n].shape, args[n].dtype) for n in far_in]
        extra += [pltpu.VMEM(outs[n].shape, outs[n].dtype) for n in far_out]
        moved = len(far_in) + len(far_out)

        def kernel(*refs):
            ins, res = list(refs[:n_in]), list(refs[n_in : n_in + n_out])
            own = refs[n_in + n_out : n_in + n_out + n_own]
            held = refs[n_in + n_out + n_own :]
            sems = held[-1] if moved else None
            copies = []
            for m, n in enumerate(far_in):
                copies.append(pltpu.make_async_copy(ins[n], held[m], sems.at[m]))
                ins[n] = held[m]
            for c in copies:
                c.start()
            arriving = dict(zip(far_in, copies))

            def ready(*places):
                for n in places:
                    arriving.pop(n).wait()

            more = {"ready": ready} if lazy else {}
            if not lazy:
                ready(*far_in)
            copies = []
            for m, n in enumerate(far_out):
                m += len(far_in)
                copies.append(pltpu.make_async_copy(held[m], res[n], sems.at[m]))
                res[n] = held[m]
            body(*ins, *res, *own, **more)
            for c in copies:
                c.start()
            for c in copies:
                c.wait()

        result = pl.pallas_call(
            kernel,
            out_shape=outs,
            in_specs=list(in_specs),
            out_specs=out_specs,
            scratch_shapes=list(scratch)
            + extra
            + ([pltpu.SemaphoreType.DMA((moved,))] if moved else []),
            compiler_params=pltpu.CompilerParams(vmem_limit_bytes=limit * 2**20),
            cost_estimate=pl.CostEstimate(
                flops=0, bytes_accessed=int(us * 3.3e6), transcendentals=0
            ),
        )(*args)
        return result if many else result[0]

    return run


def dot_nt(a, b):
    return lax.dot_general(a, b, (((1,), (1,)), ((), ())), preferred_element_type=F32)


def dot_tn(a, b):
    return lax.dot_general(a, b, (((0,), (0,)), ((), ())), preferred_element_type=F32)


def dot_nn(a, b):
    return jnp.dot(a, b, preferred_element_type=F32)


def iota(shape, dim):
    return lax.broadcasted_iota(I32, shape, dim)


def length_of(meta, slot, seqs):
    return meta[2 + seqs + meta[2 + slot]]


def pack_kernel(meta, hist, owners_t, rows_t, out, code, *, dp, seq_dev, per_peer, mp, capacity):
    here = meta[0]
    steps, part = hist.shape[1], hist.shape[2]

    def per_dest(d, carry):
        def per_slot(i, count):
            src = meta[2 + d * seq_dev + i]
            hit = lax.div(src, seq_dev) == here

            @pl.when(hit)
            def _():
                value = hist[src - here * seq_dev]
                for side in range(2):
                    start = pl.multiple_of((side * per_peer + count) * steps, steps)
                    out[jnp.bitwise_xor(d, side * (dp // 2)), pl.ds(start, steps), :] = value

            return count + hit.astype(I32)

        lax.fori_loop(0, seq_dev, per_slot, jnp.int32(0))
        return carry

    lax.fori_loop(0, dp, per_dest, jnp.int32(0))
    top, events = owners_t.shape
    devices = dp * mp
    o_id = iota((devices, events), 0)
    named = jnp.zeros((devices, events), F32)
    row = jnp.zeros((devices, events), F32)
    positive = jnp.zeros((devices, events), F32)
    for j in range(top):
        same = jnp.where(owners_t[j : j + 1, :] == o_id, 1.0, 0.0)
        named = named + same
        row = row + same * rows_t[j : j + 1, :].astype(F32)
        if j == 0:
            positive = same
    before = (iota((events, events), 0) < iota((events, events), 1)).astype(BF)
    rank = dot_nn(named.astype(BF), before)
    code[...] = jnp.where(named > 0.0, 2.0 * rank + 1.0 + positive, 0.0)
    rank = jnp.where(named > 0.0, rank, -1.0)
    lane = iota((devices, part), 1)
    wanted = jnp.zeros((devices, part), F32)
    for c in range(capacity):
        one = jnp.sum(jnp.where(rank == float(c), row, 0.0), axis=1, keepdims=True)
        wanted = jnp.where(lane == c, one, wanted)
    high = jnp.floor(wanted * (1.0 / 256.0))
    low = wanted - 256.0 * high
    none = jnp.zeros((8 - mp, part), F32)
    for d in range(dp):
        mine = slice(d * mp, (d + 1) * mp)
        digits = [high[mine], none, low[mine], none] if mp < 8 else [high[mine], low[mine]]
        out[d, 2 * per_peer * steps :, :] = jnp.concatenate(digits, axis=0).astype(BF)


def take_kernel(meta, arrived, out, digits, *, dp, seq_dev, per_peer, steps):
    for side in range(2):
        block = jnp.bitwise_xor(meta[0], side * (dp // 2))
        anchors = [lax.div(meta[2 + block * seq_dev + k], seq_dev) for k in range(seq_dev)]
        for k in range(seq_dev):
            rank = jnp.int32(side * per_peer)
            for earlier in range(k):
                rank = rank + (anchors[earlier] == anchors[k]).astype(I32)
            start = pl.multiple_of(rank * steps, steps)
            at = (side * seq_dev + k) * steps
            out[at : at + steps, :] = arrived[anchors[k], pl.ds(start, steps), :]
    for d in range(dp):
        digits[d * 16 : (d + 1) * 16, :] = arrived[d, 2 * per_peer * steps :, :]


def forward_kernel(meta, *refs, mp, dp, seqs, seq_dev, steps, width, cols, quarter):
    blocks = refs[:mp]
    w_in = refs[mp]
    wide, projected, turned, own = refs[mp + 1 : mp + 5]
    gated_out = refs[mp + 5 : 2 * mp + 5]
    feat, gated = refs[2 * mp + 5 :]
    here_mp = meta[1]
    part = width // mp
    counts = [
        length_of(meta, block * seq_dev + k, seqs)
        for block in (meta[0], jnp.bitwise_xor(meta[0], dp // 2))
        for k in range(seq_dev)
    ]
    half_rows = seq_dev * steps
    rows_all = 2 * half_rows
    for j in range(mp):
        start = pl.multiple_of(jnp.bitwise_xor(here_mp, j) * part, part)
        feat[:, pl.ds(start, part)] = blocks[j][...]
    for side in range(2):
        start = pl.multiple_of(side * half_rows + here_mp * quarter, quarter)
        own[side * quarter : (side + 1) * quarter, :] = feat[pl.ds(start, quarter), :]
    for g in range(rows_all // BLOCK):
        rows = slice(g * BLOCK, (g + 1) * BLOCK)
        x = feat[rows, :].astype(F32)
        centered = x - jnp.mean(x, axis=-1, keepdims=True)
        spread = jnp.mean(centered * centered, axis=-1, keepdims=True)
        y = (centered * lax.rsqrt(spread + EPS_NORM)).astype(BF)
        feat[rows, :] = y
        turned[:width, rows] = y.T
    for c in range(4):
        pre = dot_nn(feat[...], w_in[c])
        sigma = jax.nn.sigmoid(pre)
        projected[c] = (pre * sigma).astype(BF)
        projected[5 + c] = (sigma * (1.0 + pre * (1.0 - sigma))).astype(BF)
    root = 1.0 / math.sqrt(DH)
    t_id = iota((BLOCK, BLOCK), 0)
    s_id = iota((BLOCK, BLOCK), 1)
    per_block = BLOCK // steps
    causal = (t_id // steps == s_id // steps) & (s_id <= t_id)
    for g in range(rows_all // BLOCK):
        rows = slice(g * BLOCK, (g + 1) * BLOCK)
        count = jnp.zeros((BLOCK, BLOCK), I32)
        for i in range(per_block):
            count = jnp.where(t_id // steps == i, counts[g * per_block + i], count)
        allowed = causal & (s_id % steps < count)
        scale = jnp.where(allowed, 1.0 / count.astype(F32), 0.0)
        for h in range(cols // DH):
            lanes = slice(h * DH, (h + 1) * DH)
            scores = dot_nt(projected[2, rows, lanes], projected[3, rows, lanes]) * root
            sigma = jax.nn.sigmoid(scores)
            weights = (scores * sigma * scale).astype(BF)
            projected[4, rows, lanes] = weights
            wide[2, rows, lanes] = sigma * (1.0 + scores * (1.0 - sigma)) * (scale * root)
            mixed = dot_nn(weights, projected[1, rows, lanes])
            centered = mixed - jnp.mean(mixed, axis=-1, keepdims=True)
            spread = jnp.mean(centered * centered, axis=-1, keepdims=True)
            inv = lax.rsqrt(spread + EPS_NORM)
            norm = centered * inv
            wide[0, rows, lanes] = norm
            wide[1, rows, lanes] = jnp.broadcast_to(inv, norm.shape)
            done = (norm * projected[0, rows, lanes].astype(F32)).astype(BF)
            gated[rows, lanes] = done
            turned[width + h * DH : width + (h + 1) * DH, rows] = done.T
    for j in range(mp):
        for side in range(2):
            start = side * half_rows + jnp.bitwise_xor(here_mp, j) * quarter
            start = pl.multiple_of(start, quarter)
            gated_out[j][side * quarter : (side + 1) * quarter, :] = gated[pl.ds(start, quarter), :]


def out_kernel(own, *refs, mp):
    gathered, weights = refs[:mp], refs[mp : 2 * mp]
    unit, unit_bf, inv_o = refs[2 * mp :]
    total = own[...].astype(F32)
    for j in range(mp):
        total = total + dot_nn(gathered[j][...], weights[j][...])
    inv = lax.rsqrt(jnp.sum(total * total, axis=-1, keepdims=True) + EPS_UNIT)
    u = total * inv
    unit[...] = u
    unit_bf[...] = u.astype(BF)
    inv_o[...] = jnp.broadcast_to(inv, inv_o.shape)


def look_kernel(meta, *refs, mp, dp, capacity, chunk, share):
    blocks, catalogue, looked, incoming, returning, digits, asked = refs[:mp], *refs[mp:]
    stock, _ = catalogue.shape
    for j in range(mp):
        digits[...] = blocks[j][...].astype(F32)
        for d in range(dp):
            high = digits[pl.ds(d * 16 + meta[1], 1), :]
            low = digits[pl.ds(d * 16 + 8 + meta[1], 1), :]
            asked[j * dp + d : j * dp + d + 1, :] = (256.0 * high + low)[:, :capacity]
    groups = dp * mp
    slots = groups * capacity
    half = dp // 2
    table = asked[...]
    slot = iota((1, slots), 1).astype(F32)
    group = jnp.floor((slot + 0.5) * (1.0 / capacity))
    local = slot - group * capacity
    column = (iota((capacity, slots), 0).astype(F32) == local).astype(F32)
    spread = lax.dot_general(
        table,
        column,
        (((1,), (0,)), ((), ())),
        precision=lax.Precision.HIGHEST,
        preferred_element_type=F32,
    )
    line = iota((groups, 1), 0)
    offset = lax.div(line, dp)
    index = line - offset * dp
    side = (index >= half) != (meta[0] >= half)
    near = jnp.where(index >= half, index - half, index)
    first = (near * mp + jnp.bitwise_xor(offset, meta[1])) * 2 + side.astype(I32)
    here = jnp.where(meta[0] >= half, meta[0] - half, meta[0])
    second = (offset * half + jnp.bitwise_xor(near, here)) * 2 + side.astype(I32)
    rows = [
        jnp.sum(jnp.where(group == g.astype(F32), spread, 0.0), axis=0, keepdims=True).astype(I32)
        for g in (first, second)
    ]
    incoming[...] = rows[0]
    returning[...] = rows[1] if share else rows[0]
    for s in range(0, slots, chunk):
        hot = jnp.where(iota((stock, chunk), 0) == incoming[:, s : s + chunk], 1.0, 0.0).astype(BF)
        looked[s : s + chunk, :] = dot_tn(hot, catalogue[...]).astype(BF)


def score_kernel(
    meta, items, code, code_far, units, expo, inv_o, total_o,
    *, dp, devices, capacity, chunk,
):
    events = units.shape[0] // 2
    near = devices // 2
    slots = items.shape[0]
    half = pl.multiple_of(lax.div(meta[0], dp // 2) * near, near)
    codes_in = [c[pl.ds(half, near), :].astype(BF) for c in (code, code_far)]
    for s in range(0, slots, chunk):
        rows = slice(s, s + chunk)
        x = items[rows, :]
        xf = x.astype(F32)
        inv = lax.rsqrt(jnp.sum(xf * xf, axis=-1, keepdims=True) + EPS_UNIT)
        inv_o[rows, :] = jnp.broadcast_to(inv, (chunk, BLOCK))
        cosines = dot_nt(x, units[...]) * (inv * (1.0 / COSINE_DIVISOR))
        slot = s + iota((chunk, 1), 0).astype(F32)
        owner = jnp.floor((slot + 0.5) * (1.0 / (2 * capacity)))
        local = slot - owner * (2 * capacity)
        far = local >= capacity
        local = jnp.where(far, local - capacity, local)
        named = owner == iota((chunk, near), 1).astype(F32)
        for side in range(2):
            lanes = slice(side * events, (side + 1) * events)
            logits = cosines[:, lanes]
            spread = jnp.where(named & (far == (side == 1)), 1.0, 0.0).astype(BF)
            codes = dot_nn(spread, codes_in[side])
            first = codes == 2.0 * local + 2.0
            other = codes == 2.0 * local + 1.0
            e = jnp.exp(logits)
            total_o[:, lanes] = (
                jnp.sum(jnp.where(first | other, e, 0.0), axis=0, keepdims=True)
                + (total_o[:, lanes] if s else 0.0)
            )
            expo[rows, lanes] = jnp.where(first, -e, jnp.where(other, e, 0.0))


def shares(meta, expo, total, total_far, dp, seqs, seq_dev, steps):
    events = total.shape[1] // 2
    position = meta[1] * events + iota((1, events), 1)
    valid = []
    for base in (meta[0], jnp.bitwise_xor(meta[0], dp // 2)):
        v = jnp.zeros((1, events), F32)
        for k in range(seq_dev):
            step = position - k * steps
            v = jnp.where((step >= 0) & (step < length_of(meta, base * seq_dev + k, seqs)), 1.0, v)
        valid.append(v)
    valid = jnp.concatenate(valid, axis=1) * (1.0 / COSINE_DIVISOR)
    full = total[...] + jnp.concatenate([total_far[:, events:], total_far[:, :events]], axis=1)
    factor = valid / full
    return lambda rows: jnp.abs(expo[rows, :]) * factor - jnp.where(expo[rows, :] < 0.0, valid, 0.0)


def slope_kernel(
    meta, items, code, code_far, expo, inv, total, total_far, slopes, slopes_bf, ledger,
    *, dp, seqs, seq_dev, steps, chunk,
):
    share = shares(meta, expo, total, total_far, dp, seqs, seq_dev, steps)
    events, width = slopes.shape[0] // 2, slopes.shape[1]
    both = jnp.zeros((2 * events, width), F32)
    for s in range(0, items.shape[0], chunk):
        rows = slice(s, s + chunk)
        both = both + dot_tn((share(rows) * inv[rows, 0:1]).astype(BF), items[rows, :])
    slopes[...] = both
    slopes_bf[...] = both.astype(BF)
    near = ledger.shape[0]
    each = items.shape[0] // near
    weight = jnp.concatenate(
        [
            jnp.sum(share(slice(o * each, (o + 1) * each)), axis=0, keepdims=True)
            for o in range(near)
        ],
        axis=0,
    )
    high = weight.astype(BF)
    low = (weight - high.astype(F32)).astype(BF)
    half = pl.multiple_of(lax.div(meta[0], dp // 2) * near, near)
    codes = [c[pl.ds(half, near), :].astype(BF) for c in (code, code_far)]
    for n, part in enumerate([high, low, jnp.concatenate(codes, axis=1)]):
        ledger[:, n * 2 * events : (n + 1) * 2 * events] = part


def send_kernel(
    meta, expo, total, total_far, units, sending,
    *, dp, seqs, seq_dev, steps, chunk,
):
    share = shares(meta, expo, total, total_far, dp, seqs, seq_dev, steps)
    for s in range(0, expo.shape[0], chunk):
        rows = slice(s, s + chunk)
        hot = jnp.where(expo[rows, :] == 0.0, 0.0, 1.0).astype(BF)
        unit_rows = dot_nn(hot, units[...])
        weight = jnp.sum(share(rows), axis=1, keepdims=True)
        sending[rows, :] = (unit_rows * weight).astype(BF)


def mail_kernel(meta, *refs, half, mp, events, capacity):
    units, ledgers, outs = refs[:half], refs[half : 2 * half], refs[2 * half : -2]
    hots, ledger = refs[-2:]
    here = jnp.where(meta[0] >= half, meta[0] - half, meta[0])
    slot = iota((2 * capacity, 2 * events), 0)
    event = iota((2 * capacity, 2 * events), 1)
    far = slot >= capacity
    local = jnp.where(far, slot - capacity, slot).astype(F32)
    same = far == (event >= events)
    for j in range(half):
        ledger[...] = ledgers[j][...].astype(F32)
        weights = []
        for k in range(mp):
            line = ledger[pl.ds(here * mp + jnp.bitwise_xor(meta[1], k), 1), :]
            code = line[:, 4 * events : 6 * events]
            mine = same & (jnp.floor((code - 1.0) * 0.5) == local)
            hots[k * 2 * capacity : (k + 1) * 2 * capacity, :] = mine.astype(BF)
            weight = line[:, : 2 * events] + line[:, 2 * events : 4 * events]
            weights.append(jnp.sum(jnp.where(mine, weight, 0.0), axis=1, keepdims=True))
        rows = dot_nn(hots[...], units[j][...])
        for k in range(mp):
            part = rows[k * 2 * capacity : (k + 1) * 2 * capacity] * weights[k]
            outs[k][j * 2 * capacity : (j + 1) * 2 * capacity, :] = part.astype(BF)


def out_cot_kernel(units, inv_out, slopes, slopes_back, out_cot):
    events = units.shape[0] // 2
    for side in range(2):
        rows = slice(side * events, (side + 1) * events)
        there = slice((1 - side) * events, (2 - side) * events)
        u = units[rows, :]
        s = slopes[rows, :] + slopes_back[there, :].astype(F32)
        along = jnp.sum(u * s, axis=-1, keepdims=True)
        out_cot[rows, :] = ((s - u * along) * inv_out[rows, 0:1]).astype(BF)


def spread_kernel(incoming, catalogue, *refs, chunk):
    landed, out = refs[:-1], refs[-1]
    stock, _ = catalogue.shape
    slots = incoming.shape[1]
    for r in range(0, stock, chunk):
        hot = jnp.where(r + iota((chunk, slots), 0) == incoming[...], 1.0, 0.0).astype(BF)
        v, at = 0.0, 0
        for part in landed:
            v = v + dot_nn(hot[:, at : at + part.shape[0]], part[...])
            at += part.shape[0]
        c = catalogue[r : r + chunk, :].astype(F32)
        inv = lax.rsqrt(jnp.sum(c * c, axis=-1, keepdims=True) + EPS_UNIT)
        c = c * inv
        out[r : r + chunk, :] = (v - c * jnp.sum(c * v, axis=-1, keepdims=True)) * inv


def backward_kernel(meta, *refs, mp, dp):
    blocks = refs[:mp]
    w_out, wide, projected, turned = refs[mp : mp + 4]
    outs = refs[mp + 4 : -2]
    whole, cot = refs[-2:]
    half = dp // 2
    quarter, width = blocks[0].shape[0] // 2, blocks[0].shape[1]
    rows_all = whole.shape[0]
    cols = w_out.shape[0]
    for j in range(mp):
        for side in range(2):
            start = side * (rows_all // 2) + jnp.bitwise_xor(meta[1], j) * quarter
            rows = slice(side * quarter, (side + 1) * quarter)
            whole[pl.ds(pl.multiple_of(start, quarter), quarter), :] = blocks[j][rows, :]
    gated_cot = dot_nt(whole[...], w_out[...]).astype(BF).astype(F32)
    for g in range(rows_all // BLOCK):
        rows = slice(g * BLOCK, (g + 1) * BLOCK)
        for h in range(cols // DH):
            lanes = slice(h * DH, (h + 1) * DH)
            d_gated = gated_cot[rows, lanes]
            n = wide[0, rows, lanes]
            d_norm = d_gated * projected[0, rows, lanes].astype(F32)
            d_mixed = wide[1, rows, lanes] * (
                d_norm
                - jnp.mean(d_norm, axis=-1, keepdims=True)
                - n * jnp.mean(d_norm * n, axis=-1, keepdims=True)
            )
            d_mixed = d_mixed.astype(BF)
            d_weights = dot_nt(d_mixed, projected[1, rows, lanes]).astype(BF).astype(F32)
            d_values = dot_tn(projected[4, rows, lanes], d_mixed)
            d_scores = (d_weights * wide[2, rows, lanes]).astype(BF)
            d_queries = dot_nn(d_scores, projected[3, rows, lanes])
            d_keys = dot_tn(d_scores, projected[2, rows, lanes])
            for c, d in enumerate((d_gated * n, d_values, d_queries, d_keys)):
                step = projected[5 + c, rows, lanes].astype(F32)
                cot[c, rows, lanes] = (d.astype(BF).astype(F32) * step).astype(BF)
    share = width // dp
    mine = pl.multiple_of(lax.div(meta[0], half) * (width // 2), width // 2)
    here = jnp.where(meta[0] >= half, meta[0] - half, meta[0])
    normed = turned[pl.ds(mine, width // 2), :]
    for c in range(5):
        if c < 4:
            part = dot_nn(normed, cot[c]).astype(BF)
        else:
            lanes = pl.ds(mine, width // 2)
            part = dot_nn(turned[width:, :], whole[:, lanes]).T.astype(BF)
        for d in range(half):
            piece = part[d * share : (d + 1) * share, :]
            if len(outs) == 1:
                outs[0][d, c] = piece
                continue
            for j in range(half):

                @pl.when(jnp.bitwise_xor(here, j) == d)
                def _(j=j, piece=piece):
                    outs[j][c] = piece


def sum_kernel(*refs):
    parts, w_in_grad, w_out_grad = refs[:-2], *refs[-2:]
    for c in range(5):
        total = sum(p[c].astype(F32) for p in parts)
        if c < 4:
            w_in_grad[c] = total
        else:
            w_out_grad[...] = total.T


def swapped(x, axis, bit):
    size = lax.axis_size(axis)
    return lax.ppermute(x, axis, [(a, a ^ bit) for a in range(size)])


def gather_blocks(x, axis, half=None):
    size = lax.axis_size(axis)
    blocks = {0: x} if half is None else {0: x, size // 2: half}
    bit = size // 2 if half is None else size // 4
    while bit:
        for j in list(blocks):
            blocks[j ^ bit] = swapped(blocks[j], axis, bit)
        bit //= 2
    return [blocks[j] for j in range(size)]


def exchange(parts, axis):
    return [p if j == 0 else swapped(p, axis, j) for j, p in enumerate(parts)]


def per_device(history, lengths, source, owners, item_rows, catalogue, w_in, w_out):
    dp = lax.axis_size("dp")
    mp = lax.axis_size("mp")
    devices = dp * mp
    near = devices // 2
    seq_dev, steps, part = history.shape
    width = part * mp
    cols = w_in.shape[2]
    rows_all = seq_dev * steps
    quarter = rows_all // mp
    events, top = owners.shape
    asks = events * top
    capacity = max(2, (3 * asks + 2 * devices - 1) // (2 * devices))
    slots = devices * capacity
    stock = catalogue.shape[0]
    per_peer = (seq_dev + dp - 1) // dp
    chunk = math.gcd(slots, 512)
    short = dp <= 8 and near <= 16 and 6 * events <= width
    S = jax.ShapeDtypeStruct
    here_dp = lax.axis_index("dp")
    place = jnp.stack([here_dp, lax.axis_index("mp")]).astype(I32)
    meta = jnp.concatenate([place, source, lengths])
    seqs = source.shape[0]
    halves = [list(range(near)), list(range(near, devices))]

    def partner(x):
        return swapped(x, "dp", dp // 2)

    def in_half(x):
        return lax.all_to_all(
            x.reshape(near, 2 * capacity, width),
            ("dp", "mp"),
            split_axis=0,
            concat_axis=0,
            tiled=True,
            axis_index_groups=halves,
        ).reshape(slots, width)

    w_out_y = swapped(w_out, "mp", mp // 2)
    packed, code = call(
        functools.partial(
            pack_kernel, dp=dp, seq_dev=seq_dev, per_peer=per_peer, mp=mp, capacity=capacity
        ),
        [S((dp, 2 * per_peer * steps + 16, part), BF), S((devices, events), F32)],
        [SM, HB, HB, HB],
        4,
        limit=58,
    )(meta, history, owners.T, item_rows.T)
    arrived = lax.all_to_all(packed, "dp", split_axis=0, concat_axis=0, tiled=True)
    arrived, w_out_y = lax.optimization_barrier((arrived, w_out_y))
    rows, digits = call(
        functools.partial(take_kernel, dp=dp, seq_dev=seq_dev, per_peer=per_peer, steps=steps),
        [S((2 * rows_all, part), BF), S((16 * dp, part), BF)],
        [SM, VM],
        1,
    )(meta, arrived)
    digits_y = swapped(digits, "mp", mp // 2)
    rows, digits_y = lax.optimization_barrier((rows, digits_y))
    rows_y = swapped(rows, "mp", mp // 2)
    digits = gather_blocks(digits, "mp", digits_y)
    code_far = partner(code)
    looked, incoming, returning = call(
        functools.partial(
            look_kernel, mp=mp, dp=dp, capacity=capacity, chunk=chunk, share=short
        ),
        [S((slots, width), BF), S((1, slots), I32), S((1, slots), I32)],
        [SM] + [VM] * mp + [VM],
        4,
        scratch=[pltpu.VMEM((16 * dp, part), F32), pltpu.VMEM((devices, capacity), F32)],
    )(meta, *digits, catalogue)
    looked, rows_y, code_far = lax.optimization_barrier((looked, rows_y, code_far))
    features = gather_blocks(rows, "mp", rows_y)
    items = in_half(looked)

    wide, projected, turned, own, *gated = call(
        functools.partial(
            forward_kernel,
            mp=mp,
            dp=dp,
            seqs=seqs,
            seq_dev=seq_dev,
            steps=steps,
            width=width,
            cols=cols,
            quarter=quarter,
        ),
        [
            S((3, 2 * rows_all, cols), F32),
            S((9, 2 * rows_all, cols), BF),
            S((width + cols, 2 * rows_all), BF),
            S((2 * quarter, width), BF),
        ]
        + [S((2 * quarter, cols), BF)] * mp,
        [SM] + [VM] * mp + [VM],
        10,
        scratch=[pltpu.VMEM((2 * rows_all, width), BF), pltpu.VMEM((2 * rows_all, cols), BF)],
        limit=36,
    )(meta, *features, w_in)
    gathered = exchange(gated, "mp")
    w_out_blocks = gather_blocks(w_out, "mp", w_out_y)
    units, units_bf, inv_out = call(
        functools.partial(out_kernel, mp=mp),
        [
            S((2 * quarter, width), F32),
            S((2 * quarter, width), BF),
            S((2 * quarter, BLOCK), F32),
        ],
        [VM] + [VM] * (2 * mp),
        2,
    )(own, *gathered, *w_out_blocks)

    expo, inv_item, total = call(
        functools.partial(
            score_kernel, dp=dp, devices=devices, capacity=capacity, chunk=chunk
        ),
        [S((slots, 2 * events), F32), S((slots, BLOCK), F32), S((1, 2 * events), F32)],
        [SM, VM] + [VM] * 3,
        4,
    )(meta, items, code, code_far, units_bf)
    total_far = partner(total)
    sizes = dict(dp=dp, seqs=seqs, seq_dev=seq_dev, steps=steps, chunk=chunk)
    slopes, slopes_bf, ledger = call(
        functools.partial(slope_kernel, **sizes),
        [
            S((2 * events, width), F32),
            S((2 * events, width), BF),
            S((near, width), BF),
        ],
        [SM, VM] + [VM] * 6,
        3,
    )(meta, items, code, code_far, expo, inv_item, total, total_far)
    slopes_back = partner(slopes_bf)
    if short:
        column = range(1, dp // 2)
        ledgers = [ledger] + [swapped(ledger, "dp", j) for j in column]
        all_units = [units_bf] + [swapped(units_bf, "dp", j) for j in column]
        mail = call(
            functools.partial(
                mail_kernel, half=dp // 2, mp=mp, events=events, capacity=capacity
            ),
            [S((dp * capacity, width), BF)] * mp,
            [SM] + [VM] * dp,
            4,
            scratch=[
                pltpu.VMEM((mp * 2 * capacity, 2 * events), BF),
                pltpu.VMEM((near, width), F32),
            ],
        )(meta, *all_units, *ledgers)
        slopes_back, mail = lax.optimization_barrier((slopes_back, mail))
        landed = exchange(mail, "mp")
    out_cot = call(out_cot_kernel, S((2 * events, width), BF), [VM] * 4, 1)(
        units, inv_out, slopes, slopes_back
    )
    cots = gather_blocks(out_cot, "mp")
    pieces = [S((5, width // dp, cols), BF)] * (dp // 2)
    parts = call(
        functools.partial(backward_kernel, mp=mp, dp=dp),
        pieces if short else [S((dp // 2, 5, width // dp, cols), BF)],
        [SM] + [VM] * (mp + 4),
        10,
        scratch=[
            pltpu.VMEM((2 * rows_all, width), BF),
            pltpu.VMEM((4, 2 * rows_all, cols), BF),
        ],
        limit=36,
    )(meta, *cots, w_out, wide, projected, turned)
    if short:
        parts = exchange(parts, "dp")
        parts, landed = lax.optimization_barrier((parts, landed))
        w_in_grad, w_out_grad = call(
            sum_kernel,
            [S((4, width // dp, cols), F32), S((cols, width // dp), F32)],
            [VM] * len(parts),
            1,
        )(*parts)
    else:
        got = lax.all_to_all(
            parts[0],
            "dp",
            split_axis=0,
            concat_axis=0,
            tiled=True,
            axis_index_groups=[list(range(dp // 2)), list(range(dp // 2, dp))],
        )
        grads = jnp.sum(got.astype(F32), axis=0)
        w_in_grad, w_out_grad = grads[:4], grads[4].T
        sending = call(
            functools.partial(send_kernel, **sizes),
            S((slots, width), BF),
            [SM] + [VM] * 4,
            3,
        )(meta, expo, total, total_far, units_bf)
        landed = [in_half(sending)]
    cat_grad = call(
        functools.partial(spread_kernel, chunk=math.gcd(stock, 128)),
        S((stock, width), F32),
        [VM, VM] + [VM] * len(landed),
        4,
        out_specs=[HB],
        limit=24,
    )(returning, catalogue, *landed)
    return (w_in_grad, w_out_grad, cat_grad)


def solution(mesh):
    placed = (
        P("dp", None, "mp"),
        P(),
        P(),
        P(("dp", "mp"), None),
        P(("dp", "mp"), None),
        P(("dp", "mp"), None),
        P(None, None, "mp"),
        P("mp", None),
    )
    return jax.shard_map(
        per_device,
        mesh=mesh,
        in_specs=placed,
        out_specs=(P(None, "dp", "mp"), P("mp", "dp"), P(("dp", "mp"), None)),
        check_vma=False,
    )
```

```python
import functools
import math

import jax
import jax.numpy as jnp
from jax import lax
from jax.experimental import pallas as pl
from jax.experimental.pallas import tpu as pltpu
from jax.sharding import PartitionSpec as P

DH = 128
COSINE_DIVISOR = 0.05
EPS_NORM = 1e-05
EPS_UNIT = 1e-06
BF = jnp.bfloat16
F32 = jnp.float32
I32 = jnp.int32
BLOCK = 128

VM = pl.BlockSpec(memory_space=pltpu.VMEM)
SM = pl.BlockSpec(memory_space=pltpu.SMEM)
HB = pl.BlockSpec(memory_space=pltpu.HBM)


def call(body, out_shape, in_specs, us, scratch=(), limit=16, out_specs=None, lazy=False):
    many = isinstance(out_shape, (list, tuple))
    outs = list(out_shape) if many else [out_shape]
    out_specs = list(out_specs or [VM] * len(outs))

    def run(*args):
        args = list(args)
        far_in = [n for n, spec in enumerate(in_specs) if spec is HB]
        far_out = [n for n, spec in enumerate(out_specs) if spec is HB]
        n_in, n_out, n_own = len(in_specs), len(outs), len(scratch)
        extra = [pltpu.VMEM(args[n].shape, args[n].dtype) for n in far_in]
        extra += [pltpu.VMEM(outs[n].shape, outs[n].dtype) for n in far_out]
        moved = len(far_in) + len(far_out)

        def kernel(*refs):
            ins, res = list(refs[:n_in]), list(refs[n_in : n_in + n_out])
            own = refs[n_in + n_out : n_in + n_out + n_own]
            held = refs[n_in + n_out + n_own :]
            sems = held[-1] if moved else None
            copies = []
            for m, n in enumerate(far_in):
                copies.append(pltpu.make_async_copy(ins[n], held[m], sems.at[m]))
                ins[n] = held[m]
            for c in copies:
                c.start()
            arriving = dict(zip(far_in, copies))

            def ready(*places):
                for n in places:
                    arriving.pop(n).wait()

            more = {"ready": ready} if lazy else {}
            if not lazy:
                ready(*far_in)
            copies = []
            for m, n in enumerate(far_out):
                m += len(far_in)
                copies.append(pltpu.make_async_copy(held[m], res[n], sems.at[m]))
                res[n] = held[m]
            body(*ins, *res, *own, **more)
            for c in copies:
                c.start()
            for c in copies:
                c.wait()

        result = pl.pallas_call(
            kernel,
            out_shape=outs,
            in_specs=list(in_specs),
            out_specs=out_specs,
            scratch_shapes=list(scratch)
            + extra
            + ([pltpu.SemaphoreType.DMA((moved,))] if moved else []),
            compiler_params=pltpu.CompilerParams(vmem_limit_bytes=limit * 2**20),
            cost_estimate=pl.CostEstimate(
                flops=0, bytes_accessed=int(us * 3.3e6), transcendentals=0
            ),
        )(*args)
        return result if many else result[0]

    return run


def dot_nt(a, b):
    return lax.dot_general(a, b, (((1,), (1,)), ((), ())), preferred_element_type=F32)


def dot_tn(a, b):
    return lax.dot_general(a, b, (((0,), (0,)), ((), ())), preferred_element_type=F32)


def dot_nn(a, b):
    return jnp.dot(a, b, preferred_element_type=F32)


def iota(shape, dim):
    return lax.broadcasted_iota(I32, shape, dim)


def length_of(meta, slot, seqs):
    return meta[2 + seqs + meta[2 + slot]]


def pack_kernel(meta, hist, owners_t, rows_t, out, code, *, dp, seq_dev, per_peer, mp, capacity):
    here = meta[0]
    steps, part = hist.shape[1], hist.shape[2]

    def per_dest(d, carry):
        def per_slot(i, count):
            src = meta[2 + d * seq_dev + i]
            hit = lax.div(src, seq_dev) == here

            @pl.when(hit)
            def _():
                value = hist[src - here * seq_dev]
                for side in range(2):
                    start = pl.multiple_of((side * per_peer + count) * steps, steps)
                    out[jnp.bitwise_xor(d, side * (dp // 2)), pl.ds(start, steps), :] = value

            return count + hit.astype(I32)

        lax.fori_loop(0, seq_dev, per_slot, jnp.int32(0))
        return carry

    lax.fori_loop(0, dp, per_dest, jnp.int32(0))
    top, events = owners_t.shape
    devices = dp * mp
    o_id = iota((devices, events), 0)
    named = jnp.zeros((devices, events), F32)
    row = jnp.zeros((devices, events), F32)
    positive = jnp.zeros((devices, events), F32)
    for j in range(top):
        same = jnp.where(owners_t[j : j + 1, :] == o_id, 1.0, 0.0)
        named = named + same
        row = row + same * rows_t[j : j + 1, :].astype(F32)
        if j == 0:
            positive = same
    before = (iota((events, events), 0) < iota((events, events), 1)).astype(BF)
    rank = dot_nn(named.astype(BF), before)
    code[...] = jnp.where(named > 0.0, 2.0 * rank + 1.0 + positive, 0.0)
    rank = jnp.where(named > 0.0, rank, -1.0)
    lane = iota((devices, part), 1)
    wanted = jnp.zeros((devices, part), F32)
    for c in range(capacity):
        one = jnp.sum(jnp.where(rank == float(c), row, 0.0), axis=1, keepdims=True)
        wanted = jnp.where(lane == c, one, wanted)
    high = jnp.floor(wanted * (1.0 / 256.0))
    low = wanted - 256.0 * high
    none = jnp.zeros((8 - mp, part), F32)
    for d in range(dp):
        mine = slice(d * mp, (d + 1) * mp)
        digits = [high[mine], none, low[mine], none] if mp < 8 else [high[mine], low[mine]]
        out[d, 2 * per_peer * steps :, :] = jnp.concatenate(digits, axis=0).astype(BF)


def take_kernel(meta, arrived, out, digits, *, dp, seq_dev, per_peer, steps):
    for side in range(2):
        block = jnp.bitwise_xor(meta[0], side * (dp // 2))
        anchors = [lax.div(meta[2 + block * seq_dev + k], seq_dev) for k in range(seq_dev)]
        for k in range(seq_dev):
            rank = jnp.int32(side * per_peer)
            for earlier in range(k):
                rank = rank + (anchors[earlier] == anchors[k]).astype(I32)
            start = pl.multiple_of(rank * steps, steps)
            at = (side * seq_dev + k) * steps
            out[at : at + steps, :] = arrived[anchors[k], pl.ds(start, steps), :]
    for d in range(dp):
        digits[d * 16 : (d + 1) * 16, :] = arrived[d, 2 * per_peer * steps :, :]


def forward_kernel(meta, *refs, mp, dp, seqs, seq_dev, steps, width, cols, quarter):
    blocks = refs[:mp]
    w_in = refs[mp]
    wide, projected, turned, own = refs[mp + 1 : mp + 5]
    gated_out = refs[mp + 5 : 2 * mp + 5]
    feat, gated = refs[2 * mp + 5 :]
    here_mp = meta[1]
    part = width // mp
    counts = [
        length_of(meta, block * seq_dev + k, seqs)
        for block in (meta[0], jnp.bitwise_xor(meta[0], dp // 2))
        for k in range(seq_dev)
    ]
    half_rows = seq_dev * steps
    rows_all = 2 * half_rows
    for j in range(mp):
        start = pl.multiple_of(jnp.bitwise_xor(here_mp, j) * part, part)
        feat[:, pl.ds(start, part)] = blocks[j][...]
    for side in range(2):
        start = pl.multiple_of(side * half_rows + here_mp * quarter, quarter)
        own[side * quarter : (side + 1) * quarter, :] = feat[pl.ds(start, quarter), :]
    for g in range(rows_all // BLOCK):
        rows = slice(g * BLOCK, (g + 1) * BLOCK)
        x = feat[rows, :].astype(F32)
        centered = x - jnp.mean(x, axis=-1, keepdims=True)
        spread = jnp.mean(centered * centered, axis=-1, keepdims=True)
        y = (centered * lax.rsqrt(spread + EPS_NORM)).astype(BF)
        feat[rows, :] = y
        turned[:width, rows] = y.T
    for c in range(4):
        pre = dot_nn(feat[...], w_in[c])
        sigma = jax.nn.sigmoid(pre)
        projected[c] = (pre * sigma).astype(BF)
        projected[5 + c] = (sigma * (1.0 + pre * (1.0 - sigma))).astype(BF)
    root = 1.0 / math.sqrt(DH)
    t_id = iota((BLOCK, BLOCK), 0)
    s_id = iota((BLOCK, BLOCK), 1)
    per_block = BLOCK // steps
    causal = (t_id // steps == s_id // steps) & (s_id <= t_id)
    for g in range(rows_all // BLOCK):
        rows = slice(g * BLOCK, (g + 1) * BLOCK)
        count = jnp.zeros((BLOCK, BLOCK), I32)
        for i in range(per_block):
            count = jnp.where(t_id // steps == i, counts[g * per_block + i], count)
        allowed = causal & (s_id % steps < count)
        scale = jnp.where(allowed, 1.0 / count.astype(F32), 0.0)
        for h in range(cols // DH):
            lanes = slice(h * DH, (h + 1) * DH)
            scores = dot_nt(projected[2, rows, lanes], projected[3, rows, lanes]) * root
            sigma = jax.nn.sigmoid(scores)
            weights = (scores * sigma * scale).astype(BF)
            projected[4, rows, lanes] = weights
            wide[2, rows, lanes] = sigma * (1.0 + scores * (1.0 - sigma)) * (scale * root)
            mixed = dot_nn(weights, projected[1, rows, lanes])
            centered = mixed - jnp.mean(mixed, axis=-1, keepdims=True)
            spread = jnp.mean(centered * centered, axis=-1, keepdims=True)
            inv = lax.rsqrt(spread + EPS_NORM)
            norm = centered * inv
            wide[0, rows, lanes] = norm
            wide[1, rows, lanes] = jnp.broadcast_to(inv, norm.shape)
            done = (norm * projected[0, rows, lanes].astype(F32)).astype(BF)
            gated[rows, lanes] = done
            turned[width + h * DH : width + (h + 1) * DH, rows] = done.T
    for j in range(mp):
        for side in range(2):
            start = side * half_rows + jnp.bitwise_xor(here_mp, j) * quarter
            start = pl.multiple_of(start, quarter)
            gated_out[j][side * quarter : (side + 1) * quarter, :] = gated[pl.ds(start, quarter), :]


def out_kernel(own, *refs, mp):
    gathered, weights = refs[:mp], refs[mp : 2 * mp]
    unit, unit_bf, inv_o = refs[2 * mp :]
    total = own[...].astype(F32)
    for j in range(mp):
        total = total + dot_nn(gathered[j][...], weights[j][...])
    inv = lax.rsqrt(jnp.sum(total * total, axis=-1, keepdims=True) + EPS_UNIT)
    u = total * inv
    unit[...] = u
    unit_bf[...] = u.astype(BF)
    inv_o[...] = jnp.broadcast_to(inv, inv_o.shape)


def look_kernel(meta, *refs, mp, dp, capacity, chunk, share):
    blocks, catalogue, looked, incoming, returning, digits, asked = refs[:mp], *refs[mp:]
    stock, _ = catalogue.shape
    for j in range(mp):
        digits[...] = blocks[j][...].astype(F32)
        for d in range(dp):
            high = digits[pl.ds(d * 16 + meta[1], 1), :]
            low = digits[pl.ds(d * 16 + 8 + meta[1], 1), :]
            asked[j * dp + d : j * dp + d + 1, :] = (256.0 * high + low)[:, :capacity]
    groups = dp * mp
    slots = groups * capacity
    half = dp // 2
    table = asked[...]
    slot = iota((1, slots), 1).astype(F32)
    group = jnp.floor((slot + 0.5) * (1.0 / capacity))
    local = slot - group * capacity
    column = (iota((capacity, slots), 0).astype(F32) == local).astype(F32)
    spread = lax.dot_general(
        table,
        column,
        (((1,), (0,)), ((), ())),
        precision=lax.Precision.HIGHEST,
        preferred_element_type=F32,
    )
    line = iota((groups, 1), 0)
    offset = lax.div(line, dp)
    index = line - offset * dp
    side = (index >= half) != (meta[0] >= half)
    near = jnp.where(index >= half, index - half, index)
    first = (near * mp + jnp.bitwise_xor(offset, meta[1])) * 2 + side.astype(I32)
    here = jnp.where(meta[0] >= half, meta[0] - half, meta[0])
    second = (offset * half + jnp.bitwise_xor(near, here)) * 2 + side.astype(I32)
    rows = [
        jnp.sum(jnp.where(group == g.astype(F32), spread, 0.0), axis=0, keepdims=True).astype(I32)
        for g in (first, second)
    ]
    incoming[...] = rows[0]
    returning[...] = rows[1] if share else rows[0]
    for s in range(0, slots, chunk):
        hot = jnp.where(iota((stock, chunk), 0) == incoming[:, s : s + chunk], 1.0, 0.0).astype(BF)
        looked[s : s + chunk, :] = dot_tn(hot, catalogue[...]).astype(BF)


def score_kernel(
    meta, items, code, code_far, units, expo, inv_o, total_o,
    *, dp, devices, capacity, chunk,
):
    events = units.shape[0] // 2
    near = devices // 2
    slots = items.shape[0]
    half = pl.multiple_of(lax.div(meta[0], dp // 2) * near, near)
    codes_in = [c[pl.ds(half, near), :].astype(BF) for c in (code, code_far)]
    for s in range(0, slots, chunk):
        rows = slice(s, s + chunk)
        x = items[rows, :]
        xf = x.astype(F32)
        inv = lax.rsqrt(jnp.sum(xf * xf, axis=-1, keepdims=True) + EPS_UNIT)
        inv_o[rows, :] = jnp.broadcast_to(inv, (chunk, BLOCK))
        cosines = dot_nt(x, units[...]) * (inv * (1.0 / COSINE_DIVISOR))
        slot = s + iota((chunk, 1), 0).astype(F32)
        owner = jnp.floor((slot + 0.5) * (1.0 / (2 * capacity)))
        local = slot - owner * (2 * capacity)
        far = local >= capacity
        local = jnp.where(far, local - capacity, local)
        named = owner == iota((chunk, near), 1).astype(F32)
        for side in range(2):
            lanes = slice(side * events, (side + 1) * events)
            logits = cosines[:, lanes]
            spread = jnp.where(named & (far == (side == 1)), 1.0, 0.0).astype(BF)
            codes = dot_nn(spread, codes_in[side])
            first = codes == 2.0 * local + 2.0
            other = codes == 2.0 * local + 1.0
            e = jnp.exp(logits)
            total_o[:, lanes] = (
                jnp.sum(jnp.where(first | other, e, 0.0), axis=0, keepdims=True)
                + (total_o[:, lanes] if s else 0.0)
            )
            expo[rows, lanes] = jnp.where(first, -e, jnp.where(other, e, 0.0))


def shares(meta, expo, total, total_far, dp, seqs, seq_dev, steps):
    events = total.shape[1] // 2
    position = meta[1] * events + iota((1, events), 1)
    valid = []
    for base in (meta[0], jnp.bitwise_xor(meta[0], dp // 2)):
        v = jnp.zeros((1, events), F32)
        for k in range(seq_dev):
            step = position - k * steps
            v = jnp.where((step >= 0) & (step < length_of(meta, base * seq_dev + k, seqs)), 1.0, v)
        valid.append(v)
    valid = jnp.concatenate(valid, axis=1) * (1.0 / COSINE_DIVISOR)
    full = total[...] + jnp.concatenate([total_far[:, events:], total_far[:, :events]], axis=1)
    factor = valid / full
    return lambda rows: jnp.abs(expo[rows, :]) * factor - jnp.where(expo[rows, :] < 0.0, valid, 0.0)


def slope_kernel(
    meta, items, code, code_far, expo, inv, total, total_far, slopes, slopes_bf, ledger,
    *, dp, seqs, seq_dev, steps, chunk,
):
    share = shares(meta, expo, total, total_far, dp, seqs, seq_dev, steps)
    events, width = slopes.shape[0] // 2, slopes.shape[1]
    both = jnp.zeros((2 * events, width), F32)
    for s in range(0, items.shape[0], chunk):
        rows = slice(s, s + chunk)
        both = both + dot_tn((share(rows) * inv[rows, 0:1]).astype(BF), items[rows, :])
    slopes[...] = both
    slopes_bf[...] = both.astype(BF)
    near = ledger.shape[0]
    each = items.shape[0] // near
    weight = jnp.concatenate(
        [
            jnp.sum(share(slice(o * each, (o + 1) * each)), axis=0, keepdims=True)
            for o in range(near)
        ],
        axis=0,
    )
    high = weight.astype(BF)
    low = (weight - high.astype(F32)).astype(BF)
    half = pl.multiple_of(lax.div(meta[0], dp // 2) * near, near)
    codes = [c[pl.ds(half, near), :].astype(BF) for c in (code, code_far)]
    for n, part in enumerate([high, low, jnp.concatenate(codes, axis=1)]):
        ledger[:, n * 2 * events : (n + 1) * 2 * events] = part


def send_kernel(
    meta, expo, total, total_far, units, sending,
    *, dp, seqs, seq_dev, steps, chunk,
):
    share = shares(meta, expo, total, total_far, dp, seqs, seq_dev, steps)
    for s in range(0, expo.shape[0], chunk):
        rows = slice(s, s + chunk)
        hot = jnp.where(expo[rows, :] == 0.0, 0.0, 1.0).astype(BF)
        unit_rows = dot_nn(hot, units[...])
        weight = jnp.sum(share(rows), axis=1, keepdims=True)
        sending[rows, :] = (unit_rows * weight).astype(BF)


def mail_kernel(meta, *refs, half, mp, events, capacity):
    units, ledgers, outs = refs[:half], refs[half : 2 * half], refs[2 * half : -2]
    hots, ledger = refs[-2:]
    here = jnp.where(meta[0] >= half, meta[0] - half, meta[0])
    slot = iota((2 * capacity, 2 * events), 0)
    event = iota((2 * capacity, 2 * events), 1)
    far = slot >= capacity
    local = jnp.where(far, slot - capacity, slot).astype(F32)
    same = far == (event >= events)
    for j in range(half):
        ledger[...] = ledgers[j][...].astype(F32)
        weights = []
        for k in range(mp):
            line = ledger[pl.ds(here * mp + jnp.bitwise_xor(meta[1], k), 1), :]
            code = line[:, 4 * events : 6 * events]
            mine = same & (jnp.floor((code - 1.0) * 0.5) == local)
            hots[k * 2 * capacity : (k + 1) * 2 * capacity, :] = mine.astype(BF)
            weight = line[:, : 2 * events] + line[:, 2 * events : 4 * events]
            weights.append(jnp.sum(jnp.where(mine, weight, 0.0), axis=1, keepdims=True))
        rows = dot_nn(hots[...], units[j][...])
        for k in range(mp):
            part = rows[k * 2 * capacity : (k + 1) * 2 * capacity] * weights[k]
            outs[k][j * 2 * capacity : (j + 1) * 2 * capacity, :] = part.astype(BF)


def out_cot_kernel(units, inv_out, slopes, slopes_back, out_cot):
    events = units.shape[0] // 2
    for side in range(2):
        rows = slice(side * events, (side + 1) * events)
        there = slice((1 - side) * events, (2 - side) * events)
        u = units[rows, :]
        s = slopes[rows, :] + slopes_back[there, :].astype(F32)
        along = jnp.sum(u * s, axis=-1, keepdims=True)
        out_cot[rows, :] = ((s - u * along) * inv_out[rows, 0:1]).astype(BF)


def spread_kernel(incoming, *refs, at, chunk):
    landed, out = refs[:-1], refs[-1]
    for r in range(0, out.shape[0], chunk):
        v, first = 0.0, at
        for part in landed:
            slots = slice(first, first + part.shape[0])
            line = r + iota((chunk, part.shape[0]), 0)
            hot = jnp.where(line == incoming[:, slots], 1.0, 0.0).astype(BF)
            v = v + dot_nn(hot, part[...])
            first += part.shape[0]
        out[r : r + chunk, :] = v


def finish_kernel(incoming, catalogue, before, landed, out, *, at, chunk):
    slots = landed.shape[0]
    for r in range(0, out.shape[0], chunk):
        rows = slice(r, r + chunk)
        line = r + iota((chunk, slots), 0)
        hot = jnp.where(line == incoming[:, at : at + slots], 1.0, 0.0).astype(BF)
        v = before[rows, :] + dot_nn(hot, landed[...])
        c = catalogue[rows, :].astype(F32)
        inv = lax.rsqrt(jnp.sum(c * c, axis=-1, keepdims=True) + EPS_UNIT)
        c = c * inv
        out[rows, :] = (v - c * jnp.sum(c * v, axis=-1, keepdims=True)) * inv


def backward_kernel(meta, *refs, mp, dp):
    blocks = refs[:mp]
    w_out, wide, projected, turned = refs[mp : mp + 4]
    outs = refs[mp + 4 : -2]
    whole, cot = refs[-2:]
    half = dp // 2
    quarter, width = blocks[0].shape[0] // 2, blocks[0].shape[1]
    rows_all = whole.shape[0]
    cols = w_out.shape[0]
    for j in range(mp):
        for side in range(2):
            start = side * (rows_all // 2) + jnp.bitwise_xor(meta[1], j) * quarter
            rows = slice(side * quarter, (side + 1) * quarter)
            whole[pl.ds(pl.multiple_of(start, quarter), quarter), :] = blocks[j][rows, :]
    gated_cot = dot_nt(whole[...], w_out[...]).astype(BF).astype(F32)
    for g in range(rows_all // BLOCK):
        rows = slice(g * BLOCK, (g + 1) * BLOCK)
        for h in range(cols // DH):
            lanes = slice(h * DH, (h + 1) * DH)
            d_gated = gated_cot[rows, lanes]
            n = wide[0, rows, lanes]
            d_norm = d_gated * projected[0, rows, lanes].astype(F32)
            d_mixed = wide[1, rows, lanes] * (
                d_norm
                - jnp.mean(d_norm, axis=-1, keepdims=True)
                - n * jnp.mean(d_norm * n, axis=-1, keepdims=True)
            )
            d_mixed = d_mixed.astype(BF)
            d_weights = dot_nt(d_mixed, projected[1, rows, lanes]).astype(BF).astype(F32)
            d_values = dot_tn(projected[4, rows, lanes], d_mixed)
            d_scores = (d_weights * wide[2, rows, lanes]).astype(BF)
            d_queries = dot_nn(d_scores, projected[3, rows, lanes])
            d_keys = dot_tn(d_scores, projected[2, rows, lanes])
            for c, d in enumerate((d_gated * n, d_values, d_queries, d_keys)):
                step = projected[5 + c, rows, lanes].astype(F32)
                cot[c, rows, lanes] = (d.astype(BF).astype(F32) * step).astype(BF)
    share = width // dp
    mine = pl.multiple_of(lax.div(meta[0], half) * (width // 2), width // 2)
    here = jnp.where(meta[0] >= half, meta[0] - half, meta[0])
    normed = turned[pl.ds(mine, width // 2), :]
    for c in range(5):
        if c < 4:
            part = dot_nn(normed, cot[c]).astype(BF)
        else:
            lanes = pl.ds(mine, width // 2)
            part = dot_nn(turned[width:, :], whole[:, lanes]).T.astype(BF)
        for d in range(half):
            piece = part[d * share : (d + 1) * share, :]
            if len(outs) == 1:
                outs[0][d, c] = piece
                continue
            for j in range(half):

                @pl.when(jnp.bitwise_xor(here, j) == d)
                def _(j=j, piece=piece):
                    outs[j][c] = piece


def sum_kernel(*refs):
    parts, w_in_grad, w_out_grad = refs[:-2], *refs[-2:]
    for c in range(5):
        total = sum(p[c].astype(F32) for p in parts)
        if c < 4:
            w_in_grad[c] = total
        else:
            w_out_grad[...] = total.T


def swapped(x, axis, bit):
    size = lax.axis_size(axis)
    return lax.ppermute(x, axis, [(a, a ^ bit) for a in range(size)])


def gather_blocks(x, axis, half=None):
    size = lax.axis_size(axis)
    blocks = {0: x} if half is None else {0: x, size // 2: half}
    bit = size // 2 if half is None else size // 4
    while bit:
        for j in list(blocks):
            blocks[j ^ bit] = swapped(blocks[j], axis, bit)
        bit //= 2
    return [blocks[j] for j in range(size)]


def exchange(parts, axis):
    return [p if j == 0 else swapped(p, axis, j) for j, p in enumerate(parts)]


def per_device(history, lengths, source, owners, item_rows, catalogue, w_in, w_out):
    dp = lax.axis_size("dp")
    mp = lax.axis_size("mp")
    devices = dp * mp
    near = devices // 2
    seq_dev, steps, part = history.shape
    width = part * mp
    cols = w_in.shape[2]
    rows_all = seq_dev * steps
    quarter = rows_all // mp
    events, top = owners.shape
    asks = events * top
    capacity = max(2, (3 * asks + 2 * devices - 1) // (2 * devices))
    slots = devices * capacity
    stock = catalogue.shape[0]
    per_peer = (seq_dev + dp - 1) // dp
    chunk = math.gcd(slots, 512)
    short = dp <= 8 and near <= 16 and 6 * events <= width
    S = jax.ShapeDtypeStruct
    here_dp = lax.axis_index("dp")
    place = jnp.stack([here_dp, lax.axis_index("mp")]).astype(I32)
    meta = jnp.concatenate([place, source, lengths])
    seqs = source.shape[0]
    halves = [list(range(near)), list(range(near, devices))]

    def partner(x):
        return swapped(x, "dp", dp // 2)

    def in_half(x):
        return lax.all_to_all(
            x.reshape(near, 2 * capacity, width),
            ("dp", "mp"),
            split_axis=0,
            concat_axis=0,
            tiled=True,
            axis_index_groups=halves,
        ).reshape(slots, width)

    w_out_y = swapped(w_out, "mp", mp // 2)
    packed, code = call(
        functools.partial(
            pack_kernel, dp=dp, seq_dev=seq_dev, per_peer=per_peer, mp=mp, capacity=capacity
        ),
        [S((dp, 2 * per_peer * steps + 16, part), BF), S((devices, events), F32)],
        [SM, HB, HB, HB],
        4,
        limit=58,
    )(meta, history, owners.T, item_rows.T)
    arrived = lax.all_to_all(packed, "dp", split_axis=0, concat_axis=0, tiled=True)
    arrived, w_out_y = lax.optimization_barrier((arrived, w_out_y))
    rows, digits = call(
        functools.partial(take_kernel, dp=dp, seq_dev=seq_dev, per_peer=per_peer, steps=steps),
        [S((2 * rows_all, part), BF), S((16 * dp, part), BF)],
        [SM, VM],
        1,
    )(meta, arrived)
    digits_y = swapped(digits, "mp", mp // 2)
    rows, digits_y = lax.optimization_barrier((rows, digits_y))
    rows_y = swapped(rows, "mp", mp // 2)
    digits = gather_blocks(digits, "mp", digits_y)
    code_far = partner(code)
    looked, incoming, returning = call(
        functools.partial(
            look_kernel, mp=mp, dp=dp, capacity=capacity, chunk=chunk, share=short
        ),
        [S((slots, width), BF), S((1, slots), I32), S((1, slots), I32)],
        [SM] + [VM] * mp + [VM],
        4,
        scratch=[pltpu.VMEM((16 * dp, part), F32), pltpu.VMEM((devices, capacity), F32)],
    )(meta, *digits, catalogue)
    looked, rows_y, code_far = lax.optimization_barrier((looked, rows_y, code_far))
    features = gather_blocks(rows, "mp", rows_y)
    items = in_half(looked)

    wide, projected, turned, own, *gated = call(
        functools.partial(
            forward_kernel,
            mp=mp,
            dp=dp,
            seqs=seqs,
            seq_dev=seq_dev,
            steps=steps,
            width=width,
            cols=cols,
            quarter=quarter,
        ),
        [
            S((3, 2 * rows_all, cols), F32),
            S((9, 2 * rows_all, cols), BF),
            S((width + cols, 2 * rows_all), BF),
            S((2 * quarter, width), BF),
        ]
        + [S((2 * quarter, cols), BF)] * mp,
        [SM] + [VM] * mp + [VM],
        10,
        scratch=[pltpu.VMEM((2 * rows_all, width), BF), pltpu.VMEM((2 * rows_all, cols), BF)],
        limit=36,
    )(meta, *features, w_in)
    gathered = exchange(gated, "mp")
    w_out_blocks = gather_blocks(w_out, "mp", w_out_y)
    units, units_bf, inv_out = call(
        functools.partial(out_kernel, mp=mp),
        [
            S((2 * quarter, width), F32),
            S((2 * quarter, width), BF),
            S((2 * quarter, BLOCK), F32),
        ],
        [VM] + [VM] * (2 * mp),
        2,
    )(own, *gathered, *w_out_blocks)

    expo, inv_item, total = call(
        functools.partial(
            score_kernel, dp=dp, devices=devices, capacity=capacity, chunk=chunk
        ),
        [S((slots, 2 * events), F32), S((slots, BLOCK), F32), S((1, 2 * events), F32)],
        [SM, VM] + [VM] * 3,
        4,
    )(meta, items, code, code_far, units_bf)
    total_far = partner(total)
    sizes = dict(dp=dp, seqs=seqs, seq_dev=seq_dev, steps=steps, chunk=chunk)
    slopes, slopes_bf, ledger = call(
        functools.partial(slope_kernel, **sizes),
        [
            S((2 * events, width), F32),
            S((2 * events, width), BF),
            S((near, width), BF),
        ],
        [SM, VM] + [VM] * 6,
        3,
    )(meta, items, code, code_far, expo, inv_item, total, total_far)
    slopes_back = partner(slopes_bf)
    if short:
        column = range(1, dp // 2)
        ledgers = [ledger] + [swapped(ledger, "dp", j) for j in column]
        all_units = [units_bf] + [swapped(units_bf, "dp", j) for j in column]
        mail = call(
            functools.partial(
                mail_kernel, half=dp // 2, mp=mp, events=events, capacity=capacity
            ),
            [S((dp * capacity, width), BF)] * mp,
            [SM] + [VM] * dp,
            4,
            scratch=[
                pltpu.VMEM((mp * 2 * capacity, 2 * events), BF),
                pltpu.VMEM((near, width), F32),
            ],
        )(meta, *all_units, *ledgers)
        landed = exchange(mail, "mp")
    out_cot = call(out_cot_kernel, S((2 * events, width), BF), [VM] * 4, 1)(
        units, inv_out, slopes, slopes_back
    )
    cots = gather_blocks(out_cot, "mp")
    pieces = [S((5, width // dp, cols), BF)] * (dp // 2)
    parts = call(
        functools.partial(backward_kernel, mp=mp, dp=dp),
        pieces if short else [S((dp // 2, 5, width // dp, cols), BF)],
        [SM] + [VM] * (mp + 4),
        10,
        scratch=[
            pltpu.VMEM((2 * rows_all, width), BF),
            pltpu.VMEM((4, 2 * rows_all, cols), BF),
        ],
        limit=36,
    )(meta, *cots, w_out, wide, projected, turned)
    if short:
        parts = exchange(parts, "dp")
        parts, landed[:-1] = lax.optimization_barrier((parts, landed[:-1]))
        w_in_grad, w_out_grad = call(
            sum_kernel,
            [S((4, width // dp, cols), F32), S((cols, width // dp), F32)],
            [VM] * len(parts),
            1,
        )(*parts)
    else:
        got = lax.all_to_all(
            parts[0],
            "dp",
            split_axis=0,
            concat_axis=0,
            tiled=True,
            axis_index_groups=[list(range(dp // 2)), list(range(dp // 2, dp))],
        )
        grads = jnp.sum(got.astype(F32), axis=0)
        w_in_grad, w_out_grad = grads[:4], grads[4].T
        sending = call(
            functools.partial(send_kernel, **sizes),
            S((slots, width), BF),
            [SM] + [VM] * 4,
            3,
        )(meta, expo, total, total_far, units_bf)
        landed = [in_half(sending)]
    rows_chunk = math.gcd(stock, 128)
    last = slots // 4
    if len(landed) == 1:
        landed = [landed[0][: slots - last], landed[0][slots - last :]]
    before = call(
        functools.partial(spread_kernel, at=0, chunk=rows_chunk),
        S((stock, width), F32),
        [VM] * len(landed),
        3,
    )(returning, *landed[:-1])
    if short:
        before, _ = lax.optimization_barrier((before, w_in_grad))
    cat_grad = call(
        functools.partial(finish_kernel, at=slots - last, chunk=rows_chunk),
        S((stock, width), F32),
        [VM] * 4,
        3,
        out_specs=[HB],
    )(returning, catalogue, before, landed[-1])
    return (w_in_grad, w_out_grad, cat_grad)


def solution(mesh):
    placed = (
        P("dp", None, "mp"),
        P(),
        P(),
        P(("dp", "mp"), None),
        P(("dp", "mp"), None),
        P(("dp", "mp"), None),
        P(None, None, "mp"),
        P("mp", None),
    )
    return jax.shard_map(
        per_device,
        mesh=mesh,
        in_specs=placed,
        out_specs=(P(None, "dp", "mp"), P("mp", "dp"), P(("dp", "mp"), None)),
        check_vma=False,
    )
```

```python
import functools
import math

import jax
import jax.numpy as jnp
from jax import lax
from jax.experimental import pallas as pl
from jax.experimental.pallas import tpu as pltpu
from jax.sharding import PartitionSpec as P

DH = 128
COSINE_DIVISOR = 0.05
EPS_NORM = 1e-05
EPS_UNIT = 1e-06
BF = jnp.bfloat16
F32 = jnp.float32
I32 = jnp.int32
BLOCK = 128

VM = pl.BlockSpec(memory_space=pltpu.VMEM)
SM = pl.BlockSpec(memory_space=pltpu.SMEM)
HB = pl.BlockSpec(memory_space=pltpu.HBM)


def call(body, out_shape, in_specs, us, scratch=(), limit=16, out_specs=None, lazy=False):
    many = isinstance(out_shape, (list, tuple))
    outs = list(out_shape) if many else [out_shape]
    out_specs = list(out_specs or [VM] * len(outs))

    def run(*args):
        args = list(args)
        far_in = [n for n, spec in enumerate(in_specs) if spec is HB]
        far_out = [n for n, spec in enumerate(out_specs) if spec is HB]
        n_in, n_out, n_own = len(in_specs), len(outs), len(scratch)
        extra = [pltpu.VMEM(args[n].shape, args[n].dtype) for n in far_in]
        extra += [pltpu.VMEM(outs[n].shape, outs[n].dtype) for n in far_out]
        moved = len(far_in) + len(far_out)

        def kernel(*refs):
            ins, res = list(refs[:n_in]), list(refs[n_in : n_in + n_out])
            own = refs[n_in + n_out : n_in + n_out + n_own]
            held = refs[n_in + n_out + n_own :]
            sems = held[-1] if moved else None
            copies = []
            for m, n in enumerate(far_in):
                copies.append(pltpu.make_async_copy(ins[n], held[m], sems.at[m]))
                ins[n] = held[m]
            for c in copies:
                c.start()
            arriving = dict(zip(far_in, copies))

            def ready(*places):
                for n in places:
                    arriving.pop(n).wait()

            more = {"ready": ready} if lazy else {}
            if not lazy:
                ready(*far_in)
            copies = []
            for m, n in enumerate(far_out):
                m += len(far_in)
                copies.append(pltpu.make_async_copy(held[m], res[n], sems.at[m]))
                res[n] = held[m]
            body(*ins, *res, *own, **more)
            for c in copies:
                c.start()
            for c in copies:
                c.wait()

        result = pl.pallas_call(
            kernel,
            out_shape=outs,
            in_specs=list(in_specs),
            out_specs=out_specs,
            scratch_shapes=list(scratch)
            + extra
            + ([pltpu.SemaphoreType.DMA((moved,))] if moved else []),
            compiler_params=pltpu.CompilerParams(vmem_limit_bytes=limit * 2**20),
            cost_estimate=pl.CostEstimate(
                flops=0, bytes_accessed=int(us * 3.3e6), transcendentals=0
            ),
        )(*args)
        return result if many else result[0]

    return run


def dot_nt(a, b):
    return lax.dot_general(a, b, (((1,), (1,)), ((), ())), preferred_element_type=F32)


def dot_tn(a, b):
    return lax.dot_general(a, b, (((0,), (0,)), ((), ())), preferred_element_type=F32)


def dot_nn(a, b):
    return jnp.dot(a, b, preferred_element_type=F32)


def iota(shape, dim):
    return lax.broadcasted_iota(I32, shape, dim)


def length_of(meta, slot, seqs):
    return meta[2 + seqs + meta[2 + slot]]


def pack_kernel(meta, hist, owners_t, rows_t, out, code, *, dp, seq_dev, per_peer, mp, capacity):
    here = meta[0]
    steps, part = hist.shape[1], hist.shape[2]

    def per_dest(d, carry):
        def per_slot(i, count):
            src = meta[2 + d * seq_dev + i]
            hit = lax.div(src, seq_dev) == here

            @pl.when(hit)
            def _():
                value = hist[src - here * seq_dev]
                for side in range(2):
                    start = pl.multiple_of((side * per_peer + count) * steps, steps)
                    out[jnp.bitwise_xor(d, side * (dp // 2)), pl.ds(start, steps), :] = value

            return count + hit.astype(I32)

        lax.fori_loop(0, seq_dev, per_slot, jnp.int32(0))
        return carry

    lax.fori_loop(0, dp, per_dest, jnp.int32(0))
    top, events = owners_t.shape
    devices = dp * mp
    lanes = -(-capacity // 128) * 128
    o_id = iota((devices, events), 0)
    named = jnp.zeros((devices, events), F32)
    row = jnp.zeros((devices, events), F32)
    positive = jnp.zeros((devices, events), F32)
    for j in range(top):
        same = jnp.where(owners_t[j : j + 1, :] == o_id, 1.0, 0.0)
        named = named + same
        row = row + same * rows_t[j : j + 1, :].astype(F32)
        if j == 0:
            positive = same
    before = (iota((events, events), 0) < iota((events, events), 1)).astype(BF)
    rank = dot_nn(named.astype(BF), before)
    code[...] = jnp.where(named > 0.0, 2.0 * rank + 1.0 + positive, 0.0)
    rank = jnp.where(named > 0.0, rank, -1.0)
    lane = iota((devices, lanes), 1)
    wanted = jnp.zeros((devices, lanes), F32)
    for c in range(capacity):
        one = jnp.sum(jnp.where(rank == float(c), row, 0.0), axis=1, keepdims=True)
        wanted = jnp.where(lane == c, one, wanted)
    high = jnp.floor(wanted * (1.0 / 256.0))
    low = wanted - 256.0 * high
    none = jnp.zeros((8 - mp, lanes), F32)
    for d in range(dp):
        mine = slice(d * mp, (d + 1) * mp)
        digits = [high[mine], none, low[mine], none] if mp < 8 else [high[mine], low[mine]]
        out[d, 2 * per_peer * steps :, :lanes] = jnp.concatenate(digits, axis=0).astype(BF)


def take_kernel(meta, arrived, out, digits, *, dp, seq_dev, per_peer, steps):
    for side in range(2):
        block = jnp.bitwise_xor(meta[0], side * (dp // 2))
        anchors = [lax.div(meta[2 + block * seq_dev + k], seq_dev) for k in range(seq_dev)]
        for k in range(seq_dev):
            rank = jnp.int32(side * per_peer)
            for earlier in range(k):
                rank = rank + (anchors[earlier] == anchors[k]).astype(I32)
            start = pl.multiple_of(rank * steps, steps)
            at = (side * seq_dev + k) * steps
            out[at : at + steps, :] = arrived[anchors[k], pl.ds(start, steps), :]
    for d in range(dp):
        digits[d * 16 : (d + 1) * 16, :] = arrived[d, 2 * per_peer * steps :, :]


def forward_kernel(meta, *refs, mp, dp, seqs, seq_dev, steps, width, cols, quarter):
    blocks = refs[:mp]
    w_in = refs[mp]
    wide, projected, turned, own = refs[mp + 1 : mp + 5]
    gated_out = refs[mp + 5 : 2 * mp + 5]
    feat, gated = refs[2 * mp + 5 :]
    here_mp = meta[1]
    part = width // mp
    counts = [
        length_of(meta, block * seq_dev + k, seqs)
        for block in (meta[0], jnp.bitwise_xor(meta[0], dp // 2))
        for k in range(seq_dev)
    ]
    half_rows = seq_dev * steps
    rows_all = 2 * half_rows
    for j in range(mp):
        start = pl.multiple_of(jnp.bitwise_xor(here_mp, j) * part, part)
        feat[:, pl.ds(start, part)] = blocks[j][...]
    for side in range(2):
        start = pl.multiple_of(side * half_rows + here_mp * quarter, quarter)
        own[side * quarter : (side + 1) * quarter, :] = feat[pl.ds(start, quarter), :]
    for g in range(rows_all // BLOCK):
        rows = slice(g * BLOCK, (g + 1) * BLOCK)
        x = feat[rows, :].astype(F32)
        centered = x - jnp.mean(x, axis=-1, keepdims=True)
        spread = jnp.mean(centered * centered, axis=-1, keepdims=True)
        y = (centered * lax.rsqrt(spread + EPS_NORM)).astype(BF)
        feat[rows, :] = y
        turned[:width, rows] = y.T
    for c in range(4):
        pre = dot_nn(feat[...], w_in[c])
        sigma = jax.nn.sigmoid(pre)
        projected[c] = (pre * sigma).astype(BF)
        projected[5 + c] = (sigma * (1.0 + pre * (1.0 - sigma))).astype(BF)
    root = 1.0 / math.sqrt(DH)
    t_id = iota((BLOCK, BLOCK), 0)
    s_id = iota((BLOCK, BLOCK), 1)
    per_block = BLOCK // steps
    causal = (t_id // steps == s_id // steps) & (s_id <= t_id)
    for g in range(rows_all // BLOCK):
        rows = slice(g * BLOCK, (g + 1) * BLOCK)
        count = jnp.zeros((BLOCK, BLOCK), I32)
        for i in range(per_block):
            count = jnp.where(t_id // steps == i, counts[g * per_block + i], count)
        allowed = causal & (s_id % steps < count)
        scale = jnp.where(allowed, 1.0 / count.astype(F32), 0.0)
        for h in range(cols // DH):
            lanes = slice(h * DH, (h + 1) * DH)
            scores = dot_nt(projected[2, rows, lanes], projected[3, rows, lanes]) * root
            sigma = jax.nn.sigmoid(scores)
            weights = (scores * sigma * scale).astype(BF)
            projected[4, rows, lanes] = weights
            wide[2, rows, lanes] = sigma * (1.0 + scores * (1.0 - sigma)) * (scale * root)
            mixed = dot_nn(weights, projected[1, rows, lanes])
            centered = mixed - jnp.mean(mixed, axis=-1, keepdims=True)
            spread = jnp.mean(centered * centered, axis=-1, keepdims=True)
            inv = lax.rsqrt(spread + EPS_NORM)
            norm = centered * inv
            wide[0, rows, lanes] = norm
            wide[1, rows, lanes] = jnp.broadcast_to(inv, norm.shape)
            done = (norm * projected[0, rows, lanes].astype(F32)).astype(BF)
            gated[rows, lanes] = done
            turned[width + h * DH : width + (h + 1) * DH, rows] = done.T
    for j in range(mp):
        for side in range(2):
            start = side * half_rows + jnp.bitwise_xor(here_mp, j) * quarter
            start = pl.multiple_of(start, quarter)
            gated_out[j][side * quarter : (side + 1) * quarter, :] = gated[pl.ds(start, quarter), :]


def out_kernel(own, *refs, mp):
    gathered, weights = refs[:mp], refs[mp : 2 * mp]
    unit, unit_bf, inv_o, *sides = refs[2 * mp :]
    half = own.shape[0] // 2
    for side, rows in enumerate((slice(0, half), slice(half, 2 * half))):
        total = own[rows, :].astype(F32)
        for j in range(mp):
            total = total + dot_nn(gathered[j][rows, :], weights[j][...])
        inv = lax.rsqrt(jnp.sum(total * total, axis=-1, keepdims=True) + EPS_UNIT)
        u = total * inv
        unit[rows, :] = u
        unit_bf[rows, :] = u.astype(BF)
        sides[side][...] = u.astype(BF)
        inv_o[rows, :] = jnp.broadcast_to(inv, (half, BLOCK))


def look_kernel(meta, *refs, mp, dp, capacity, chunk, share):
    blocks, catalogue, looked, incoming, returning, digits, asked = refs[:mp], *refs[mp:]
    stock, _ = catalogue.shape
    for j in range(mp):
        digits[...] = blocks[j][...].astype(F32)
        for d in range(dp):
            high = digits[pl.ds(d * 16 + meta[1], 1), :]
            low = digits[pl.ds(d * 16 + 8 + meta[1], 1), :]
            asked[j * dp + d : j * dp + d + 1, :] = (256.0 * high + low)[:, :capacity]
    groups = dp * mp
    slots = groups * capacity
    half = dp // 2
    table = asked[...]
    slot = iota((1, slots), 1).astype(F32)
    group = jnp.floor((slot + 0.5) * (1.0 / capacity))
    local = slot - group * capacity
    column = (iota((capacity, slots), 0).astype(F32) == local).astype(F32)
    spread = lax.dot_general(
        table,
        column,
        (((1,), (0,)), ((), ())),
        precision=lax.Precision.HIGHEST,
        preferred_element_type=F32,
    )
    line = iota((groups, 1), 0)
    offset = lax.div(line, dp)
    index = line - offset * dp
    side = (index >= half) != (meta[0] >= half)
    near = jnp.where(index >= half, index - half, index)
    first = (near * mp + jnp.bitwise_xor(offset, meta[1])) * 2 + side.astype(I32)
    here = jnp.where(meta[0] >= half, meta[0] - half, meta[0])
    second = (offset * half + jnp.bitwise_xor(near, here)) * 2 + side.astype(I32)
    rows = [
        jnp.sum(jnp.where(group == g.astype(F32), spread, 0.0), axis=0, keepdims=True).astype(I32)
        for g in (first, second)
    ]
    incoming[...] = rows[0]
    returning[...] = rows[1] if share else rows[0]
    for s in range(0, slots, chunk):
        hot = jnp.where(iota((stock, chunk), 0) == incoming[:, s : s + chunk], 1.0, 0.0).astype(BF)
        looked[s : s + chunk, :] = dot_tn(hot, catalogue[...]).astype(BF)


def score_kernel(
    meta, items, code, code_far, units, expo, inv_o, total_o,
    *, dp, devices, capacity, chunk,
):
    events = units.shape[0] // 2
    near = devices // 2
    slots = items.shape[0]
    half = pl.multiple_of(lax.div(meta[0], dp // 2) * near, near)
    codes_in = [c[pl.ds(half, near), :].astype(BF) for c in (code, code_far)]
    for s in range(0, slots, chunk):
        rows = slice(s, s + chunk)
        x = items[rows, :]
        xf = x.astype(F32)
        inv = lax.rsqrt(jnp.sum(xf * xf, axis=-1, keepdims=True) + EPS_UNIT)
        inv_o[rows, :] = jnp.broadcast_to(inv, (chunk, BLOCK))
        cosines = dot_nt(x, units[...]) * (inv * (1.0 / COSINE_DIVISOR))
        slot = s + iota((chunk, 1), 0).astype(F32)
        owner = jnp.floor((slot + 0.5) * (1.0 / (2 * capacity)))
        local = slot - owner * (2 * capacity)
        far = local >= capacity
        local = jnp.where(far, local - capacity, local)
        named = owner == iota((chunk, near), 1).astype(F32)
        for side in range(2):
            lanes = slice(side * events, (side + 1) * events)
            logits = cosines[:, lanes]
            spread = jnp.where(named & (far == (side == 1)), 1.0, 0.0).astype(BF)
            codes = dot_nn(spread, codes_in[side])
            first = codes == 2.0 * local + 2.0
            other = codes == 2.0 * local + 1.0
            e = jnp.exp(logits)
            total_o[:, lanes] = (
                jnp.sum(jnp.where(first | other, e, 0.0), axis=0, keepdims=True)
                + (total_o[:, lanes] if s else 0.0)
            )
            expo[rows, lanes] = jnp.where(first, -e, jnp.where(other, e, 0.0))


def shares(meta, expo, total, total_far, dp, seqs, seq_dev, steps):
    events = total.shape[1] // 2
    position = meta[1] * events + iota((1, events), 1)
    valid = []
    for base in (meta[0], jnp.bitwise_xor(meta[0], dp // 2)):
        v = jnp.zeros((1, events), F32)
        for k in range(seq_dev):
            step = position - k * steps
            v = jnp.where((step >= 0) & (step < length_of(meta, base * seq_dev + k, seqs)), 1.0, v)
        valid.append(v)
    valid = jnp.concatenate(valid, axis=1) * (1.0 / COSINE_DIVISOR)
    full = total[...] + jnp.concatenate([total_far[:, events:], total_far[:, :events]], axis=1)
    factor = valid / full
    return lambda rows: jnp.abs(expo[rows, :]) * factor - jnp.where(expo[rows, :] < 0.0, valid, 0.0)


def slope_kernel(
    meta, items, code, code_far, expo, inv, total, total_far, slopes, slopes_bf, ledger,
    *, dp, seqs, seq_dev, steps, chunk,
):
    share = shares(meta, expo, total, total_far, dp, seqs, seq_dev, steps)
    events, width = slopes.shape[0] // 2, slopes.shape[1]
    both = jnp.zeros((2 * events, width), F32)
    for s in range(0, items.shape[0], chunk):
        rows = slice(s, s + chunk)
        both = both + dot_tn((share(rows) * inv[rows, 0:1]).astype(BF), items[rows, :])
    slopes[...] = both
    slopes_bf[...] = both.astype(BF)
    near = ledger.shape[0]
    each = items.shape[0] // near
    weight = jnp.concatenate(
        [
            jnp.sum(share(slice(o * each, (o + 1) * each)), axis=0, keepdims=True)
            for o in range(near)
        ],
        axis=0,
    )
    high = weight.astype(BF)
    low = (weight - high.astype(F32)).astype(BF)
    half = pl.multiple_of(lax.div(meta[0], dp // 2) * near, near)
    codes = [c[pl.ds(half, near), :].astype(BF) for c in (code, code_far)]
    for n, part in enumerate([high, low, jnp.concatenate(codes, axis=1)]):
        ledger[:, n * 2 * events : (n + 1) * 2 * events] = part


def send_kernel(
    meta, expo, total, total_far, units, sending,
    *, dp, seqs, seq_dev, steps, chunk,
):
    share = shares(meta, expo, total, total_far, dp, seqs, seq_dev, steps)
    for s in range(0, expo.shape[0], chunk):
        rows = slice(s, s + chunk)
        hot = jnp.where(expo[rows, :] == 0.0, 0.0, 1.0).astype(BF)
        unit_rows = dot_nn(hot, units[...])
        weight = jnp.sum(share(rows), axis=1, keepdims=True)
        sending[rows, :] = (unit_rows * weight).astype(BF)


def mail_kernel(meta, *refs, half, mp, events, capacity):
    units, ledgers, outs = refs[: 2 * half], refs[2 * half : 3 * half], refs[3 * half : -2]
    hots, ledger = refs[-2:]
    here = jnp.where(meta[0] >= half, meta[0] - half, meta[0])
    slot = iota((2 * capacity, 2 * events), 0)
    event = iota((2 * capacity, 2 * events), 1)
    far = slot >= capacity
    local = jnp.where(far, slot - capacity, slot).astype(F32)
    same = far == (event >= events)
    for j in range(half):
        ledger[...] = ledgers[j][...].astype(F32)
        weights = []
        for k in range(mp):
            line = ledger[pl.ds(here * mp + jnp.bitwise_xor(meta[1], k), 1), :]
            code = line[:, 4 * events : 6 * events]
            mine = same & (jnp.floor((code - 1.0) * 0.5) == local)
            hots[k * 2 * capacity : (k + 1) * 2 * capacity, :] = mine.astype(BF)
            weight = line[:, : 2 * events] + line[:, 2 * events : 4 * events]
            weights.append(jnp.sum(jnp.where(mine, weight, 0.0), axis=1, keepdims=True))
        rows = dot_nn(hots[:, :events], units[j][...])
        rows = rows + dot_nn(hots[:, events:], units[half + j][...])
        for k in range(mp):
            part = rows[k * 2 * capacity : (k + 1) * 2 * capacity] * weights[k]
            outs[k][j * 2 * capacity : (j + 1) * 2 * capacity, :] = part.astype(BF)


def out_cot_kernel(units, inv_out, slopes, slopes_back, out_cot):
    events = units.shape[0] // 2
    for side in range(2):
        rows = slice(side * events, (side + 1) * events)
        there = slice((1 - side) * events, (2 - side) * events)
        u = units[rows, :]
        s = slopes[rows, :] + slopes_back[there, :].astype(F32)
        along = jnp.sum(u * s, axis=-1, keepdims=True)
        out_cot[rows, :] = ((s - u * along) * inv_out[rows, 0:1]).astype(BF)


def spread_kernel(incoming, *refs, at, chunk):
    landed, out = refs[:-1], refs[-1]
    for r in range(0, out.shape[0], chunk):
        v, first = 0.0, at
        for part in landed:
            slots = slice(first, first + part.shape[0])
            line = r + iota((chunk, part.shape[0]), 0)
            hot = jnp.where(line == incoming[:, slots], 1.0, 0.0).astype(BF)
            v = v + dot_nn(hot, part[...])
            first += part.shape[0]
        out[r : r + chunk, :] = v


def finish_kernel(incoming, catalogue, before, landed, out, *, at, chunk):
    slots = landed.shape[0]
    for r in range(0, out.shape[0], chunk):
        rows = slice(r, r + chunk)
        line = r + iota((chunk, slots), 0)
        hot = jnp.where(line == incoming[:, at : at + slots], 1.0, 0.0).astype(BF)
        v = before[rows, :] + dot_nn(hot, landed[...])
        c = catalogue[rows, :].astype(F32)
        inv = lax.rsqrt(jnp.sum(c * c, axis=-1, keepdims=True) + EPS_UNIT)
        c = c * inv
        out[rows, :] = (v - c * jnp.sum(c * v, axis=-1, keepdims=True)) * inv


def backward_kernel(meta, *refs, mp, dp):
    blocks = refs[:mp]
    w_out, wide, projected, turned = refs[mp : mp + 4]
    outs = refs[mp + 4 : -2]
    whole, cot = refs[-2:]
    half = dp // 2
    quarter, width = blocks[0].shape[0] // 2, blocks[0].shape[1]
    rows_all = whole.shape[0]
    cols = w_out.shape[0]
    for j in range(mp):
        for side in range(2):
            start = side * (rows_all // 2) + jnp.bitwise_xor(meta[1], j) * quarter
            rows = slice(side * quarter, (side + 1) * quarter)
            whole[pl.ds(pl.multiple_of(start, quarter), quarter), :] = blocks[j][rows, :]
    gated_cot = dot_nt(whole[...], w_out[...]).astype(BF).astype(F32)
    for g in range(rows_all // BLOCK):
        rows = slice(g * BLOCK, (g + 1) * BLOCK)
        for h in range(cols // DH):
            lanes = slice(h * DH, (h + 1) * DH)
            d_gated = gated_cot[rows, lanes]
            n = wide[0, rows, lanes]
            d_norm = d_gated * projected[0, rows, lanes].astype(F32)
            d_mixed = wide[1, rows, lanes] * (
                d_norm
                - jnp.mean(d_norm, axis=-1, keepdims=True)
                - n * jnp.mean(d_norm * n, axis=-1, keepdims=True)
            )
            d_mixed = d_mixed.astype(BF)
            d_weights = dot_nt(d_mixed, projected[1, rows, lanes]).astype(BF).astype(F32)
            d_values = dot_tn(projected[4, rows, lanes], d_mixed)
            d_scores = (d_weights * wide[2, rows, lanes]).astype(BF)
            d_queries = dot_nn(d_scores, projected[3, rows, lanes])
            d_keys = dot_tn(d_scores, projected[2, rows, lanes])
            for c, d in enumerate((d_gated * n, d_values, d_queries, d_keys)):
                step = projected[5 + c, rows, lanes].astype(F32)
                cot[c, rows, lanes] = (d.astype(BF).astype(F32) * step).astype(BF)
    share = width // dp
    mine = pl.multiple_of(lax.div(meta[0], half) * (width // 2), width // 2)
    here = jnp.where(meta[0] >= half, meta[0] - half, meta[0])
    normed = turned[pl.ds(mine, width // 2), :]
    for c in range(5):
        if c < 4:
            part = dot_nn(normed, cot[c]).astype(BF)
        else:
            lanes = pl.ds(mine, width // 2)
            part = dot_nn(turned[width:, :], whole[:, lanes]).T.astype(BF)
        for d in range(half):
            piece = part[d * share : (d + 1) * share, :]
            if len(outs) == 1:
                outs[0][d, c] = piece
                continue
            for j in range(half):

                @pl.when(jnp.bitwise_xor(here, j) == d)
                def _(j=j, piece=piece):
                    outs[j][c] = piece


def sum_kernel(*refs):
    parts, w_in_grad, w_out_grad = refs[:-2], *refs[-2:]
    for c in range(5):
        total = sum(p[c].astype(F32) for p in parts)
        if c < 4:
            w_in_grad[c] = total
        else:
            w_out_grad[...] = total.T


def swapped(x, axis, bit):
    size = lax.axis_size(axis)
    return lax.ppermute(x, axis, [(a, a ^ bit) for a in range(size)])


def gather_blocks(x, axis, half=None, size=None):
    size = size or lax.axis_size(axis)
    blocks = {0: x} if half is None else {0: x, size // 2: half}
    bit = size // 2 if half is None else size // 4
    while bit:
        for j in list(blocks):
            blocks[j ^ bit] = swapped(blocks[j], axis, bit)
        bit //= 2
    return [blocks[j] for j in range(size)]


def exchange(parts, axis):
    return [p if j == 0 else swapped(p, axis, j) for j, p in enumerate(parts)]


def per_device(history, lengths, source, owners, item_rows, catalogue, w_in, w_out):
    dp = lax.axis_size("dp")
    mp = lax.axis_size("mp")
    devices = dp * mp
    near = devices // 2
    seq_dev, steps, part = history.shape
    width = part * mp
    cols = w_in.shape[2]
    rows_all = seq_dev * steps
    quarter = rows_all // mp
    events, top = owners.shape
    asks = events * top
    capacity = max(2, (3 * asks + 2 * devices - 1) // (2 * devices))
    slots = devices * capacity
    stock = catalogue.shape[0]
    per_peer = (seq_dev + dp - 1) // dp
    chunk = math.gcd(slots, 512)
    short = dp <= 8 and near <= 16 and 6 * events <= width
    S = jax.ShapeDtypeStruct
    here_dp = lax.axis_index("dp")
    place = jnp.stack([here_dp, lax.axis_index("mp")]).astype(I32)
    meta = jnp.concatenate([place, source, lengths])
    seqs = source.shape[0]
    halves = [list(range(near)), list(range(near, devices))]

    def partner(x):
        return swapped(x, "dp", dp // 2)

    def in_half(x):
        return lax.all_to_all(
            x.reshape(near, 2 * capacity, width),
            ("dp", "mp"),
            split_axis=0,
            concat_axis=0,
            tiled=True,
            axis_index_groups=halves,
        ).reshape(slots, width)

    w_out_y = swapped(w_out, "mp", mp // 2)
    packed, code = call(
        functools.partial(
            pack_kernel, dp=dp, seq_dev=seq_dev, per_peer=per_peer, mp=mp, capacity=capacity
        ),
        [S((dp, 2 * per_peer * steps + 16, part), BF), S((devices, events), F32)],
        [SM, HB, HB, HB],
        4,
        limit=58,
    )(meta, history, owners.T, item_rows.T)
    arrived = lax.all_to_all(packed, "dp", split_axis=0, concat_axis=0, tiled=True)
    arrived, w_out_y = lax.optimization_barrier((arrived, w_out_y))
    rows, digits = call(
        functools.partial(take_kernel, dp=dp, seq_dev=seq_dev, per_peer=per_peer, steps=steps),
        [S((2 * rows_all, part), BF), S((16 * dp, part), BF)],
        [SM, VM],
        1,
    )(meta, arrived)
    digits_y = swapped(digits, "mp", mp // 2)
    rows, digits_y = lax.optimization_barrier((rows, digits_y))
    rows_y = swapped(rows, "mp", mp // 2)
    digits = gather_blocks(digits, "mp", digits_y)
    code_far = partner(code)
    looked, incoming, returning = call(
        functools.partial(
            look_kernel, mp=mp, dp=dp, capacity=capacity, chunk=chunk, share=short
        ),
        [S((slots, width), BF), S((1, slots), I32), S((1, slots), I32)],
        [SM] + [VM] * mp + [VM],
        4,
        scratch=[pltpu.VMEM((16 * dp, part), F32), pltpu.VMEM((devices, capacity), F32)],
    )(meta, *digits, catalogue)
    looked, rows_y, code_far = lax.optimization_barrier((looked, rows_y, code_far))
    features = gather_blocks(rows, "mp", rows_y)
    items = in_half(looked)

    wide, projected, turned, own, *gated = call(
        functools.partial(
            forward_kernel,
            mp=mp,
            dp=dp,
            seqs=seqs,
            seq_dev=seq_dev,
            steps=steps,
            width=width,
            cols=cols,
            quarter=quarter,
        ),
        [
            S((3, 2 * rows_all, cols), F32),
            S((9, 2 * rows_all, cols), BF),
            S((width + cols, 2 * rows_all), BF),
            S((2 * quarter, width), BF),
        ]
        + [S((2 * quarter, cols), BF)] * mp,
        [SM] + [VM] * mp + [VM],
        10,
        scratch=[pltpu.VMEM((2 * rows_all, width), BF), pltpu.VMEM((2 * rows_all, cols), BF)],
        limit=36,
    )(meta, *features, w_in)
    gathered = exchange(gated, "mp")
    w_out_blocks = gather_blocks(w_out, "mp", w_out_y)
    units, units_bf, inv_out, *unit_sides = call(
        functools.partial(out_kernel, mp=mp),
        [
            S((2 * quarter, width), F32),
            S((2 * quarter, width), BF),
            S((2 * quarter, BLOCK), F32),
            S((quarter, width), BF),
            S((quarter, width), BF),
        ],
        [VM] + [VM] * (2 * mp),
        2,
    )(own, *gathered, *w_out_blocks)

    expo, inv_item, total = call(
        functools.partial(
            score_kernel, dp=dp, devices=devices, capacity=capacity, chunk=chunk
        ),
        [S((slots, 2 * events), F32), S((slots, BLOCK), F32), S((1, 2 * events), F32)],
        [SM, VM] + [VM] * 3,
        4,
    )(meta, items, code, code_far, units_bf)
    total_far = partner(total)
    sizes = dict(dp=dp, seqs=seqs, seq_dev=seq_dev, steps=steps, chunk=chunk)
    slopes, slopes_bf, ledger = call(
        functools.partial(slope_kernel, **sizes),
        [
            S((2 * events, width), F32),
            S((2 * events, width), BF),
            S((near, width), BF),
        ],
        [SM, VM] + [VM] * 6,
        3,
    )(meta, items, code, code_far, expo, inv_item, total, total_far)
    slopes_back = partner(slopes_bf)
    if short:
        column = range(1, dp // 2)
        ledgers = [ledger] + [swapped(ledger, "dp", j) for j in column]
        all_units = [b for u in unit_sides for b in gather_blocks(u, "dp", size=dp // 2)]
        mail = call(
            functools.partial(
                mail_kernel, half=dp // 2, mp=mp, events=events, capacity=capacity
            ),
            [S((dp * capacity, width), BF)] * mp,
            [SM] + [VM] * (dp + dp // 2),
            4,
            scratch=[
                pltpu.VMEM((mp * 2 * capacity, 2 * events), BF),
                pltpu.VMEM((near, width), F32),
            ],
        )(meta, *all_units, *ledgers)
        landed = exchange(mail, "mp")
    out_cot = call(out_cot_kernel, S((2 * events, width), BF), [VM] * 4, 1)(
        units, inv_out, slopes, slopes_back
    )
    cots = gather_blocks(out_cot, "mp")
    pieces = [S((5, width // dp, cols), BF)] * (dp // 2)
    parts = call(
        functools.partial(backward_kernel, mp=mp, dp=dp),
        pieces if short else [S((dp // 2, 5, width // dp, cols), BF)],
        [SM] + [VM] * (mp + 4),
        10,
        scratch=[
            pltpu.VMEM((2 * rows_all, width), BF),
            pltpu.VMEM((4, 2 * rows_all, cols), BF),
        ],
        limit=36,
    )(meta, *cots, w_out, wide, projected, turned)
    if short:
        parts = exchange(parts, "dp")
        parts, landed[:-1] = lax.optimization_barrier((parts, landed[:-1]))
        w_in_grad, w_out_grad = call(
            sum_kernel,
            [S((4, width // dp, cols), F32), S((cols, width // dp), F32)],
            [VM] * len(parts),
            1,
        )(*parts)
    else:
        got = lax.all_to_all(
            parts[0],
            "dp",
            split_axis=0,
            concat_axis=0,
            tiled=True,
            axis_index_groups=[list(range(dp // 2)), list(range(dp // 2, dp))],
        )
        grads = jnp.sum(got.astype(F32), axis=0)
        w_in_grad, w_out_grad = grads[:4], grads[4].T
        sending = call(
            functools.partial(send_kernel, **sizes),
            S((slots, width), BF),
            [SM] + [VM] * 4,
            3,
        )(meta, expo, total, total_far, units_bf)
        landed = [in_half(sending)]
    rows_chunk = math.gcd(stock, 128)
    last = slots // 4
    if len(landed) == 1:
        landed = [landed[0][: slots - last], landed[0][slots - last :]]
    before = call(
        functools.partial(spread_kernel, at=0, chunk=rows_chunk),
        S((stock, width), F32),
        [VM] * len(landed),
        3,
    )(returning, *landed[:-1])
    if short:
        before, _ = lax.optimization_barrier((before, w_in_grad))
    cat_grad = call(
        functools.partial(finish_kernel, at=slots - last, chunk=rows_chunk),
        S((stock, width), F32),
        [VM] * 4,
        3,
        out_specs=[HB],
    )(returning, catalogue, before, landed[-1])
    return (w_in_grad, w_out_grad, cat_grad)


def solution(mesh):
    placed = (
        P("dp", None, "mp"),
        P(),
        P(),
        P(("dp", "mp"), None),
        P(("dp", "mp"), None),
        P(("dp", "mp"), None),
        P(None, None, "mp"),
        P("mp", None),
    )
    return jax.shard_map(
        per_device,
        mesh=mesh,
        in_specs=placed,
        out_specs=(P(None, "dp", "mp"), P("mp", "dp"), P(("dp", "mp"), None)),
        check_vma=False,
    )
```

```python
import functools
import math

import jax
import jax.numpy as jnp
from jax import lax
from jax.experimental import pallas as pl
from jax.experimental.pallas import tpu as pltpu
from jax.sharding import PartitionSpec as P

DH = 128
COSINE_DIVISOR = 0.05
EPS_NORM = 1e-05
EPS_UNIT = 1e-06
BF = jnp.bfloat16
F32 = jnp.float32
I32 = jnp.int32
BLOCK = 128

VM = pl.BlockSpec(memory_space=pltpu.VMEM)
SM = pl.BlockSpec(memory_space=pltpu.SMEM)
HB = pl.BlockSpec(memory_space=pltpu.HBM)


def call(body, out_shape, in_specs, us, scratch=(), limit=16, out_specs=None, lazy=False):
    many = isinstance(out_shape, (list, tuple))
    outs = list(out_shape) if many else [out_shape]
    out_specs = list(out_specs or [VM] * len(outs))

    def run(*args):
        args = list(args)
        far_in = [n for n, spec in enumerate(in_specs) if spec is HB]
        far_out = [n for n, spec in enumerate(out_specs) if spec is HB]
        n_in, n_out, n_own = len(in_specs), len(outs), len(scratch)
        extra = [pltpu.VMEM(args[n].shape, args[n].dtype) for n in far_in]
        extra += [pltpu.VMEM(outs[n].shape, outs[n].dtype) for n in far_out]
        moved = len(far_in) + len(far_out)

        def kernel(*refs):
            ins, res = list(refs[:n_in]), list(refs[n_in : n_in + n_out])
            own = refs[n_in + n_out : n_in + n_out + n_own]
            held = refs[n_in + n_out + n_own :]
            sems = held[-1] if moved else None
            copies = []
            for m, n in enumerate(far_in):
                copies.append(pltpu.make_async_copy(ins[n], held[m], sems.at[m]))
                ins[n] = held[m]
            for c in copies:
                c.start()
            arriving = dict(zip(far_in, copies))

            def ready(*places):
                for n in places:
                    arriving.pop(n).wait()

            more = {"ready": ready} if lazy else {}
            if not lazy:
                ready(*far_in)
            copies = []
            for m, n in enumerate(far_out):
                m += len(far_in)
                copies.append(pltpu.make_async_copy(held[m], res[n], sems.at[m]))
                res[n] = held[m]
            body(*ins, *res, *own, **more)
            for c in copies:
                c.start()
            for c in copies:
                c.wait()

        result = pl.pallas_call(
            kernel,
            out_shape=outs,
            in_specs=list(in_specs),
            out_specs=out_specs,
            scratch_shapes=list(scratch)
            + extra
            + ([pltpu.SemaphoreType.DMA((moved,))] if moved else []),
            compiler_params=pltpu.CompilerParams(vmem_limit_bytes=limit * 2**20),
            cost_estimate=pl.CostEstimate(
                flops=0, bytes_accessed=int(us * 3.3e6), transcendentals=0
            ),
        )(*args)
        return result if many else result[0]

    return run


def dot_nt(a, b):
    return lax.dot_general(a, b, (((1,), (1,)), ((), ())), preferred_element_type=F32)


def dot_tn(a, b):
    return lax.dot_general(a, b, (((0,), (0,)), ((), ())), preferred_element_type=F32)


def dot_nn(a, b):
    return jnp.dot(a, b, preferred_element_type=F32)


def iota(shape, dim):
    return lax.broadcasted_iota(I32, shape, dim)


def length_of(meta, slot, seqs):
    return meta[2 + seqs + meta[2 + slot]]


def pack_kernel(meta, hist, owners_t, rows_t, out, code, *, dp, seq_dev, per_peer, mp, capacity):
    here = meta[0]
    steps, part = hist.shape[1], hist.shape[2]

    def per_dest(d, carry):
        def per_slot(i, count):
            src = meta[2 + d * seq_dev + i]
            hit = lax.div(src, seq_dev) == here

            @pl.when(hit)
            def _():
                value = hist[src - here * seq_dev]
                for side in range(2):
                    start = pl.multiple_of((side * per_peer + count) * steps, steps)
                    out[jnp.bitwise_xor(d, side * (dp // 2)), pl.ds(start, steps), :] = value

            return count + hit.astype(I32)

        lax.fori_loop(0, seq_dev, per_slot, jnp.int32(0))
        return carry

    lax.fori_loop(0, dp, per_dest, jnp.int32(0))
    top, events = owners_t.shape
    devices = dp * mp
    lanes = -(-capacity // 128) * 128
    o_id = iota((devices, events), 0)
    named = jnp.zeros((devices, events), F32)
    row = jnp.zeros((devices, events), F32)
    positive = jnp.zeros((devices, events), F32)
    for j in range(top):
        same = jnp.where(owners_t[j : j + 1, :] == o_id, 1.0, 0.0)
        named = named + same
        row = row + same * rows_t[j : j + 1, :].astype(F32)
        if j == 0:
            positive = same
    before = (iota((events, events), 0) < iota((events, events), 1)).astype(BF)
    rank = dot_nn(named.astype(BF), before)
    code[...] = jnp.where(named > 0.0, 2.0 * rank + 1.0 + positive, 0.0)
    rank = jnp.where(named > 0.0, rank, -1.0)
    lane = iota((devices, lanes), 1)
    wanted = jnp.zeros((devices, lanes), F32)
    for c in range(capacity):
        one = jnp.sum(jnp.where(rank == float(c), row, 0.0), axis=1, keepdims=True)
        wanted = jnp.where(lane == c, one, wanted)
    high = jnp.floor(wanted * (1.0 / 256.0))
    low = wanted - 256.0 * high
    none = jnp.zeros((8 - mp, lanes), F32)
    for d in range(dp):
        mine = slice(d * mp, (d + 1) * mp)
        digits = [high[mine], none, low[mine], none] if mp < 8 else [high[mine], low[mine]]
        out[d, 2 * per_peer * steps :, :lanes] = jnp.concatenate(digits, axis=0).astype(BF)


def take_kernel(meta, arrived, out, digits, *, dp, seq_dev, per_peer, steps):
    for side in range(2):
        block = jnp.bitwise_xor(meta[0], side * (dp // 2))
        anchors = [lax.div(meta[2 + block * seq_dev + k], seq_dev) for k in range(seq_dev)]
        for k in range(seq_dev):
            rank = jnp.int32(side * per_peer)
            for earlier in range(k):
                rank = rank + (anchors[earlier] == anchors[k]).astype(I32)
            start = pl.multiple_of(rank * steps, steps)
            at = (side * seq_dev + k) * steps
            out[at : at + steps, :] = arrived[anchors[k], pl.ds(start, steps), :]
    for d in range(dp):
        digits[d * 16 : (d + 1) * 16, :] = arrived[d, 2 * per_peer * steps :, :]


def forward_kernel(meta, *refs, mp, dp, seqs, seq_dev, steps, width, cols, quarter):
    blocks = refs[:mp]
    w_in = refs[mp]
    wide, projected, turned, own = refs[mp + 1 : mp + 5]
    gated_out = refs[mp + 5 : 2 * mp + 5]
    feat, gated = refs[2 * mp + 5 :]
    here_mp = meta[1]
    part = width // mp
    counts = [
        length_of(meta, block * seq_dev + k, seqs)
        for block in (meta[0], jnp.bitwise_xor(meta[0], dp // 2))
        for k in range(seq_dev)
    ]
    half_rows = seq_dev * steps
    rows_all = 2 * half_rows
    for j in range(mp):
        start = pl.multiple_of(jnp.bitwise_xor(here_mp, j) * part, part)
        feat[:, pl.ds(start, part)] = blocks[j][...]
    for side in range(2):
        start = pl.multiple_of(side * half_rows + here_mp * quarter, quarter)
        own[side * quarter : (side + 1) * quarter, :] = feat[pl.ds(start, quarter), :]
    for g in range(rows_all // BLOCK):
        rows = slice(g * BLOCK, (g + 1) * BLOCK)
        x = feat[rows, :].astype(F32)
        centered = x - jnp.mean(x, axis=-1, keepdims=True)
        spread = jnp.mean(centered * centered, axis=-1, keepdims=True)
        y = (centered * lax.rsqrt(spread + EPS_NORM)).astype(BF)
        feat[rows, :] = y
        turned[:width, rows] = y.T
    for c in range(4):
        pre = dot_nn(feat[...], w_in[c])
        sigma = jax.nn.sigmoid(pre)
        projected[c] = (pre * sigma).astype(BF)
        projected[5 + c] = (sigma * (1.0 + pre * (1.0 - sigma))).astype(BF)
    root = 1.0 / math.sqrt(DH)
    t_id = iota((BLOCK, BLOCK), 0)
    s_id = iota((BLOCK, BLOCK), 1)
    per_block = BLOCK // steps
    causal = (t_id // steps == s_id // steps) & (s_id <= t_id)
    for g in range(rows_all // BLOCK):
        rows = slice(g * BLOCK, (g + 1) * BLOCK)
        count = jnp.zeros((BLOCK, BLOCK), I32)
        for i in range(per_block):
            count = jnp.where(t_id // steps == i, counts[g * per_block + i], count)
        allowed = causal & (s_id % steps < count)
        scale = jnp.where(allowed, 1.0 / count.astype(F32), 0.0)
        for h in range(cols // DH):
            lanes = slice(h * DH, (h + 1) * DH)
            scores = dot_nt(projected[2, rows, lanes], projected[3, rows, lanes]) * root
            sigma = jax.nn.sigmoid(scores)
            weights = (scores * sigma * scale).astype(BF)
            projected[4, rows, lanes] = weights
            wide[2, rows, lanes] = sigma * (1.0 + scores * (1.0 - sigma)) * (scale * root)
            mixed = dot_nn(weights, projected[1, rows, lanes])
            centered = mixed - jnp.mean(mixed, axis=-1, keepdims=True)
            spread = jnp.mean(centered * centered, axis=-1, keepdims=True)
            inv = lax.rsqrt(spread + EPS_NORM)
            norm = centered * inv
            wide[0, rows, lanes] = norm
            wide[1, rows, lanes] = jnp.broadcast_to(inv, norm.shape)
            done = (norm * projected[0, rows, lanes].astype(F32)).astype(BF)
            gated[rows, lanes] = done
            turned[width + h * DH : width + (h + 1) * DH, rows] = done.T
    for j in range(mp):
        for side in range(2):
            start = side * half_rows + jnp.bitwise_xor(here_mp, j) * quarter
            start = pl.multiple_of(start, quarter)
            gated_out[j][side * quarter : (side + 1) * quarter, :] = gated[pl.ds(start, quarter), :]


def out_kernel(own, *refs, mp):
    gathered, weights = refs[:mp], refs[mp : 2 * mp]
    inv_o, *sides = refs[2 * mp :]
    half = own.shape[0] // 2
    for side, rows in enumerate((slice(0, half), slice(half, 2 * half))):
        total = own[rows, :].astype(F32)
        for j in range(mp):
            total = total + dot_nn(gathered[j][rows, :], weights[j][...])
        inv = lax.rsqrt(jnp.sum(total * total, axis=-1, keepdims=True) + EPS_UNIT)
        sides[side][...] = (total * inv).astype(BF)
        inv_o[rows, :] = jnp.broadcast_to(inv, (half, BLOCK))


def look_kernel(meta, *refs, mp, dp, capacity, chunk, share):
    blocks, catalogue, looked, incoming, returning, digits, asked = refs[:mp], *refs[mp:]
    stock, _ = catalogue.shape
    for j in range(mp):
        digits[...] = blocks[j][...].astype(F32)
        for d in range(dp):
            high = digits[pl.ds(d * 16 + meta[1], 1), :]
            low = digits[pl.ds(d * 16 + 8 + meta[1], 1), :]
            asked[j * dp + d : j * dp + d + 1, :] = (256.0 * high + low)[:, :capacity]
    groups = dp * mp
    slots = groups * capacity
    half = dp // 2
    table = asked[...]
    slot = iota((1, slots), 1).astype(F32)
    group = jnp.floor((slot + 0.5) * (1.0 / capacity))
    local = slot - group * capacity
    column = (iota((capacity, slots), 0).astype(F32) == local).astype(F32)
    spread = lax.dot_general(
        table,
        column,
        (((1,), (0,)), ((), ())),
        precision=lax.Precision.HIGHEST,
        preferred_element_type=F32,
    )
    line = iota((groups, 1), 0)
    offset = lax.div(line, dp)
    index = line - offset * dp
    side = (index >= half) != (meta[0] >= half)
    near = jnp.where(index >= half, index - half, index)
    first = (near * mp + jnp.bitwise_xor(offset, meta[1])) * 2 + side.astype(I32)
    here = jnp.where(meta[0] >= half, meta[0] - half, meta[0])
    second = (offset * half + jnp.bitwise_xor(near, here)) * 2 + side.astype(I32)
    rows = [
        jnp.sum(jnp.where(group == g.astype(F32), spread, 0.0), axis=0, keepdims=True).astype(I32)
        for g in (first, second)
    ]
    incoming[...] = rows[0]
    returning[...] = rows[1] if share else rows[0]
    for s in range(0, slots, chunk):
        hot = jnp.where(iota((stock, chunk), 0) == incoming[:, s : s + chunk], 1.0, 0.0).astype(BF)
        looked[s : s + chunk, :] = dot_tn(hot, catalogue[...]).astype(BF)


def score_kernel(
    meta, items, code, code_far, unit_near, unit_far, expo, inv_o, total_o,
    *, dp, devices, capacity, chunk,
):
    events = unit_near.shape[0]
    near = devices // 2
    slots = items.shape[0]
    half = pl.multiple_of(lax.div(meta[0], dp // 2) * near, near)
    codes_in = [c[pl.ds(half, near), :].astype(BF) for c in (code, code_far)]
    for s in range(0, slots, chunk):
        rows = slice(s, s + chunk)
        x = items[rows, :]
        xf = x.astype(F32)
        inv = lax.rsqrt(jnp.sum(xf * xf, axis=-1, keepdims=True) + EPS_UNIT)
        inv_o[rows, :] = jnp.broadcast_to(inv, (chunk, BLOCK))
        scale = inv * (1.0 / COSINE_DIVISOR)
        slot = s + iota((chunk, 1), 0).astype(F32)
        owner = jnp.floor((slot + 0.5) * (1.0 / (2 * capacity)))
        local = slot - owner * (2 * capacity)
        far = local >= capacity
        local = jnp.where(far, local - capacity, local)
        named = owner == iota((chunk, near), 1).astype(F32)
        for side in range(2):
            lanes = slice(side * events, (side + 1) * events)
            logits = dot_nt(x, (unit_near, unit_far)[side][...]) * scale
            spread = jnp.where(named & (far == (side == 1)), 1.0, 0.0).astype(BF)
            codes = dot_nn(spread, codes_in[side])
            first = codes == 2.0 * local + 2.0
            other = codes == 2.0 * local + 1.0
            e = jnp.exp(logits)
            total_o[:, lanes] = (
                jnp.sum(jnp.where(first | other, e, 0.0), axis=0, keepdims=True)
                + (total_o[:, lanes] if s else 0.0)
            )
            expo[rows, lanes] = jnp.where(first, -e, jnp.where(other, e, 0.0))


def shares(meta, expo, total, total_far, dp, seqs, seq_dev, steps):
    events = total.shape[1] // 2
    position = meta[1] * events + iota((1, events), 1)
    valid = []
    for base in (meta[0], jnp.bitwise_xor(meta[0], dp // 2)):
        v = jnp.zeros((1, events), F32)
        for k in range(seq_dev):
            step = position - k * steps
            v = jnp.where((step >= 0) & (step < length_of(meta, base * seq_dev + k, seqs)), 1.0, v)
        valid.append(v)
    valid = jnp.concatenate(valid, axis=1) * (1.0 / COSINE_DIVISOR)
    full = total[...] + jnp.concatenate([total_far[:, events:], total_far[:, :events]], axis=1)
    factor = valid / full
    return lambda rows: jnp.abs(expo[rows, :]) * factor - jnp.where(expo[rows, :] < 0.0, valid, 0.0)


def slope_kernel(
    meta, items, code, code_far, expo, inv, total, total_far, slopes, slopes_bf, ledger,
    *, dp, seqs, seq_dev, steps, chunk,
):
    share = shares(meta, expo, total, total_far, dp, seqs, seq_dev, steps)
    events, width = slopes.shape[0] // 2, slopes.shape[1]
    both = jnp.zeros((2 * events, width), F32)
    for s in range(0, items.shape[0], chunk):
        rows = slice(s, s + chunk)
        both = both + dot_tn((share(rows) * inv[rows, 0:1]).astype(BF), items[rows, :])
    slopes[...] = both
    slopes_bf[...] = both.astype(BF)
    near = ledger.shape[0]
    each = items.shape[0] // near
    weight = jnp.concatenate(
        [
            jnp.sum(share(slice(o * each, (o + 1) * each)), axis=0, keepdims=True)
            for o in range(near)
        ],
        axis=0,
    )
    high = weight.astype(BF)
    low = (weight - high.astype(F32)).astype(BF)
    half = pl.multiple_of(lax.div(meta[0], dp // 2) * near, near)
    codes = [c[pl.ds(half, near), :].astype(BF) for c in (code, code_far)]
    for n, part in enumerate([high, low, jnp.concatenate(codes, axis=1)]):
        ledger[:, n * 2 * events : (n + 1) * 2 * events] = part


def send_kernel(
    meta, expo, total, total_far, units, sending,
    *, dp, seqs, seq_dev, steps, chunk,
):
    share = shares(meta, expo, total, total_far, dp, seqs, seq_dev, steps)
    for s in range(0, expo.shape[0], chunk):
        rows = slice(s, s + chunk)
        hot = jnp.where(expo[rows, :] == 0.0, 0.0, 1.0).astype(BF)
        unit_rows = dot_nn(hot, units[...])
        weight = jnp.sum(share(rows), axis=1, keepdims=True)
        sending[rows, :] = (unit_rows * weight).astype(BF)


def mail_kernel(meta, *refs, half, mp, events, capacity):
    units, ledgers, outs = refs[: 2 * half], refs[2 * half : 3 * half], refs[3 * half : -2]
    hots, ledger = refs[-2:]
    here = jnp.where(meta[0] >= half, meta[0] - half, meta[0])
    slot = iota((2 * capacity, 2 * events), 0)
    event = iota((2 * capacity, 2 * events), 1)
    far = slot >= capacity
    local = jnp.where(far, slot - capacity, slot).astype(F32)
    same = far == (event >= events)
    for j in range(half):
        ledger[...] = ledgers[j][...].astype(F32)
        weights = []
        for k in range(mp):
            line = ledger[pl.ds(here * mp + jnp.bitwise_xor(meta[1], k), 1), :]
            code = line[:, 4 * events : 6 * events]
            mine = same & (jnp.floor((code - 1.0) * 0.5) == local)
            hots[k * 2 * capacity : (k + 1) * 2 * capacity, :] = mine.astype(BF)
            weight = line[:, : 2 * events] + line[:, 2 * events : 4 * events]
            weights.append(jnp.sum(jnp.where(mine, weight, 0.0), axis=1, keepdims=True))
        rows = dot_nn(hots[:, :events], units[j][...])
        rows = rows + dot_nn(hots[:, events:], units[half + j][...])
        for k in range(mp):
            part = rows[k * 2 * capacity : (k + 1) * 2 * capacity] * weights[k]
            outs[k][j * 2 * capacity : (j + 1) * 2 * capacity, :] = part.astype(BF)


def out_cot_kernel(unit_near, unit_far, inv_out, slopes, slopes_back, out_cot):
    events = unit_near.shape[0]
    for side, unit in enumerate((unit_near, unit_far)):
        rows = slice(side * events, (side + 1) * events)
        there = slice((1 - side) * events, (2 - side) * events)
        u = unit[...].astype(F32)
        s = slopes[rows, :] + slopes_back[there, :].astype(F32)
        along = jnp.sum(u * s, axis=-1, keepdims=True)
        out_cot[rows, :] = ((s - u * along) * inv_out[rows, 0:1]).astype(BF)


def spread_kernel(incoming, *refs, at, chunk):
    landed, out = refs[:-1], refs[-1]
    for r in range(0, out.shape[0], chunk):
        v, first = 0.0, at
        for part in landed:
            slots = slice(first, first + part.shape[0])
            line = r + iota((chunk, part.shape[0]), 0)
            hot = jnp.where(line == incoming[:, slots], 1.0, 0.0).astype(BF)
            v = v + dot_nn(hot, part[...])
            first += part.shape[0]
        out[r : r + chunk, :] = v


def finish_kernel(incoming, catalogue, before, landed, out, *, at, chunk):
    slots = landed.shape[0]
    for r in range(0, out.shape[0], chunk):
        rows = slice(r, r + chunk)
        line = r + iota((chunk, slots), 0)
        hot = jnp.where(line == incoming[:, at : at + slots], 1.0, 0.0).astype(BF)
        v = before[rows, :] + dot_nn(hot, landed[...])
        c = catalogue[rows, :].astype(F32)
        inv = lax.rsqrt(jnp.sum(c * c, axis=-1, keepdims=True) + EPS_UNIT)
        c = c * inv
        out[rows, :] = (v - c * jnp.sum(c * v, axis=-1, keepdims=True)) * inv


def backward_kernel(meta, *refs, mp, dp):
    blocks = refs[:mp]
    w_out, wide, projected, turned = refs[mp : mp + 4]
    outs = refs[mp + 4 : -2]
    whole, cot = refs[-2:]
    half = dp // 2
    quarter, width = blocks[0].shape[0] // 2, blocks[0].shape[1]
    rows_all = whole.shape[0]
    cols = w_out.shape[0]
    for j in range(mp):
        for side in range(2):
            start = side * (rows_all // 2) + jnp.bitwise_xor(meta[1], j) * quarter
            rows = slice(side * quarter, (side + 1) * quarter)
            whole[pl.ds(pl.multiple_of(start, quarter), quarter), :] = blocks[j][rows, :]
    gated_cot = dot_nt(whole[...], w_out[...]).astype(BF).astype(F32)
    for g in range(rows_all // BLOCK):
        rows = slice(g * BLOCK, (g + 1) * BLOCK)
        for h in range(cols // DH):
            lanes = slice(h * DH, (h + 1) * DH)
            d_gated = gated_cot[rows, lanes]
            n = wide[0, rows, lanes]
            d_norm = d_gated * projected[0, rows, lanes].astype(F32)
            d_mixed = wide[1, rows, lanes] * (
                d_norm
                - jnp.mean(d_norm, axis=-1, keepdims=True)
                - n * jnp.mean(d_norm * n, axis=-1, keepdims=True)
            )
            d_mixed = d_mixed.astype(BF)
            d_weights = dot_nt(d_mixed, projected[1, rows, lanes]).astype(BF).astype(F32)
            d_values = dot_tn(projected[4, rows, lanes], d_mixed)
            d_scores = (d_weights * wide[2, rows, lanes]).astype(BF)
            d_queries = dot_nn(d_scores, projected[3, rows, lanes])
            d_keys = dot_tn(d_scores, projected[2, rows, lanes])
            for c, d in enumerate((d_gated * n, d_values, d_queries, d_keys)):
                step = projected[5 + c, rows, lanes].astype(F32)
                cot[c, rows, lanes] = (d.astype(BF).astype(F32) * step).astype(BF)
    share = width // dp
    mine = pl.multiple_of(lax.div(meta[0], half) * (width // 2), width // 2)
    here = jnp.where(meta[0] >= half, meta[0] - half, meta[0])
    normed = turned[pl.ds(mine, width // 2), :]
    for c in range(5):
        if c < 4:
            part = dot_nn(normed, cot[c]).astype(BF)
        else:
            lanes = pl.ds(mine, width // 2)
            part = dot_nn(turned[width:, :], whole[:, lanes]).T.astype(BF)
        for d in range(half):
            piece = part[d * share : (d + 1) * share, :]
            if len(outs) == 1:
                outs[0][d, c] = piece
                continue
            for j in range(half):

                @pl.when(jnp.bitwise_xor(here, j) == d)
                def _(j=j, piece=piece):
                    outs[j][c] = piece


def sum_kernel(*refs):
    parts, w_in_grad, w_out_grad = refs[:-2], *refs[-2:]
    for c in range(5):
        total = sum(p[c].astype(F32) for p in parts)
        if c < 4:
            w_in_grad[c] = total
        else:
            w_out_grad[...] = total.T


def swapped(x, axis, bit):
    size = lax.axis_size(axis)
    return lax.ppermute(x, axis, [(a, a ^ bit) for a in range(size)])


def gather_blocks(x, axis, half=None, size=None):
    size = size or lax.axis_size(axis)
    blocks = {0: x} if half is None else {0: x, size // 2: half}
    bit = size // 2 if half is None else size // 4
    while bit:
        for j in list(blocks):
            blocks[j ^ bit] = swapped(blocks[j], axis, bit)
        bit //= 2
    return [blocks[j] for j in range(size)]


def exchange(parts, axis):
    return [p if j == 0 else swapped(p, axis, j) for j, p in enumerate(parts)]


def per_device(history, lengths, source, owners, item_rows, catalogue, w_in, w_out):
    dp = lax.axis_size("dp")
    mp = lax.axis_size("mp")
    devices = dp * mp
    near = devices // 2
    seq_dev, steps, part = history.shape
    width = part * mp
    cols = w_in.shape[2]
    rows_all = seq_dev * steps
    quarter = rows_all // mp
    events, top = owners.shape
    asks = events * top
    capacity = max(2, (3 * asks + 2 * devices - 1) // (2 * devices))
    slots = devices * capacity
    stock = catalogue.shape[0]
    per_peer = (seq_dev + dp - 1) // dp
    chunk = math.gcd(slots, 512)
    short = dp <= 8 and near <= 16 and 6 * events <= width
    S = jax.ShapeDtypeStruct
    here_dp = lax.axis_index("dp")
    place = jnp.stack([here_dp, lax.axis_index("mp")]).astype(I32)
    meta = jnp.concatenate([place, source, lengths])
    seqs = source.shape[0]
    halves = [list(range(near)), list(range(near, devices))]

    def partner(x):
        return swapped(x, "dp", dp // 2)

    def in_half(x):
        return lax.all_to_all(
            x.reshape(near, 2 * capacity, width),
            ("dp", "mp"),
            split_axis=0,
            concat_axis=0,
            tiled=True,
            axis_index_groups=halves,
        ).reshape(slots, width)

    w_out_y = swapped(w_out, "mp", mp // 2)
    packed, code = call(
        functools.partial(
            pack_kernel, dp=dp, seq_dev=seq_dev, per_peer=per_peer, mp=mp, capacity=capacity
        ),
        [S((dp, 2 * per_peer * steps + 16, part), BF), S((devices, events), F32)],
        [SM, HB, HB, HB],
        4,
        limit=58,
    )(meta, history, owners.T, item_rows.T)
    arrived = lax.all_to_all(packed, "dp", split_axis=0, concat_axis=0, tiled=True)
    arrived, w_out_y = lax.optimization_barrier((arrived, w_out_y))
    rows, digits = call(
        functools.partial(take_kernel, dp=dp, seq_dev=seq_dev, per_peer=per_peer, steps=steps),
        [S((2 * rows_all, part), BF), S((16 * dp, part), BF)],
        [SM, VM],
        1,
    )(meta, arrived)
    digits_y = swapped(digits, "mp", mp // 2)
    rows, digits_y = lax.optimization_barrier((rows, digits_y))
    rows_y = swapped(rows, "mp", mp // 2)
    digits = gather_blocks(digits, "mp", digits_y)
    code_far = partner(code)
    looked, incoming, returning = call(
        functools.partial(
            look_kernel, mp=mp, dp=dp, capacity=capacity, chunk=chunk, share=short
        ),
        [S((slots, width), BF), S((1, slots), I32), S((1, slots), I32)],
        [SM] + [VM] * mp + [VM],
        4,
        scratch=[pltpu.VMEM((16 * dp, part), F32), pltpu.VMEM((devices, capacity), F32)],
    )(meta, *digits, catalogue)
    looked, rows_y, code_far = lax.optimization_barrier((looked, rows_y, code_far))
    features = gather_blocks(rows, "mp", rows_y)
    items = in_half(looked)

    wide, projected, turned, own, *gated = call(
        functools.partial(
            forward_kernel,
            mp=mp,
            dp=dp,
            seqs=seqs,
            seq_dev=seq_dev,
            steps=steps,
            width=width,
            cols=cols,
            quarter=quarter,
        ),
        [
            S((3, 2 * rows_all, cols), F32),
            S((9, 2 * rows_all, cols), BF),
            S((width + cols, 2 * rows_all), BF),
            S((2 * quarter, width), BF),
        ]
        + [S((2 * quarter, cols), BF)] * mp,
        [SM] + [VM] * mp + [VM],
        10,
        scratch=[pltpu.VMEM((2 * rows_all, width), BF), pltpu.VMEM((2 * rows_all, cols), BF)],
        limit=36,
    )(meta, *features, w_in)
    gathered = exchange(gated, "mp")
    w_out_blocks = gather_blocks(w_out, "mp", w_out_y)
    inv_out, *unit_sides = call(
        functools.partial(out_kernel, mp=mp),
        [
            S((2 * quarter, BLOCK), F32),
            S((quarter, width), BF),
            S((quarter, width), BF),
        ],
        [VM] + [VM] * (2 * mp),
        2,
    )(own, *gathered, *w_out_blocks)

    expo, inv_item, total = call(
        functools.partial(
            score_kernel, dp=dp, devices=devices, capacity=capacity, chunk=chunk
        ),
        [S((slots, 2 * events), F32), S((slots, BLOCK), F32), S((1, 2 * events), F32)],
        [SM, VM] + [HB] * 4,
        4,
    )(meta, items, code, code_far, *unit_sides)
    total_far = partner(total)
    sizes = dict(dp=dp, seqs=seqs, seq_dev=seq_dev, steps=steps, chunk=chunk)
    slopes, slopes_bf, ledger = call(
        functools.partial(slope_kernel, **sizes),
        [
            S((2 * events, width), F32),
            S((2 * events, width), BF),
            S((near, width), BF),
        ],
        [SM, VM] + [VM] * 6,
        3,
    )(meta, items, code, code_far, expo, inv_item, total, total_far)
    slopes_back = partner(slopes_bf)
    if short:
        column = range(1, dp // 2)
        ledgers = [ledger] + [swapped(ledger, "dp", j) for j in column]
        all_units = [b for u in unit_sides for b in gather_blocks(u, "dp", size=dp // 2)]
        mail = call(
            functools.partial(
                mail_kernel, half=dp // 2, mp=mp, events=events, capacity=capacity
            ),
            [S((dp * capacity, width), BF)] * mp,
            [SM] + [VM] * (dp + dp // 2),
            4,
            scratch=[
                pltpu.VMEM((mp * 2 * capacity, 2 * events), BF),
                pltpu.VMEM((near, width), F32),
            ],
        )(meta, *all_units, *ledgers)
        landed = exchange(mail, "mp")
    out_cot = call(out_cot_kernel, S((2 * events, width), BF), [VM] * 5, 1)(
        *unit_sides, inv_out, slopes, slopes_back
    )
    cots = gather_blocks(out_cot, "mp")
    pieces = [S((5, width // dp, cols), BF)] * (dp // 2)
    parts = call(
        functools.partial(backward_kernel, mp=mp, dp=dp),
        pieces if short else [S((dp // 2, 5, width // dp, cols), BF)],
        [SM] + [VM] * (mp + 4),
        10,
        scratch=[
            pltpu.VMEM((2 * rows_all, width), BF),
            pltpu.VMEM((4, 2 * rows_all, cols), BF),
        ],
        limit=36,
    )(meta, *cots, w_out, wide, projected, turned)
    if short:
        parts = exchange(parts, "dp")
        parts, landed[:-1] = lax.optimization_barrier((parts, landed[:-1]))
        w_in_grad, w_out_grad = call(
            sum_kernel,
            [S((4, width // dp, cols), F32), S((cols, width // dp), F32)],
            [VM] * len(parts),
            1,
        )(*parts)
    else:
        got = lax.all_to_all(
            parts[0],
            "dp",
            split_axis=0,
            concat_axis=0,
            tiled=True,
            axis_index_groups=[list(range(dp // 2)), list(range(dp // 2, dp))],
        )
        grads = jnp.sum(got.astype(F32), axis=0)
        w_in_grad, w_out_grad = grads[:4], grads[4].T
        sending = call(
            functools.partial(send_kernel, **sizes),
            S((slots, width), BF),
            [SM] + [VM] * 4,
            3,
        )(meta, expo, total, total_far, jnp.concatenate(unit_sides))
        landed = [in_half(sending)]
    rows_chunk = math.gcd(stock, 128)
    last = slots // 4
    if len(landed) == 1:
        landed = [landed[0][: slots - last], landed[0][slots - last :]]
    before = call(
        functools.partial(spread_kernel, at=0, chunk=rows_chunk),
        S((stock, width), F32),
        [VM] * len(landed),
        3,
    )(returning, *landed[:-1])
    if short:
        before, _ = lax.optimization_barrier((before, w_in_grad))
    cat_grad = call(
        functools.partial(finish_kernel, at=slots - last, chunk=rows_chunk),
        S((stock, width), F32),
        [VM] * 4,
        3,
        out_specs=[HB],
    )(returning, catalogue, before, landed[-1])
    return (w_in_grad, w_out_grad, cat_grad)


def solution(mesh):
    placed = (
        P("dp", None, "mp"),
        P(),
        P(),
        P(("dp", "mp"), None),
        P(("dp", "mp"), None),
        P(("dp", "mp"), None),
        P(None, None, "mp"),
        P("mp", None),
    )
    return jax.shard_map(
        per_device,
        mesh=mesh,
        in_specs=placed,
        out_specs=(P(None, "dp", "mp"), P("mp", "dp"), P(("dp", "mp"), None)),
        check_vma=False,
    )
```
